128 devices in a mesh: row: 8 (over z, core), col: 16 (over y, x).
Axes of the slice: x: 4, y: 4, z: 4, core: 2. Of those that a mesh axis runs over, the one named last changes fastest.
Arguments:
- inputs: bfloat16 [8192, 2048], P('row', 'col'), may hold values from -6 to 6
- seq_lengths: int32 [8, 2], P('row'), may hold values from 256 to 768, as said below
- query_key_value_weight: bfloat16 [2048, 3, 2048], P('row', None, 'col'), may hold values from -0.125 to 0.125
- query_key_value_bias: bfloat16 [3, 2048], P(None, ('col', 'row')), may hold values from -1.796875 to 1.796875
- w_out: bfloat16 [2048, 2048], P('col', 'row'), may hold values from -2 to 2
- b_out: bfloat16 [2048], P(('col', 'row')), may hold values from -1.796875 to 1.796875
- w_up: bfloat16 [2048, 8192], P('row', 'col'), may hold values from -0.125 to 0.125
- b_up: bfloat16 [8192], P(('col', 'row')), may hold values from -1.796875 to 1.796875
- w_down: bfloat16 [8192, 2048], P('col', 'row'), may hold values from -0.0625 to 0.0625
- b_down: bfloat16 [2048], P(('col', 'row')), may hold values from -1.796875 to 1.796875
- ln_gain: bfloat16 [2048], P(('col', 'row')), may hold values from 0.5 to 1.5
- ln_bias: bfloat16 [2048], P(('col', 'row')), may hold values from -1.796875 to 1.796875
- cotangent: bfloat16 [8192, 2048], P('row', 'col'), may hold values from -6 to 6
Outputs:
- block_out: bfloat16 [8192, 2048], P('row', 'col')
- input_grad: float32 [8192, 2048], P('row', 'col')
- query_key_value_gradient: float32 [2048, 3, 2048], P('row', None, 'col')
- grad_qkv_bias: float32 [3, 2048], P(None, ('col', 'row'))
- grad_out: float32 [2048, 2048], P('col', 'row')
- grad_out_bias: float32 [2048], P(('col', 'row'))
- grad_up: float32 [2048, 8192], P('row', 'col')
- grad_up_bias: float32 [8192], P(('col', 'row'))
- grad_down: float32 [8192, 2048], P('col', 'row')
- grad_down_bias: float32 [2048], P(('col', 'row'))
- grad_ln_gain: float32 [2048], P(('col', 'row'))
- grad_ln_bias: float32 [2048], P(('col', 'row'))
The draws below stay inside these ranges and needn't reach their ends.
Inputs may be any that keep to these rules, and one draw needn't show every extreme that they name: `seq_lengths`: row r holds the lengths of the 2 sequences of group r in order; in every row one length is 768 and the other 256, in either order.
All inputs are finite; a program needn't handle non-finite values.
Results may differ from the reference program's by a relative error of at most 0.01.
Values may be sent and summed in bfloat16 or wider, within the bound.
No kernel may reach another device: no remote copies, remote signals or barrier semaphores. Data moves between devices by JAX's collectives and lax.ppermute only.
A program may use at most 128 MiB of HBM per device.

```python
import math
import jax
import jax.numpy as jnp
from jax import lax

D = 2048
HEADS = 32
HEAD_DIM = 64
FF = 8192
ROT = 32
TOK_ROW = 1024
MOST = 768
TOKENS = 8192
N_ROW = 8


def draw_seq_lengths(key, part):
    key = jax.random.fold_in(key, 11)
    order = jax.random.randint(key, (N_ROW,), 0, 2).astype(jnp.int32)
    first = jnp.where(order == 1, MOST, TOK_ROW - MOST).astype(jnp.int32)
    second = (TOK_ROW - first).astype(jnp.int32)
    return jnp.stack([first, second], axis=1).astype(jnp.int32)


def block_levels(rng, shape, split, smallest, top_value):
    gain = 1.0
    for position, blocks in split:
        steps = jax.random.uniform(jax.random.fold_in(jax.random.fold_in(rng, 6), position), (blocks,), jnp.float32, smallest / len(split), top_value / len(split))
        gain = gain * jnp.repeat(jnp.exp(steps), shape[position] // blocks).reshape((-1,) + (1,) * (len(shape) - 1 - position))
    return gain


def scatter_about(key, shape, deviation, bound, cuts=(), held_as=jnp.bfloat16):
    level = block_levels(key, shape, cuts, -0.22, 0.18) if cuts else 1.0
    array = jax.random.normal(key, shape, jnp.float32) * deviation * level
    return jnp.minimum(jnp.maximum(array, -bound), bound).astype(held_as)


def setup_inputs(seed: int = 0) -> dict:
    arg_keys = jax.random.split(jax.random.key(seed), 14)
    return {
        "inputs": scatter_about(arg_keys[0], (TOKENS, D), 1.0, 6.0, ((0, 8), (1, 16))),
        "seq_lengths": draw_seq_lengths(jax.random.fold_in(arg_keys[13], 71), 0),
        "query_key_value_weight": scatter_about(arg_keys[2], (D, 3, D), D ** -0.5, 0.125, ((0, 8), (2, 16))),
        "query_key_value_bias": scatter_about(arg_keys[3], (3, D), 0.3, 1.796875, ((1, 128),)),
        "w_out": scatter_about(arg_keys[4], (D, D), (max(4, D // 256)) ** -0.5, 2.0, ((0, 16), (1, 8))),
        "b_out": scatter_about(arg_keys[5], (D,), 0.3, 1.796875, ((0, 128),)),
        "w_up": scatter_about(arg_keys[6], (D, FF), D ** -0.5, 0.125, ((0, 8), (1, 16))),
        "b_up": scatter_about(arg_keys[7], (FF,), 0.3, 1.796875, ((0, 128),)),
        "w_down": scatter_about(arg_keys[8], (FF, D), FF ** -0.5, 0.0625, ((0, 16), (1, 8))),
        "b_down": scatter_about(arg_keys[9], (D,), 0.3, 1.796875, ((0, 128),)),
        "ln_gain": jnp.clip(1.0 + 0.1 * jax.random.normal(arg_keys[10], (D,), jnp.float32), 0.5, 1.5).astype(jnp.bfloat16),
        "ln_bias": scatter_about(arg_keys[11], (D,), 0.3, 1.796875, ((0, 128),)),
        "cotangent": scatter_about(arg_keys[12], (TOKENS, D), 1.0, 6.0, ((0, 8), (1, 16))),
    }


NORM_EPSILON = 1e-05
EXACT_PRECISION = lax.Precision.HIGHEST

@jax.custom_vjp
def low(v):
    return lax.optimization_barrier(v.astype(jnp.bfloat16)).astype(jnp.float32)

@jax.custom_vjp
def lowered_backward(v):
    return v

def low_keep(v):
    return (low(v), None)

def low_pass(kept, grad):
    return (grad,)

def back_keep(v):
    return (v, None)

def back_low(kept, grad):
    return (low(grad),)
low.defvjp(low_keep, low_pass)
lowered_backward.defvjp(back_keep, back_low)

def gelu_tanh(pre_act):
    return 0.5 * pre_act * (1.0 + jnp.tanh(0.7978845608028654 * (pre_act + 0.044715 * pre_act * pre_act * pre_act)))

def doc_layout(lengths_row, rows_here):
    doc_ends = jnp.cumsum(lengths_row).astype(jnp.int32)
    doc_starts = (doc_ends - lengths_row).astype(jnp.int32)
    row_places = jnp.arange(rows_here, dtype=jnp.int32)
    doc_ids = lax.optimization_barrier(jnp.sum((row_places[:, None] >= doc_ends[None, :]).astype(jnp.int32), axis=1)).astype(jnp.int32)
    member = doc_ids[:, None] == jnp.arange(lengths_row.shape[0], dtype=jnp.int32)[None, :]
    doc_begin = lax.optimization_barrier(jnp.sum(jnp.where(member, doc_starts[None, :], 0), axis=1)).astype(jnp.int32)
    return (doc_ids, (row_places - doc_begin).astype(jnp.int32))

def rotary_tables(positions):
    half_rot = ROT // 2
    inverse = 10000.0 ** (-2.0 * jnp.arange(half_rot, dtype=jnp.float32) / ROT)
    angles = positions.astype(jnp.float32)[:, None] * inverse[None, :]
    return (jnp.cos(angles), jnp.sin(angles))

def rotate(heads_in, cosine, sine_table):
    half_rot = ROT // 2
    first_half = heads_in[..., :half_rot]
    second_half = heads_in[..., half_rot:ROT]
    cos_wide = cosine[:, None, :]
    sin_wide = sine_table[:, None, :]
    return jnp.concatenate([first_half * cos_wide - second_half * sin_wide, second_half * cos_wide + first_half * sin_wide, heads_in[..., ROT:]], axis=-1)

def layer(params, activations, doc_ids, positions):
    query_key_value_weight, query_key_value_bias, w_out, b_out, w_up, b_up, w_down, b_down, ln_gain, ln_bias = params
    rows_here = activations.shape[0]
    row_mean = lax.optimization_barrier(jnp.mean(activations, axis=1, keepdims=True))
    row_square = lax.optimization_barrier(jnp.mean(activations * activations, axis=1, keepdims=True))
    inv_std = lax.rsqrt(row_square - row_mean * row_mean + NORM_EPSILON)
    normalized_rows = low((activations - row_mean) * inv_std * ln_gain + ln_bias)
    query_key_value_mixed = lowered_backward(jnp.einsum('wg,gkm->wkm', normalized_rows, query_key_value_weight, precision=EXACT_PRECISION) + query_key_value_bias)
    cosine, sine_table = rotary_tables(positions)
    queries = low(rotate(query_key_value_mixed[:, 0].reshape(rows_here, HEADS, HEAD_DIM), cosine, sine_table))
    keys_all = low(rotate(query_key_value_mixed[:, 1].reshape(rows_here, HEADS, HEAD_DIM), cosine, sine_table))
    values_all = low(query_key_value_mixed[:, 2].reshape(rows_here, HEADS, HEAD_DIM))
    block_rows = min(512, rows_here)
    score_scale = 1.0 / math.sqrt(HEAD_DIM)
    key_places = jnp.arange(rows_here, dtype=jnp.int32)

    def one_block(block_index):
        first_row = (block_index * block_rows).astype(jnp.int32)
        q_block = lax.dynamic_slice_in_dim(queries, first_row, block_rows, 0)
        doc_block = lax.dynamic_slice_in_dim(doc_ids, first_row, block_rows, 0)
        query_places = first_row + jnp.arange(block_rows, dtype=jnp.int32)
        allowed = (doc_block[:, None] == doc_ids[None, :]) & (query_places[:, None] >= key_places[None, :])
        raw_scores = lowered_backward(jnp.einsum('qhd,khd->hqk', q_block, keys_all, precision=EXACT_PRECISION))
        scores = jnp.where(allowed[None], raw_scores * score_scale, -1e+30)
        row_max = lax.optimization_barrier(jnp.max(scores, axis=-1, keepdims=True))
        exp_scores = jnp.exp(scores - row_max)
        attn_probs = low(exp_scores / lax.optimization_barrier(jnp.sum(exp_scores, axis=-1, keepdims=True)))
        return jnp.einsum('hqk,khd->qhd', attn_probs, values_all, precision=EXACT_PRECISION)
    attended = lax.map(jax.checkpoint(one_block), jnp.arange(rows_here // block_rows, dtype=jnp.int32))
    attended = low(lowered_backward(attended.reshape(rows_here, D)))
    attn_branch = jnp.dot(attended, w_out, precision=EXACT_PRECISION) + b_out
    hidden_pre = lowered_backward(jnp.dot(normalized_rows, w_up, precision=EXACT_PRECISION) + b_up)
    hidden_act = low(gelu_tanh(hidden_pre))
    mlp_branch = jnp.dot(hidden_act, w_down, precision=EXACT_PRECISION) + b_down
    return activations + attn_branch + mlp_branch

def reference(inputs, seq_lengths, query_key_value_weight, query_key_value_bias, w_out, b_out, w_up, b_up, w_down, b_down, ln_gain, ln_bias, cotangent):
    params = (query_key_value_weight.astype(jnp.float32), query_key_value_bias.astype(jnp.float32), w_out.astype(jnp.float32), b_out.astype(jnp.float32), w_up.astype(jnp.float32), b_up.astype(jnp.float32), w_down.astype(jnp.float32), b_down.astype(jnp.float32), ln_gain.astype(jnp.float32), ln_bias.astype(jnp.float32))
    rows_here = TOK_ROW
    groups_in = inputs.astype(jnp.float32).reshape(N_ROW, rows_here, D)
    groups_cot = cotangent.astype(jnp.float32).reshape(N_ROW, rows_here, D)

    def group_step(totals, group_data):
        group_in, group_cot, group_lengths = group_data
        doc_ids, positions = doc_layout(group_lengths, rows_here)
        result, pullback = jax.vjp(lambda weights, activations: layer(weights, activations, doc_ids, positions), params, group_in)
        param_grads, input_grad = pullback(group_cot)
        totals = jax.tree.map(lambda left_sum, right_sum: left_sum + right_sum, totals, param_grads)
        return (totals, (result, input_grad))
    zero_grads = tuple((jnp.zeros_like(param_item) for param_item in params))
    totals, (results, input_grads) = lax.scan(group_step, zero_grads, (groups_in, groups_cot, seq_lengths))
    g_qkv, g_qkv_bias, g_out, g_out_bias, g_up, g_up_bias, g_down, g_down_bias, g_gain, g_shift = totals
    return (results.reshape(TOKENS, D).astype(jnp.bfloat16), input_grads.reshape(TOKENS, D), g_qkv, g_qkv_bias, g_out, g_out_bias, g_up, g_up_bias, g_down, g_down_bias, g_gain, g_shift)
```

```python
import functools

import jax
import jax.numpy as jnp
from jax import lax
from jax.experimental import pallas as pl
from jax.experimental.pallas import tpu as pltpu
from jax.sharding import PartitionSpec as P

D = 2048
HEAD_DIM = 64
ROT = 32
EPS = 1e-05
TOK = 1024
HALF = 512
QKV = 384
FFL = 512
CAT = QKV + FFL
ACT = 128 + FFL
PAD = 16
BLK = 256
F32 = jnp.float32
BF16 = jnp.bfloat16
VMEM_LIMIT = 52 * 1024 * 1024

MASKS = ((1, 3), (3, 1))


def exchange(value, axis, step=0):
    pairs = []
    for z in range(4):
        for k in range(2):
            m = MASKS[k][step]
            for y in range(4):
                for x in range(4):
                    to = {
                        "x": (x ^ m, y, z, k),
                        "y": (x, y ^ m, z, k),
                        "z": (x, y, z ^ m, k),
                        "c": (x, y, z, 1 - k),
                    }[axis]
                    pairs.append(((z * 2 + k) * 16 + y * 4 + x, (to[2] * 2 + to[3]) * 16 + to[1] * 4 + to[0]))
    return lax.ppermute(value, ("row", "col"), pairs)


def cat(*parts):
    return jnp.concatenate(parts, axis=0)


def gather_plane(piece, first, second):
    p0 = piece[None]
    p1 = exchange(p0, first, 0)
    p2 = exchange(cat(p0, p1), first, 1)
    p3 = exchange(cat(p0, p1, p2), second, 0)
    p4 = exchange(cat(p0, p1, p2, p3), second, 1)
    return p0, p1, p2, p3, p4


def gather_row(piece):
    p0 = piece[None]
    p1 = exchange(p0, "z", 0)
    both = cat(p0, p1)
    c1 = exchange(both, "c")
    p2 = exchange(both, "z", 1)
    c2 = exchange(p2, "c")
    return p0, p1, p2, c1, c2


def scatter_step(kept, axis, step):
    half = kept.shape[0] // 2
    got = exchange(kept[half:].astype(BF16), axis, step)
    return kept[:half].astype(F32) + got.astype(F32)


def scatter_plane(blocks, first, second):
    kept = scatter_step(blocks, first, 0)
    kept = scatter_step(kept, first, 1)
    kept = scatter_step(kept, second, 0)
    return scatter_step(kept, second, 1)[0]


def scatter_row(blocks):
    kept = scatter_step(blocks, "c", 0)
    kept = scatter_step(kept, "z", 0)
    return scatter_step(kept, "z", 1)[0]


PIECES = (1, 1, 2, 4, 8)
ROW_PIECES = (1, 1, 2, 2, 2)
PIECE_OF = [(a, i) for a, n in enumerate(PIECES) for i in range(n)]
ROW_PIECE_OF = [(a, i) for a, n in enumerate(ROW_PIECES) for i in range(n)]


def dot(a, b, dims):
    return lax.dot_general(a, b, (dims, ((), ())), preferred_element_type=F32)


NN = ((1,), (0,))
NT = ((1,), (1,))
TN = ((0,), (0,))


def gelu_parts(v):
    inner = 0.7978845608028654 * (v + 0.044715 * v * v * v)
    return jnp.tanh(inner)


def any_spec():
    return pl.BlockSpec(memory_space=pl.ANY)


def params():
    return pltpu.CompilerParams(vmem_limit_bytes=VMEM_LIMIT, dimension_semantics=("arbitrary",))


def norm_kernel(tab, *refs):
    xa, xb, tiny, wts = refs[0:5], refs[5:10], refs[10:15], refs[15:20]
    cos_ref, sa_ref, sb_ref = refs[20:23]
    normed_ref, qkv_ref, pre_ref, act_ref, cen_ref, inv_ref = refs[23:29]
    xs, gb, wn, wb, gb_raw, sem_x, sem_t, sem_w, sem_b = refs[29:]
    step = pl.program_id(0)

    def x_copy(half, j):
        a, i = PIECE_OF[j]
        src = (xa, xb)[half][a].at[i]
        col = pl.multiple_of(tab[half * 16 + j] * 128, 128)
        return pltpu.make_async_copy(src, xs.at[pl.ds(half * HALF, HALF), pl.ds(col, 128)], sem_x.at[half * 16 + j])

    def t_copy(j):
        a, i = PIECE_OF[j]
        col = pl.multiple_of(tab[j] * 128, 128)
        return pltpu.make_async_copy(tiny[a].at[i], gb_raw.at[:, pl.ds(col, 128)], sem_t.at[j])

    def w_copy(j):
        a, i = ROW_PIECE_OF[j]
        row = pl.multiple_of(tab[32 + j] * BLK, BLK)
        return pltpu.make_async_copy(wts[a].at[i, pl.ds(0, BLK)], wn.at[pl.ds(row, BLK)], sem_w.at[j])

    def b_copy(j):
        a, i = ROW_PIECE_OF[j]
        return pltpu.make_async_copy(wts[a].at[i, pl.ds(BLK, PAD)], wb.at[j], sem_b.at[j])

    @pl.when(step == 0)
    def _():
        for j in range(16):
            x_copy(0, j).start()
            t_copy(j).start()
        for j in range(8):
            b_copy(j).start()
            w_copy(j).start()
        for j in range(16):
            x_copy(1, j).start()
        for j in range(16):
            x_copy(0, j).wait()
            t_copy(j).wait()
        gb[...] = gb_raw[...].astype(F32)

    @pl.when(step == 2)
    def _():
        for j in range(16):
            x_copy(1, j).wait()

    base = step * BLK
    own = pl.multiple_of(tab[0] * 128, 128)

    @pl.loop(0, BLK // 16)
    def _(t):
        rows = pl.ds(pl.multiple_of(base + t * 16, 16), 16)
        here = pl.ds(pl.multiple_of(t * 16, 16), 16)
        x = xs[rows, :].astype(F32)
        mean = jnp.sum(x, axis=1, keepdims=True) * (1.0 / D)
        square = jnp.sum(x * x, axis=1, keepdims=True) * (1.0 / D)
        inv = lax.rsqrt(square - mean * mean + EPS)
        normed_ref[here, :] = ((x - mean) * inv * gb[0:1, :] + gb[1:2, :]).astype(BF16)
        mine = xs[rows, pl.ds(own, 128)].astype(F32)
        cen_ref[here, :] = (mine - mean) * inv
        inv_ref[here, :] = jnp.broadcast_to(inv, (16, 128))

    @pl.when(step == 0)
    def _():
        for j in range(8):
            b_copy(j).wait()
            w_copy(j).wait()

    bias = wb[0].astype(F32)
    for j in range(1, 8):
        bias = bias + wb[j].astype(F32)
    bias = bias[0:1, :]
    normed = normed_ref[...]
    mixed = dot(normed, wn[:, 0:QKV], NN) + bias[:, 0:QKV]
    for s in range(2):
        v = mixed[:, s * 128 : (s + 1) * 128]
        v = v * cos_ref[...] + pltpu.roll(v, 128 - 16, 1) * sa_ref[...] + pltpu.roll(v, 16, 1) * sb_ref[...]
        qkv_ref[:, s * 128 : (s + 1) * 128] = v.astype(BF16)
    qkv_ref[:, 256:384] = mixed[:, 256:384].astype(BF16)
    pre = dot(normed, wn[:, QKV:CAT], NN) + bias[:, QKV:CAT]
    pre_ref[...] = pre
    act_ref[...] = (0.5 * pre * (1.0 + gelu_parts(pre))).astype(BF16)


def norm_call(tab, xa, xb, tiny, wts, cos, sa, sb):
    row_block = lambda width: pl.BlockSpec((BLK, width), lambda i, t: (i, 0))
    return pl.pallas_call(
        norm_kernel,
        grid_spec=pltpu.PrefetchScalarGridSpec(
            num_scalar_prefetch=1,
            grid=(TOK // BLK,),
            in_specs=[any_spec()] * 20 + [row_block(128)] * 3,
            out_specs=[row_block(D), row_block(QKV), row_block(FFL), row_block(FFL), row_block(128), row_block(128)],
            scratch_shapes=[
                pltpu.VMEM((TOK, D), BF16),
                pltpu.VMEM((PAD, D), F32),
                pltpu.VMEM((D, CAT), BF16),
                pltpu.VMEM((8, PAD, CAT), BF16),
                pltpu.VMEM((PAD, D), BF16),
                pltpu.SemaphoreType.DMA((32,)),
                pltpu.SemaphoreType.DMA((16,)),
                pltpu.SemaphoreType.DMA((8,)),
                pltpu.SemaphoreType.DMA((8,)),
            ],
        ),
        out_shape=[
            jax.ShapeDtypeStruct((TOK, D), BF16),
            jax.ShapeDtypeStruct((TOK, QKV), BF16),
            jax.ShapeDtypeStruct((TOK, FFL), F32),
            jax.ShapeDtypeStruct((TOK, FFL), BF16),
            jax.ShapeDtypeStruct((TOK, 128), F32),
            jax.ShapeDtypeStruct((TOK, 128), F32),
        ],
        compiler_params=params(),
        cost_estimate=pl.CostEstimate(flops=2 * TOK * D * CAT, bytes_accessed=16 * 2**20, transcendentals=TOK * FFL),
        name="norm_proj",
    )(tab, *xa, *xb, *tiny, *wts, cos, sa, sb)


def head_masks():
    lane = lax.broadcasted_iota(jnp.int32, (1, 128), 1)
    return [(lane < HEAD_DIM).astype(BF16), (lane >= HEAD_DIM).astype(BF16)]


def masked_scores(qh, k, qi):
    s = dot(qh, k, NT)
    row = lax.broadcasted_iota(jnp.int32, (BLK, BLK), 0)
    column = lax.broadcasted_iota(jnp.int32, (BLK, BLK), 1)
    last = jnp.where(row >= column, s[:, qi * BLK :], -1e30)
    return last if qi == 0 else jnp.concatenate([s[:, : qi * BLK], last], axis=1)


def documents(tab):
    return ((tab[0], 3), (tab[1], 1))


def attend_kernel(tab, qkv_ref, out_ref):
    masks = head_masks()
    for start, blocks in documents(tab):
        for qi in range(blocks):
            rows = pl.ds(pl.multiple_of(start + qi * BLK, BLK), BLK)
            keys = pl.ds(pl.multiple_of(start, BLK), (qi + 1) * BLK)
            q = qkv_ref[rows, 0:128] * jnp.asarray(0.125, BF16)
            k = qkv_ref[keys, 128:256]
            v = qkv_ref[keys, 256:384]
            total = None
            for m in masks:
                s = masked_scores(q * m, k, qi)
                e = jnp.exp(s - jnp.max(s, axis=1, keepdims=True))
                p = (e * (1.0 / jnp.sum(e, axis=1, keepdims=True))).astype(BF16)
                o = dot(p, v * m, NN)
                total = o if total is None else total + o
            out_ref[rows, :] = total.astype(BF16)


def attend_call(tab, qkv):
    vmem = pl.BlockSpec(memory_space=pltpu.VMEM)
    return pl.pallas_call(
        attend_kernel,
        in_specs=[pl.BlockSpec(memory_space=pltpu.SMEM), vmem],
        out_specs=vmem,
        out_shape=jax.ShapeDtypeStruct((TOK, 128), BF16),
        compiler_params=pltpu.CompilerParams(vmem_limit_bytes=VMEM_LIMIT),
        cost_estimate=pl.CostEstimate(flops=2**31, bytes_accessed=2**20, transcendentals=2**20),
        name="attend",
    )(tab, qkv)


def attend_back_kernel(tab, qkv_ref, do_ref, cos_ref, sa_ref, sb_ref, out_ref, sum_ref, dq, dk, dv):
    masks = head_masks()
    dk[...] = jnp.zeros_like(dk)
    dv[...] = jnp.zeros_like(dv)
    for start, blocks in documents(tab):
        for qi in range(blocks):
            rows = pl.ds(pl.multiple_of(start + qi * BLK, BLK), BLK)
            keys = pl.ds(pl.multiple_of(start, BLK), (qi + 1) * BLK)
            q = qkv_ref[rows, 0:128]
            k = qkv_ref[keys, 128:256]
            v = qkv_ref[keys, 256:384]
            do = do_ref[rows, :]
            for h, m in enumerate(masks):
                qh = q * m
                doh = do * m
                s = masked_scores(qh * jnp.asarray(0.125, BF16), k, qi)
                e = jnp.exp(s - jnp.max(s, axis=1, keepdims=True))
                p = e * (1.0 / jnp.sum(e, axis=1, keepdims=True))
                dp = dot(doh, v, NT)
                delta = jnp.sum(p * dp, axis=1, keepdims=True)
                ds = (p * (dp - delta) * 0.125).astype(BF16)
                part = dot(ds, k * m, NN)
                if h == 0:
                    dq[rows, :] = part
                else:
                    dq[rows, :] += part
                dk[keys, :] += dot(ds, qh, TN)
                dv[keys, :] += dot(p.astype(BF16), doh, TN)
    for s, ref in enumerate((dq, dk, dv)):
        d = ref[...]
        if s < 2:
            d = d * cos_ref[...] - pltpu.roll(d, 128 - 16, 1) * sa_ref[...] - pltpu.roll(d, 16, 1) * sb_ref[...]
        low = d.astype(BF16)
        out_ref[:, s * 128 : (s + 1) * 128] = low
        sum_ref[:, s * 128 : (s + 1) * 128] = jnp.broadcast_to(jnp.sum(low.astype(F32), axis=0, keepdims=True), (8, 128))


def attend_back_call(tab, qkv, do, cos, sa, sb):
    vmem = pl.BlockSpec(memory_space=pltpu.VMEM)
    return pl.pallas_call(
        attend_back_kernel,
        in_specs=[pl.BlockSpec(memory_space=pltpu.SMEM)] + [vmem] * 5,
        out_specs=[vmem, vmem],
        out_shape=[jax.ShapeDtypeStruct((TOK, QKV), BF16), jax.ShapeDtypeStruct((8, QKV), F32)],
        scratch_shapes=[pltpu.VMEM((TOK, 128), F32)] * 3,
        compiler_params=pltpu.CompilerParams(vmem_limit_bytes=VMEM_LIMIT),
        cost_estimate=pl.CostEstimate(flops=2**33, bytes_accessed=4 * 2**20, transcendentals=2**20),
        name="attend_back",
    )(tab, qkv, do, cos, sa, sb)


def project_kernel(tab, att_ref, act_ref, *refs):
    wts, out_ref, wn, sem = refs[0:5], refs[5], refs[6], refs[7]
    step = pl.program_id(0)

    def w_copy(j):
        a, i = ROW_PIECE_OF[j]
        column = pl.multiple_of(tab[16 + j] * BLK, BLK)
        return pltpu.make_async_copy(wts[a].at[i], wn.at[:, pl.ds(column, BLK)], sem.at[j])

    @pl.when(step == 0)
    def _():
        for j in range(8):
            w_copy(j).start()
        for j in range(8):
            w_copy(j).wait()

    att = att_ref[...]
    act = act_ref[...]
    for r in range(8):
        columns = slice(r * BLK, (r + 1) * BLK)
        part = dot(att, wn[0:128, columns], NN) + dot(act, wn[128:ACT, columns], NN)
        part = part.astype(BF16)
        out_ref[tab[2 * r]] = part[:, 0:128]
        out_ref[tab[2 * r + 1]] = part[:, 128:256]


def project_call(half, tab, att, act, wts):
    first = half * (HALF // BLK)
    return pl.pallas_call(
        project_kernel,
        grid_spec=pltpu.PrefetchScalarGridSpec(
            num_scalar_prefetch=1,
            grid=(HALF // BLK,),
            in_specs=[
                pl.BlockSpec((BLK, 128), lambda i, t: (i + first, 0)),
                pl.BlockSpec((BLK, FFL), lambda i, t: (i + first, 0)),
            ]
            + [any_spec()] * 5,
            out_specs=pl.BlockSpec((16, BLK, 128), lambda i, t: (0, i, 0)),
            scratch_shapes=[pltpu.VMEM((ACT, D), BF16), pltpu.SemaphoreType.DMA((8,))],
        ),
        out_shape=jax.ShapeDtypeStruct((16, HALF, 128), BF16),
        compiler_params=params(),
        cost_estimate=pl.CostEstimate(flops=2 * HALF * D * ACT, bytes_accessed=5 * 2**20, transcendentals=0),
        name="project",
    )(tab, att, act, *wts)


def upstream_kernel(tab, *refs):
    ga, gb, wts, pre_ref = refs[0:5], refs[5:10], refs[10:15], refs[15]
    hid_ref, att_ref, hsum_ref, gsum_ref = refs[16:20]
    gs, wn, sem_g, sem_w = refs[20:]
    step = pl.program_id(0)

    def g_copy(half, j):
        a, i = PIECE_OF[j]
        col = pl.multiple_of(tab[half * 16 + j] * 128, 128)
        return pltpu.make_async_copy(
            (ga, gb)[half][a].at[i], gs.at[pl.ds(half * HALF, HALF), pl.ds(col, 128)], sem_g.at[half * 16 + j]
        )

    def w_copy(j):
        a, i = ROW_PIECE_OF[j]
        column = pl.multiple_of(tab[32 + j] * BLK, BLK)
        return pltpu.make_async_copy(wts[a].at[i], wn.at[:, pl.ds(column, BLK)], sem_w.at[j])

    @pl.when(step == 0)
    def _():
        for j in range(16):
            g_copy(0, j).start()
        for j in range(8):
            w_copy(j).start()
        for j in range(16):
            g_copy(1, j).start()
        for j in range(16):
            g_copy(0, j).wait()
        for j in range(8):
            w_copy(j).wait()
        hsum_ref[...] = jnp.zeros_like(hsum_ref)
        gsum_ref[...] = jnp.zeros_like(gsum_ref)

    @pl.when(step == 2)
    def _():
        for j in range(16):
            g_copy(1, j).wait()

    rows = pl.ds(pl.multiple_of(step * BLK, BLK), BLK)
    g = gs[rows, :]
    att_ref[...] = dot(g, wn[0:128, :], NT).astype(BF16)
    d_act = dot(g, wn[128:ACT, :], NT)
    v = pre_ref[...]
    t = gelu_parts(v)
    slope = 0.5 * (1.0 + t) + 0.5 * v * (1.0 - t * t) * (0.7978845608028654 * (1.0 + 3.0 * 0.044715 * v * v))
    low = (d_act * slope).astype(BF16)
    hid_ref[...] = low
    hsum_ref[...] += jnp.broadcast_to(jnp.sum(low.astype(F32), axis=0, keepdims=True), (8, FFL))
    own = pl.multiple_of(tab[0] * 128, 128)
    mine = gs[rows, pl.ds(own, 128)].astype(F32)
    gsum_ref[...] += jnp.broadcast_to(jnp.sum(mine, axis=0, keepdims=True), (8, 128))


def upstream_call(tab, ga, gb, wts, pre):
    row_block = lambda width: pl.BlockSpec((BLK, width), lambda i, t: (i, 0))
    whole = lambda width: pl.BlockSpec((8, width), lambda i, t: (0, 0))
    return pl.pallas_call(
        upstream_kernel,
        grid_spec=pltpu.PrefetchScalarGridSpec(
            num_scalar_prefetch=1,
            grid=(TOK // BLK,),
            in_specs=[any_spec()] * 15 + [row_block(FFL)],
            out_specs=[row_block(FFL), row_block(128), whole(FFL), whole(128)],
            scratch_shapes=[
                pltpu.VMEM((TOK, D), BF16),
                pltpu.VMEM((ACT, D), BF16),
                pltpu.SemaphoreType.DMA((32,)),
                pltpu.SemaphoreType.DMA((8,)),
            ],
        ),
        out_shape=[
            jax.ShapeDtypeStruct((TOK, FFL), BF16),
            jax.ShapeDtypeStruct((TOK, 128), BF16),
            jax.ShapeDtypeStruct((8, FFL), F32),
            jax.ShapeDtypeStruct((8, 128), F32),
        ],
        compiler_params=params(),
        cost_estimate=pl.CostEstimate(flops=2 * TOK * D * ACT, bytes_accessed=10 * 2**20, transcendentals=TOK * FFL),
        name="upstream",
    )(tab, *ga, *gb, *wts, pre)


def downstream_kernel(tab, dm_ref, dh_ref, normed_ref, *refs):
    tiny, wts, out_ref = refs[0:5], refs[5:10], refs[10]
    wn, gb, sem_w, sem_t = refs[11:]

    def w_copy(j):
        a, i = ROW_PIECE_OF[j]
        row = pl.multiple_of(tab[16 + j] * BLK, BLK)
        return pltpu.make_async_copy(wts[a].at[i, pl.ds(0, BLK)], wn.at[pl.ds(row, BLK)], sem_w.at[j])

    def t_copy(j):
        a, i = PIECE_OF[j]
        col = pl.multiple_of(tab[24 + j] * 128, 128)
        return pltpu.make_async_copy(tiny[a].at[i], gb.at[:, pl.ds(col, 128)], sem_t.at[j])

    for j in range(8):
        w_copy(j).start()
    for j in range(16):
        t_copy(j).start()
    for j in range(8):
        w_copy(j).wait()
    for j in range(16):
        t_copy(j).wait()

    for b in range(HALF // BLK):
        rows = slice(b * BLK, (b + 1) * BLK)
        dm = dm_ref[rows, :]
        dh = dh_ref[rows, :]
        s1 = jnp.zeros((BLK, 128), F32)
        s2 = jnp.zeros((BLK, 128), F32)
        for r in range(8):
            lines = slice(r * BLK, (r + 1) * BLK)
            part = dot(dm, wn[lines, 0:QKV], NT) + dot(dh, wn[lines, QKV:CAT], NT)
            low = part.astype(BF16)
            gain = gb[0:1, lines].astype(F32)
            shift = gb[1:2, lines].astype(F32)
            u1 = part * gain
            u2 = part * (normed_ref[rows, lines].astype(F32) - shift)
            for i in range(2):
                out_ref[tab[2 * r + i], rows, :] = low[:, i * 128 : (i + 1) * 128]
                s1 = s1 + u1[:, i * 128 : (i + 1) * 128]
                s2 = s2 + u2[:, i * 128 : (i + 1) * 128]
        for i in range(BLK // 128):
            lines = slice(i * 128, (i + 1) * 128)
            at = b * 2 + i
            v1 = jnp.sum(jnp.transpose(s1[lines, :]), axis=0, keepdims=True)
            v2 = jnp.sum(jnp.transpose(s2[lines, :]), axis=0, keepdims=True)
            both = jnp.concatenate([v1, v2], axis=0)
            if at == 0:
                sums = [both]
            else:
                sums.append(both)
    flat = jnp.concatenate(sums + [jnp.zeros((8, 128), F32)], axis=0).astype(BF16)
    for c in range(16):
        out_ref[c, HALF : HALF + PAD, :] = flat


def downstream_call(half, tab, dm, dh, normed, tiny, wts):
    rows = lambda width: pl.BlockSpec((HALF, width), lambda i, t: (half, 0))
    return pl.pallas_call(
        downstream_kernel,
        grid_spec=pltpu.PrefetchScalarGridSpec(
            num_scalar_prefetch=1,
            grid=(1,),
            in_specs=[rows(QKV), rows(FFL), rows(D)] + [any_spec()] * 10,
            out_specs=pl.BlockSpec((16, HALF + PAD, 128), lambda i, t: (0, 0, 0)),
            scratch_shapes=[
                pltpu.VMEM((D, CAT), BF16),
                pltpu.VMEM((PAD, D), BF16),
                pltpu.SemaphoreType.DMA((8,)),
                pltpu.SemaphoreType.DMA((16,)),
            ],
        ),
        out_shape=jax.ShapeDtypeStruct((16, HALF + PAD, 128), BF16),
        compiler_params=params(),
        cost_estimate=pl.CostEstimate(flops=2 * HALF * D * CAT, bytes_accessed=8 * 2**20, transcendentals=0),
        name="downstream",
    )(tab, dm, dh, normed, *tiny, *wts)


def grad_cat_kernel(tab, normed_ref, dm_ref, dh_ref, msum_ref, hsum_ref, out_ref):
    normed = normed_ref[...]
    out_ref[0, 0:BLK, 0:QKV] = dot(normed, dm_ref[...], TN).astype(BF16)
    out_ref[0, 0:BLK, QKV:CAT] = dot(normed, dh_ref[...], TN).astype(BF16)
    zero = jnp.zeros((8, CAT), F32)
    sums = jnp.concatenate([msum_ref[...], hsum_ref[...]], axis=1)
    out_ref[0, BLK : BLK + PAD, :] = jnp.concatenate([sums, zero], axis=0).astype(BF16)


def grad_cat_call(tab, normed, dm, dh, msum, hsum):
    whole = lambda rows, width: pl.BlockSpec((rows, width), lambda i, t: (0, 0))
    return pl.pallas_call(
        grad_cat_kernel,
        grid_spec=pltpu.PrefetchScalarGridSpec(
            num_scalar_prefetch=1,
            grid=(8,),
            in_specs=[
                pl.BlockSpec((TOK, BLK), lambda i, t: (0, t[i])),
                whole(TOK, QKV),
                whole(TOK, FFL),
                whole(8, QKV),
                whole(8, FFL),
            ],
            out_specs=pl.BlockSpec((1, BLK + PAD, CAT), lambda i, t: (i, 0, 0)),
        ),
        out_shape=jax.ShapeDtypeStruct((8, BLK + PAD, CAT), BF16),
        compiler_params=params(),
        cost_estimate=pl.CostEstimate(flops=2 * TOK * D * CAT, bytes_accessed=10 * 2**20, transcendentals=0),
        name="grad_cat",
    )(tab, normed, dm, dh, msum, hsum)


def grad_two_kernel(tab, att_ref, act_ref, gsum_ref, *refs):
    ga, gb, out_ref = refs[0:5], refs[5:10], refs[10]
    gs, turned, sem = refs[11:]
    step = pl.program_id(0)

    def g_copy(half, j):
        a, i = PIECE_OF[j]
        col = pl.multiple_of(tab[half * 16 + j] * 128, 128)
        return pltpu.make_async_copy(
            (ga, gb)[half][a].at[i], gs.at[pl.ds(half * HALF, HALF), pl.ds(col, 128)], sem.at[half * 16 + j]
        )

    @pl.when(step == 0)
    def _():
        for half in range(2):
            for j in range(16):
                g_copy(half, j).start()
        turned[0:128, :] = jnp.transpose(att_ref[...])
        turned[128:ACT, :] = jnp.transpose(act_ref[...])
        for half in range(2):
            for j in range(16):
                g_copy(half, j).wait()

    column = pl.multiple_of(tab[32 + step] * BLK, BLK)
    out_ref[0, 0:ACT, :] = dot(turned[...], gs[:, pl.ds(column, BLK)], NN).astype(BF16)
    row = jnp.concatenate([gsum_ref[...], jnp.zeros((8, 128), F32)], axis=1)
    out_ref[0, ACT : ACT + PAD, :] = jnp.concatenate([row, jnp.zeros((8, BLK), F32)], axis=0).astype(BF16)


def grad_two_call(tab, att, act, gsum, ga, gb):
    whole = lambda rows, width: pl.BlockSpec((rows, width), lambda i, t: (0, 0))
    return pl.pallas_call(
        grad_two_kernel,
        grid_spec=pltpu.PrefetchScalarGridSpec(
            num_scalar_prefetch=1,
            grid=(8,),
            in_specs=[whole(TOK, 128), whole(TOK, FFL), whole(8, 128)] + [any_spec()] * 10,
            out_specs=pl.BlockSpec((1, ACT + PAD, BLK), lambda i, t: (i, 0, 0)),
            scratch_shapes=[
                pltpu.VMEM((TOK, D), BF16),
                pltpu.VMEM((ACT, TOK), BF16),
                pltpu.SemaphoreType.DMA((32,)),
            ],
        ),
        out_shape=jax.ShapeDtypeStruct((8, ACT + PAD, BLK), BF16),
        compiler_params=params(),
        cost_estimate=pl.CostEstimate(flops=2 * TOK * D * ACT, bytes_accessed=8 * 2**20, transcendentals=0),
        name="grad_two",
    )(tab, att, act, gsum, *ga, *gb)


def finish_kernel(ra_ref, rb_ref, g_ref, cen_ref, inv_ref, tiny_ref, out_ref, sum_ref):
    gain = tiny_ref[0:1, :].astype(F32)
    total_gain = jnp.zeros((1, 128), F32)
    total_shift = jnp.zeros((1, 128), F32)
    for half, ref in enumerate((ra_ref, rb_ref)):
        sums = jnp.transpose(ref[HALF : HALF + PAD, :]) * (1.0 / D)
        for i in range(HALF // 128):
            here = slice(i * 128, (i + 1) * 128)
            rows = slice(half * HALF + i * 128, half * HALF + (i + 1) * 128)
            d = ref[here, :]
            cen = cen_ref[rows, :]
            total_gain = total_gain + jnp.sum(d * cen, axis=0, keepdims=True)
            total_shift = total_shift + jnp.sum(d, axis=0, keepdims=True)
            m1 = sums[:, 2 * i : 2 * i + 1]
            m2 = sums[:, 2 * i + 1 : 2 * i + 2]
            out_ref[rows, :] = g_ref[rows, :].astype(F32) + inv_ref[rows, :] * (d * gain - m1 - cen * m2)
    sum_ref[...] = jnp.concatenate([total_gain, total_shift, jnp.zeros((6, 128), F32)], axis=0)


def finish_call(ra, rb, g, cen, inv, tiny):
    vmem = pl.BlockSpec(memory_space=pltpu.VMEM)
    return pl.pallas_call(
        finish_kernel,
        in_specs=[vmem] * 6,
        out_specs=[vmem] * 2,
        out_shape=[jax.ShapeDtypeStruct((TOK, 128), F32), jax.ShapeDtypeStruct((8, 128), F32)],
        compiler_params=pltpu.CompilerParams(vmem_limit_bytes=VMEM_LIMIT),
        cost_estimate=pl.CostEstimate(flops=2**21, bytes_accessed=4 * 2**20, transcendentals=0),
        name="finish",
    )(ra, rb, g, cen, inv, tiny)


def rotary_tables(long_start):
    places = jnp.arange(TOK, dtype=jnp.int32)
    begin_second = jnp.where(long_start == 0, 768, 256)
    positions = jnp.where(places >= begin_second, places - begin_second, places)
    lane = jnp.arange(128, dtype=jnp.int32)
    spot = lane % HEAD_DIM
    half = ROT // 2
    inverse = 10000.0 ** (-2.0 * (spot % half).astype(F32) / ROT)
    angles = positions.astype(F32)[:, None] * inverse[None, :]
    turned = (spot < ROT)[None, :]
    cos = jnp.where(turned, jnp.cos(angles), 1.0)
    sine = jnp.sin(angles)
    low = jnp.where((spot < half)[None, :], -sine, 0.0)
    high = jnp.where(((spot >= half) & (spot < ROT))[None, :], sine, 0.0)
    return cos, low, high


def shards(x, lengths, w_qkv, b_qkv, w_out, b_out, w_up, b_up, w_down, b_down, gain, shift, g):
    row = lax.axis_index("row")
    col = lax.axis_index("col")
    z, core, y, xx = row // 2, row % 2, col // 4, col % 4
    m1 = jnp.where(core == 0, 1, 3)
    m2 = 4 - m1
    seen = (0 * m1, m1, m2, 0 * m1 + 2)
    sent = (0 * m1, m2, m1, 0 * m1 + 2)
    cols_a = [(y ^ seen[j // 4]) * 4 + (xx ^ seen[j % 4]) for j in range(16)]
    cols_b = [(y ^ seen[j % 4]) * 4 + (xx ^ seen[j // 4]) for j in range(16)]
    rows_of = [
        z * 2 + core,
        (z ^ m1) * 2 + core,
        (z ^ m2) * 2 + core,
        (z ^ 2) * 2 + core,
        z * 2 + 1 - core,
        (z ^ m2) * 2 + 1 - core,
        (z ^ m1) * 2 + 1 - core,
        (z ^ 2) * 2 + 1 - core,
    ]
    spots = jnp.where(jnp.arange(4) == m1, 2, jnp.where(jnp.arange(4) == m2, 1, jnp.where(jnp.arange(4) == 2, 3, 0)))
    block = jnp.arange(16, dtype=jnp.int32)
    spot_y = spots[(block // 4) ^ y]
    spot_x = spots[(block % 4) ^ xx]
    place_a = spot_y * 4 + spot_x
    place_b = spot_x * 4 + spot_y
    grads_of = [(z ^ sent[i]) * 2 + core for i in range(4)] + [(z ^ seen[i]) * 2 + 1 - core for i in range(4)]
    as_table = lambda *lists: jnp.concatenate(
        [jnp.stack([jnp.asarray(v, jnp.int32) for v in part]) if isinstance(part, list) else part.astype(jnp.int32) for part in lists]
    )
    gather_tab = as_table(cols_a, cols_b, rows_of)
    send_a = as_table(place_a, rows_of, cols_a)
    send_b = as_table(place_b, rows_of, cols_a)
    grads_tab = as_table(grads_of)
    two_tab = as_table(cols_a, cols_b, grads_of)
    first_long = lengths[0, 0] > lengths[0, 1]
    long_start = jnp.where(first_long, 0, 256).astype(jnp.int32)
    docs = jnp.stack([long_start, jnp.where(first_long, 768, 0).astype(jnp.int32)])
    cos, sa, sb = rotary_tables(long_start)

    def spread(v, width):
        wide = jnp.zeros(v.shape[:-1] + (8, width), BF16)
        return lax.dynamic_update_slice_in_dim(wide, v[..., None, :], row, v.ndim - 1).reshape(v.shape[:-1] + (8 * width,))

    four = jnp.concatenate([spread(jnp.stack([gain, shift, b_out, b_down]), 16), jnp.zeros((PAD - 4, 128), BF16)])
    for axis, step in (("c", 0), ("z", 0), ("z", 1)):
        four = four + exchange(four, axis, step)
    tiny = gather_plane(four, "x", "y")
    bias = jnp.concatenate([spread(b_qkv, 16).reshape(1, QKV), spread(b_up, 64)[None]], axis=1)
    w_cat = jnp.concatenate([w_qkv.reshape(256, QKV), w_up], axis=1)
    w_cat = jnp.concatenate([w_cat, bias, jnp.zeros((PAD - 1, CAT), BF16)], axis=0)
    w_two = jnp.concatenate([w_out, w_down], axis=0)

    xa = gather_plane(x[:HALF], "x", "y")
    xb = gather_plane(x[HALF:], "y", "x")
    cats = gather_row(w_cat)
    twos = gather_row(w_two)
    ga = gather_plane(g[:HALF], "x", "y")
    gb = gather_plane(g[HALF:], "y", "x")

    normed, qkv, pre, act, centered, inv = norm_call(gather_tab, xa, xb, tiny, cats, cos, sa, sb)
    att = attend_call(docs, qkv)
    out_a = scatter_plane(project_call(0, send_a, att, act, twos), "y", "x")
    out_b = scatter_plane(project_call(1, send_b, att, act, twos), "x", "y")
    d_hid, d_att, hsum, gsum = upstream_call(gather_tab, ga, gb, twos, pre)
    d_mix, msum = attend_back_call(docs, qkv, d_att, cos, sa, sb)
    back_a = scatter_plane(downstream_call(0, send_a, d_mix, d_hid, normed, tiny, cats), "y", "x")
    back_b = scatter_plane(downstream_call(1, send_b, d_mix, d_hid, normed, tiny, cats), "x", "y")
    two = scatter_row(grad_two_call(two_tab, att, act, gsum, ga, gb))
    cat_grad = scatter_row(grad_cat_call(grads_tab, normed, d_mix, d_hid, msum, hsum))

    block_out = (x.astype(F32) + cat(out_a, out_b) + four[2:3].astype(F32) + four[3:4].astype(F32)).astype(BF16)
    input_grad, sums = finish_call(back_a, back_b, g, centered, inv, four)
    for axis, step in (("c", 0), ("z", 0), ("z", 1)):
        sums = sums + exchange(sums, axis, step)
    mine = lambda v, width: lax.dynamic_slice_in_dim(v, row * width, width, v.ndim - 1)
    out_bias = mine(two[ACT, 0:128], 16)
    return (
        block_out,
        input_grad,
        cat_grad[0:BLK, 0:QKV].reshape(BLK, 3, 128),
        mine(cat_grad[BLK, 0:QKV].reshape(3, 128), 16),
        two[0:128],
        out_bias,
        cat_grad[0:BLK, QKV:CAT],
        mine(cat_grad[BLK, QKV:CAT], 64),
        two[128:ACT],
        out_bias,
        mine(sums[0], 16),
        mine(sums[1], 16),
    )


def solution(mesh):
    both = P(("col", "row"))
    in_specs = (
        P("row", "col"),
        P("row", None),
        P("row", None, "col"),
        P(None, ("col", "row")),
        P("col", "row"),
        both,
        P("row", "col"),
        both,
        P("col", "row"),
        both,
        both,
        both,
        P("row", "col"),
    )
    out_specs = (
        P("row", "col"),
        P("row", "col"),
        P("row", None, "col"),
        P(None, ("col", "row")),
        P("col", "row"),
        both,
        P("row", "col"),
        both,
        P("col", "row"),
        both,
        both,
        both,
    )
    return jax.shard_map(shards, mesh=mesh, in_specs=in_specs, out_specs=out_specs, check_vma=False)
```

```python
import functools
import math

import jax
import jax.numpy as jnp
from jax import lax
from jax.experimental import pallas as pl
from jax.experimental.pallas import tpu as pltpu
from jax.sharding import PartitionSpec as P

D = 2048
HEAD_DIM = 64
ROT = 32
EPS = 1e-05
TOK = 1024
HALF = 512
QKV = 384
FFL = 512
CAT = QKV + FFL
ACT = 128 + FFL
ALL = CAT + ACT
PAD = 16
BLK = 256
F32 = jnp.float32
BF16 = jnp.bfloat16
VMEM_LIMIT = 12 * 1024 * 1024

MASKS = ((1, 3, 2), (3, 1, 2))


def exchange(value, axis, step=0):
    pairs = []
    for z in range(4):
        for k in range(2):
            m = MASKS[k][step]
            for y in range(4):
                for x in range(4):
                    to = {
                        "x": (x ^ m, y, z, k),
                        "y": (x, y ^ m, z, k),
                        "z": (x, y, z ^ m, k),
                        "c": (x, y, z, 1 - k),
                    }[axis]
                    pairs.append(((z * 2 + k) * 16 + y * 4 + x, (to[2] * 2 + to[3]) * 16 + to[1] * 4 + to[0]))
    return lax.ppermute(value, ("row", "col"), pairs)


def scatter_step(kept, axis, step):
    half = kept.shape[0] // 2
    got = exchange(kept[half:].astype(BF16), axis, step)
    return kept[:half].astype(F32) + got.astype(F32)


def scatter_row(blocks):
    kept = scatter_step(blocks, "c", 0)
    kept = scatter_step(kept, "z", 0)
    return scatter_step(kept, "z", 1)[0]


PIECE_OF = [(i // 8, i % 8) for i in range(16)]
ROW_PIECES = (2, 2, 2, 2)
GRAD_ORDER = (0, 2, 1, 3, 4, 6, 5, 7)
NN = ((1,), (0,))
NT = ((1,), (1,))
TN = ((0,), (0,))


def dot(a, b, dims):
    return lax.dot_general(a, b, (dims, ((), ())), preferred_element_type=F32)


def weight_blocks(refs):
    first = 0
    for n, ref in zip(ROW_PIECES, refs):
        yield first, n, ref
        first += n


def weight_of(refs, j):
    for first, n, ref in weight_blocks(refs):
        if first <= j < first + n:
            return ref.at[j - first]


def gelu_tanh_part(v):
    return jnp.tanh(0.7978845608028654 * (v + 0.044715 * v * v * v))


def vmem():
    return pl.BlockSpec(memory_space=pltpu.VMEM)


def smem():
    return pl.BlockSpec(memory_space=pltpu.SMEM)


def any_spec():
    return pl.BlockSpec(memory_space=pl.ANY)


def shape(dims, dtype):
    return jax.ShapeDtypeStruct(dims, dtype)


def call(name, kernel, specs, outs, args, flops, scratch=(), transcendentals=0, after=()):
    if after:
        body, n = kernel, len(args)
        kernel = lambda *refs: body(*refs[:n], *refs[n + len(after) :])
        specs = list(specs) + [any_spec()] * len(after)
    moved = sum(int(a.size) * a.dtype.itemsize for a in args) + sum(math.prod(o.shape) * o.dtype.itemsize for o in outs)
    return pl.pallas_call(
        kernel,
        in_specs=specs,
        out_specs=[vmem()] * len(outs),
        out_shape=outs,
        scratch_shapes=list(scratch),
        compiler_params=pltpu.CompilerParams(vmem_limit_bytes=VMEM_LIMIT),
        cost_estimate=pl.CostEstimate(flops=flops, bytes_accessed=moved, transcendentals=transcendentals),
        name=name,
    )(*args, *after)


def norm_kernel(tab, *refs):
    halves, tiny, wts = (refs[0:2], refs[2:4]), refs[4:6], refs[6:10]
    cos_ref, sa_ref, sb_ref = refs[10:13]
    normed_ref, qkv_ref, pre_ref, act_ref, cen_ref, inv_ref, gb_ref = refs[13:]

    def lane(half, i):
        return pl.multiple_of(tab[half * 16 + i] * 128, 128)

    def tiny_row(i, row):
        a, k = PIECE_OF[i]
        return tiny[a][k, row : row + 1, :].astype(F32)

    for i in range(16):
        a, k = PIECE_OF[i]
        gb_ref[:, pl.ds(lane(0, i), 128)] = tiny[a][k].astype(F32)[0:8]
    bias = jnp.concatenate([tiny_row(0, 4 + i) for i in range(7)], axis=1)

    for half in range(2):
        pieces = halves[half]

        def chunk(t, _, half=half, pieces=pieces):
            here = pl.ds(pl.multiple_of(t * 16, 16), 16)
            rows = pl.ds(pl.multiple_of(half * HALF + t * 16, 16), 16)
            xs = [pieces[a][k, here, :].astype(F32) for a, k in PIECE_OF]
            total = xs[0]
            square = xs[0] * xs[0]
            for x in xs[1:]:
                total = total + x
                square = square + x * x
            mean = jnp.sum(total, axis=1, keepdims=True) * (1.0 / D)
            square = jnp.sum(square, axis=1, keepdims=True) * (1.0 / D)
            inv = lax.rsqrt(square - mean * mean + EPS)
            for i, x in enumerate(xs):
                j = i if half == 0 else (i % 4) * 4 + i // 4
                centered = (x - mean) * inv
                if i == 0:
                    cen_ref[rows, :] = centered
                normed_ref[rows, pl.ds(lane(half, i), 128)] = (centered * tiny_row(j, 0) + tiny_row(j, 1)).astype(BF16)
            inv_ref[rows, :] = jnp.broadcast_to(inv, (16, 128))
            return _

        lax.fori_loop(0, HALF // 16, chunk, 0, unroll=4)

    @pl.loop(0, TOK // BLK)
    def _(t):
        rows = pl.ds(pl.multiple_of(t * BLK, BLK), BLK)
        mixed = bias
        for first, n, ref in weight_blocks(wts):
            lines = slice(first * BLK, (first + n) * BLK)
            mixed = mixed + dot(normed_ref[rows, lines], ref[...].reshape(n * BLK, CAT), NN)
        for s in range(2):
            v = mixed[:, s * 128 : (s + 1) * 128]
            v = v * cos_ref[rows, :] + pltpu.roll(v, 128 - 16, 1) * sa_ref[rows, :] + pltpu.roll(v, 16, 1) * sb_ref[rows, :]
            qkv_ref[rows, s * 128 : (s + 1) * 128] = v.astype(BF16)
        qkv_ref[rows, 256:384] = mixed[:, 256:384].astype(BF16)
        pre = mixed[:, QKV:CAT]
        pre_ref[rows, :] = pre
        act_ref[rows, :] = (0.5 * pre * (1.0 + gelu_tanh_part(pre))).astype(BF16)


def norm_call(tab, xa, xb, tiny, wts, cos, sa, sb):
    outs = [
        shape((TOK, D), BF16),
        shape((TOK, QKV), BF16),
        shape((TOK, FFL), F32),
        shape((TOK, FFL), BF16),
        shape((TOK, 128), F32),
        shape((TOK, 128), F32),
        shape((8, D), F32),
    ]
    args = (tab, *xa, *xb, *tiny, *wts, cos, sa, sb)
    return call("norm_proj", norm_kernel, [smem()] + [vmem()] * 13, outs, args, 2 * TOK * D * CAT, (), TOK * FFL)


def head_masks():
    lane = lax.broadcasted_iota(jnp.int32, (1, 128), 1)
    return [(lane < HEAD_DIM).astype(BF16), (lane >= HEAD_DIM).astype(BF16)]


def masked_scores(qh, k, qi):
    s = dot(qh, k, NT)
    row = lax.broadcasted_iota(jnp.int32, (BLK, BLK), 0)
    column = lax.broadcasted_iota(jnp.int32, (BLK, BLK), 1)
    last = jnp.where(row >= column, s[:, qi * BLK :], -1e30)
    return last if qi == 0 else jnp.concatenate([s[:, : qi * BLK], last], axis=1)


def documents(tab):
    return ((tab[0], 3), (tab[1], 1))


def attend_kernel(tab, qkv_ref, out_ref):
    masks = head_masks()
    for start, blocks in documents(tab):
        for qi in range(blocks):
            rows = pl.ds(pl.multiple_of(start + qi * BLK, BLK), BLK)
            keys = pl.ds(pl.multiple_of(start, BLK), (qi + 1) * BLK)
            q = qkv_ref[rows, 0:128] * jnp.asarray(0.125, BF16)
            k = qkv_ref[keys, 128:256]
            v = qkv_ref[keys, 256:384]
            total = None
            for m in masks:
                s = masked_scores(q * m, k, qi)
                e = jnp.exp(s - jnp.max(s, axis=1, keepdims=True))
                p = (e * (1.0 / jnp.sum(e, axis=1, keepdims=True))).astype(BF16)
                o = dot(p, v * m, NN)
                total = o if total is None else total + o
            out_ref[rows, :] = total.astype(BF16)


def attend_call(tab, qkv):
    outs = [shape((TOK, 128), BF16)]
    return call("attend", attend_kernel, [smem(), vmem()], outs, (tab, qkv), 2**31, (), 2**20)[0]


def attend_back_kernel(tab, qkv_ref, do_ref, cos_ref, sa_ref, sb_ref, out_ref, sum_ref, dq, dk, dv):
    masks = head_masks()
    dk[...] = jnp.zeros_like(dk)
    dv[...] = jnp.zeros_like(dv)
    for start, blocks in documents(tab):
        for qi in range(blocks):
            rows = pl.ds(pl.multiple_of(start + qi * BLK, BLK), BLK)
            keys = pl.ds(pl.multiple_of(start, BLK), (qi + 1) * BLK)
            q = qkv_ref[rows, 0:128]
            k = qkv_ref[keys, 128:256]
            v = qkv_ref[keys, 256:384]
            do = do_ref[rows, :]
            for h, m in enumerate(masks):
                qh = q * m
                doh = do * m
                s = masked_scores(qh * jnp.asarray(0.125, BF16), k, qi)
                e = jnp.exp(s - jnp.max(s, axis=1, keepdims=True))
                p = e * (1.0 / jnp.sum(e, axis=1, keepdims=True))
                dp = dot(doh, v, NT)
                delta = jnp.sum(p * dp, axis=1, keepdims=True)
                ds = (p * (dp - delta) * 0.125).astype(BF16)
                part = dot(ds, k * m, NN)
                if h == 0:
                    dq[rows, :] = part
                else:
                    dq[rows, :] += part
                dk[keys, :] += dot(ds, qh, TN)
                dv[keys, :] += dot(p.astype(BF16), doh, TN)
    for s, ref in enumerate((dq, dk, dv)):
        d = ref[...]
        if s < 2:
            d = d * cos_ref[...] - pltpu.roll(d, 128 - 16, 1) * sa_ref[...] - pltpu.roll(d, 16, 1) * sb_ref[...]
        low = d.astype(BF16)
        out_ref[:, s * 128 : (s + 1) * 128] = low
        sum_ref[:, s * 128 : (s + 1) * 128] = jnp.broadcast_to(jnp.sum(low.astype(F32), axis=0, keepdims=True), (8, 128))


def attend_back_call(tab, qkv, do, cos, sa, sb):
    outs = [shape((TOK, QKV), BF16), shape((8, QKV), F32)]
    scratch = [pltpu.VMEM((TOK, 128), F32)] * 3
    args = (tab, qkv, do, cos, sa, sb)
    return call("attend_back", attend_back_kernel, [smem()] + [vmem()] * 5, outs, args, 2**33, scratch, 2**20)


def project_kernel(half, tab, att_ref, act_ref, *refs):
    wts, out_ref = refs[0:4], refs[4]

    @pl.loop(0, HALF // BLK)
    def _(t):
        rows = pl.ds(pl.multiple_of(half * HALF + t * BLK, BLK), BLK)
        here = pl.ds(pl.multiple_of(t * BLK, BLK), BLK)
        both = jnp.concatenate([att_ref[rows, :], act_ref[rows, :]], axis=1)
        for j in range(8):
            part = dot(both, weight_of(wts, j)[...], NT).astype(BF16)
            out_ref[tab[2 * j], here, :] = part[:, 0:128]
            out_ref[tab[2 * j + 1], here, :] = part[:, 128:256]


def project_call(half, tab, att, act, wts):
    kernel = functools.partial(project_kernel, half)
    outs = [shape((16, HALF, 128), BF16)]
    return call("project", kernel, [smem()] + [vmem()] * 6, outs, (tab, att, act, *wts), 2 * HALF * D * ACT)[0]


def upstream_kernel(tab, *refs):
    halves, wts, pre_ref = (refs[0:2], refs[2:4]), refs[4:8], refs[8]
    g_ref, hid_ref, att_ref, hsum_ref, gsum_ref = refs[9:14]
    mine = jnp.zeros((1, 128), F32)
    for half in range(2):
        for i, (a, k) in enumerate(PIECE_OF):
            lane = pl.multiple_of(tab[half * 16 + i] * 128, 128)
            g_ref[half * HALF : (half + 1) * HALF, pl.ds(lane, 128)] = halves[half][a][k]
        mine = mine + jnp.sum(halves[half][0][0].astype(F32), axis=0, keepdims=True)
    gsum_ref[...] = jnp.broadcast_to(mine, (8, 128))
    hsum_ref[...] = jnp.zeros_like(hsum_ref)

    @pl.loop(0, TOK // BLK)
    def _(t):
        rows = pl.ds(pl.multiple_of(t * BLK, BLK), BLK)
        d_act = None
        for first, n, ref in weight_blocks(wts):
            lines = slice(first * BLK, (first + n) * BLK)
            part = dot(g_ref[rows, lines], ref[...].reshape(n * BLK, ACT), NN)
            d_act = part if d_act is None else d_act + part
        att_ref[rows, :] = d_act[:, 0:128].astype(BF16)
        v = pre_ref[rows, :]
        th = gelu_tanh_part(v)
        slope = 0.5 * (1.0 + th) + 0.5 * v * (1.0 - th * th) * (0.7978845608028654 * (1.0 + 3.0 * 0.044715 * v * v))
        low = (d_act[:, 128:ACT] * slope).astype(BF16)
        hid_ref[rows, :] = low
        hsum_ref[...] += jnp.broadcast_to(jnp.sum(low.astype(F32), axis=0, keepdims=True), (8, FFL))


def upstream_call(tab, ga, gb, wts, pre, after):
    outs = [
        shape((TOK, D), BF16),
        shape((TOK, FFL), BF16),
        shape((TOK, 128), BF16),
        shape((8, FFL), F32),
        shape((8, 128), F32),
    ]
    args = (tab, *ga, *gb, *wts, pre)
    return call("upstream", upstream_kernel, [smem()] + [vmem()] * 9, outs, args, 2 * TOK * D * ACT, (), TOK * FFL, after)


def downstream_kernel(half, tab, dm_ref, dh_ref, normed_ref, gb_ref, *refs):
    wts, out_ref = refs[0:4], refs[4]
    sums = []
    for b in range(HALF // BLK):
        rows = slice(half * HALF + b * BLK, half * HALF + (b + 1) * BLK)
        here = slice(b * BLK, (b + 1) * BLK)
        both = jnp.concatenate([dm_ref[rows, :], dh_ref[rows, :]], axis=1)
        s1 = jnp.zeros((BLK, 128), F32)
        s2 = jnp.zeros((BLK, 128), F32)
        for j in range(8):
            lines = slice(j * BLK, (j + 1) * BLK)
            part = dot(both, weight_of(wts, j)[...], NT)
            low = part.astype(BF16)
            u1 = part * gb_ref[0:1, lines]
            u2 = part * (normed_ref[rows, lines].astype(F32) - gb_ref[1:2, lines])
            for i in range(2):
                cut = slice(i * 128, (i + 1) * 128)
                out_ref[tab[2 * j + i], here, :] = low[:, cut]
                s1 = s1 + u1[:, cut]
                s2 = s2 + u2[:, cut]
        for i in range(BLK // 128):
            cut = slice(i * 128, (i + 1) * 128)
            sums.append(jnp.sum(jnp.transpose(s1[cut, :]), axis=0, keepdims=True))
            sums.append(jnp.sum(jnp.transpose(s2[cut, :]), axis=0, keepdims=True))
    flat = jnp.concatenate(sums + [jnp.zeros((8, 128), F32)], axis=0).astype(BF16)
    for c in range(16):
        out_ref[c, HALF : HALF + PAD, :] = flat


def downstream_call(half, tab, dm, dh, normed, gb, wts, after):
    kernel = functools.partial(downstream_kernel, half)
    outs = [shape((16, HALF + PAD, 128), BF16)]
    args = (tab, dm, dh, normed, gb, *wts)
    return call("downstream", kernel, [smem()] + [vmem()] * 8, outs, args, 2 * HALF * D * CAT, after=after)[0]


def grad_cat_kernel(normed_ref, dm_ref, dh_ref, msum_ref, hsum_ref, out_ref):
    sums = jnp.concatenate([msum_ref[...], hsum_ref[...]], axis=1)
    sums = jnp.concatenate([sums, jnp.zeros((8, CAT), F32)], axis=0).astype(BF16)
    for p, j in enumerate(GRAD_ORDER):
        block = normed_ref[:, j * BLK : (j + 1) * BLK]
        out_ref[p, 0:BLK, 0:QKV] = dot(block, dm_ref[...], TN).astype(BF16)
        out_ref[p, 0:BLK, QKV:CAT] = dot(block, dh_ref[...], TN).astype(BF16)
        out_ref[p, BLK : BLK + PAD, :] = sums


def grad_cat_call(*args, after):
    outs = [shape((8, BLK + PAD, CAT), BF16)]
    return call("grad_cat", grad_cat_kernel, [vmem()] * 5, outs, args, 2 * TOK * D * CAT, after=after)[0]


def grad_two_kernel(att_ref, act_ref, g_ref, gsum_ref, out_ref, turned):
    turned[0:128, :] = jnp.transpose(att_ref[...])
    turned[128:ACT, :] = jnp.transpose(act_ref[...])
    row = jnp.concatenate([gsum_ref[...], jnp.zeros((8, 128), F32)], axis=1)
    row = jnp.concatenate([row, jnp.zeros((8, BLK), F32)], axis=0).astype(BF16)
    for p, j in enumerate(GRAD_ORDER):
        out_ref[p, 0:ACT, :] = dot(turned[...], g_ref[:, j * BLK : (j + 1) * BLK], NN).astype(BF16)
        out_ref[p, ACT : ACT + PAD, :] = row


def grad_two_call(*args, after):
    outs = [shape((8, ACT + PAD, BLK), BF16)]
    scratch = [pltpu.VMEM((ACT, TOK), BF16)]
    return call("grad_two", grad_two_kernel, [vmem()] * 4, outs, args, 2 * TOK * D * ACT, scratch, after=after)[0]


def fold_kernel(blocks, out_ref, back_ref, got_refs, keep_out, keep_back, send):
    for i in range(blocks):
        for ref, rows, keep, first in ((out_ref, HALF, keep_out, 0), (back_ref, HALF + PAD, keep_back, blocks * HALF // 2)):
            if len(got_refs) == 2:
                got = got_refs[ref is back_ref][i]
            else:
                base = (0 if ref is out_ref else blocks * HALF) + i * rows
                got = got_refs[0][base : base + rows, :]
            total = ref[i].astype(F32) + got.astype(F32)
            if i < blocks // 2:
                keep[i] = total
            else:
                at = first + (i - blocks // 2) * rows
                send[at : at + rows, :] = total.astype(BF16)


def fold_call(blocks, out, back, *got):
    half = blocks // 2

    def kernel(out_ref, back_ref, *refs):
        fold_kernel(blocks, out_ref, back_ref, refs[: len(got)], *refs[len(got) :])

    outs = [
        shape((half, HALF, 128), F32),
        shape((half, HALF + PAD, 128), F32),
        shape((half * (2 * HALF + PAD), 128), BF16),
    ]
    return call("fold", kernel, [vmem()] * (2 + len(got)), outs, (out, back, *got), 0)


def finish_kernel(oa, ba, ga, ob, bb, gb, x_ref, g_ref, cen_ref, inv_ref, small_ref, out_ref, grad_ref, sum_ref):
    gain = small_ref[0:1, :].astype(F32)
    shift = small_ref[2:3, :].astype(F32) + small_ref[3:4, :].astype(F32)
    total_gain = jnp.zeros((1, 128), F32)
    total_shift = jnp.zeros((1, 128), F32)
    for half, (o_ref, b_ref, got) in enumerate(((oa, ba, ga), (ob, bb, gb))):
        sums = b_ref[0, HALF : HALF + PAD, :] + got[2 * HALF : 2 * HALF + PAD, :].astype(F32)
        sums = jnp.transpose(sums) * (1.0 / D)
        for i in range(HALF // 128):
            here = slice(i * 128, (i + 1) * 128)
            there = slice(HALF + i * 128, HALF + (i + 1) * 128)
            rows = slice(half * HALF + i * 128, half * HALF + (i + 1) * 128)
            branch = o_ref[0, here, :] + got[here, :].astype(F32)
            out_ref[rows, :] = (x_ref[rows, :].astype(F32) + branch + shift).astype(BF16)
            d = b_ref[0, here, :] + got[there, :].astype(F32)
            cen = cen_ref[rows, :]
            total_gain = total_gain + jnp.sum(d * cen, axis=0, keepdims=True)
            total_shift = total_shift + jnp.sum(d, axis=0, keepdims=True)
            m1 = sums[:, 2 * i : 2 * i + 1]
            m2 = sums[:, 2 * i + 1 : 2 * i + 2]
            grad_ref[rows, :] = g_ref[rows, :].astype(F32) + inv_ref[rows, :] * (d * gain - m1 - cen * m2)
    sum_ref[...] = jnp.concatenate([total_gain, total_shift, jnp.zeros((6, 128), F32)], axis=0)


def finish_call(*args):
    outs = [shape((TOK, 128), BF16), shape((TOK, 128), F32), shape((8, 128), F32)]
    return call("finish", finish_kernel, [vmem()] * 11, outs, args, 2**21)


def join(*parts, after=()):
    parts = [p if isinstance(p, tuple) else (p, 0, p.shape[0]) for p in parts]
    rows = sum(hi - lo for _, lo, hi in parts)

    def kernel(*refs):
        at = 0
        for ref, (_, lo, hi) in zip(refs, parts):
            refs[-1][at : at + hi - lo] = ref[lo:hi]
            at += hi - lo

    first = parts[0][0]
    outs = [shape((rows,) + first.shape[1:], first.dtype)]
    return call("join", kernel, [vmem()] * len(parts), outs, [p[0] for p in parts], 0, after=after)[0]


def begin_kernel(x_ref, g_ref, a_ref, b_ref):
    for half, ref in enumerate((a_ref, b_ref)):
        rows = slice(half * HALF, (half + 1) * HALF)
        ref[0] = x_ref[rows, :]
        ref[1] = g_ref[rows, :]


def begin_call(*args):
    return call("begin", begin_kernel, [vmem()] * 2, [shape((2, HALF, 128), BF16)] * 2, args, 0)


def joined(mine, got, after):
    n = mine.shape[0] // 2
    return join((mine, 0, n), (got, 0, n), (mine, n, 2 * n), (got, n, 2 * n), after=after)


def rotary_tables(long_start):
    places = jnp.arange(TOK, dtype=jnp.int32)
    begin_second = jnp.where(long_start == 0, 768, 256)
    positions = jnp.where(places >= begin_second, places - begin_second, places)
    lane = jnp.arange(128, dtype=jnp.int32)
    spot = lane % HEAD_DIM
    half = ROT // 2
    inverse = 10000.0 ** (-2.0 * (spot % half).astype(F32) / ROT)
    angles = positions.astype(F32)[:, None] * inverse[None, :]
    turned = (spot < ROT)[None, :]
    cos = jnp.where(turned, jnp.cos(angles), 1.0)
    sine = jnp.sin(angles)
    low = jnp.where((spot < half)[None, :], -sine, 0.0)
    high = jnp.where(((spot >= half) & (spot < ROT))[None, :], sine, 0.0)
    return cos, low, high


def shards(x, lengths, w_qkv, b_qkv, w_out, b_out, w_up, b_up, w_down, b_down, gain, shift, g):
    row = lax.axis_index("row")
    col = lax.axis_index("col")
    z, core, y, xx = row // 2, row % 2, col // 4, col % 4
    m1 = jnp.where(core == 0, 1, 3)
    m2 = 4 - m1
    ring = jnp.arange(4, dtype=jnp.int32)
    seen = jnp.stack([0 * m1, m1, m2, 0 * m1 + 2])
    cols_a = ((y ^ seen)[:, None] * 4 + (xx ^ seen)[None, :]).reshape(16)
    cols_b = ((y ^ seen)[None, :] * 4 + (xx ^ seen)[:, None]).reshape(16)
    swapped = jnp.stack([0 * m1, m2, m1, 0 * m1 + 2])
    rows_of = jnp.concatenate([(z ^ seen) * 2 + core, (z ^ swapped) * 2 + 1 - core])
    arrival = jnp.sum(jnp.where(rows_of[None, :] == jnp.arange(8)[:, None], jnp.arange(8)[None, :], 0), axis=1)
    lanes = lambda cols: jnp.sum(jnp.where((cols // 2)[:, None] == jnp.arange(8)[None, :], arrival[None, :], 0), axis=1) * 2 + cols % 2
    gather_tab = jnp.concatenate([lanes(cols_a), lanes(cols_b)]).astype(jnp.int32)
    order = lambda mask: jnp.where(mask == m1, 2, jnp.where(mask == m2, 1, jnp.where(mask == 2, 3, 0)))
    blocks = (rows_of[:, None] * 2 + jnp.arange(2)[None, :]).reshape(16)
    spot_y = order((blocks // 4) ^ y)
    spot_x = order((blocks % 4) ^ xx)
    send_a = (spot_y * 4 + spot_x).astype(jnp.int32)
    send_b = (spot_x * 4 + spot_y).astype(jnp.int32)
    first_long = lengths[0, 0] > lengths[0, 1]
    long_start = jnp.where(first_long, 0, 256).astype(jnp.int32)
    docs = jnp.stack([long_start, jnp.where(first_long, 768, 0).astype(jnp.int32)])
    cos, sa, sb = rotary_tables(long_start)

    def spread(v, width):
        wide = jnp.zeros(v.shape[:-1] + (8, width), BF16)
        return lax.dynamic_update_slice_in_dim(wide, v[..., None, :], row, v.ndim - 1).reshape(-1, 128)

    small = [spread(jnp.stack([gain, shift, b_out, b_down]), 16), spread(b_qkv, 16), spread(b_up, 64)]
    small = jnp.concatenate(small + [jnp.zeros((PAD - 11, 128), BF16)])
    cats = jnp.concatenate([w_qkv.reshape(256, QKV), w_up], axis=1)[None]
    twos = jnp.concatenate([w_out.T, w_down.T], axis=1)[None]
    a1, b1 = begin_call(x, g)
    a1_got, b1_got = exchange(a1, "x", 0), exchange(b1, "y", 0)
    cats_got = exchange(cats, "z", 0)
    small = small + exchange(small, "c")
    small = small + exchange(small, "z", 0)
    step = (a1_got, b1_got, small)
    a2, b2 = joined(a1, a1_got, step), joined(b1, b1_got, step)
    a2_got, b2_got = exchange(a2, "x", 1), exchange(b2, "y", 1)
    twos_got = exchange(join(twos, after=(cats_got,)), "z", 0)
    small = small + exchange(join(small, after=step), "z", 1)
    t1 = small[None]
    t1_got = exchange(t1, "x", 0)
    step = (a2_got, b2_got, t1_got, cats_got)
    a3, b3 = joined(a2, a2_got, step), joined(b2, b2_got, step)
    a3_got, b3_got = exchange(a3, "y", 0), exchange(b3, "x", 0)
    cats = join(cats, cats_got, after=step)
    cats = (cats, exchange(cats, "z", 1), exchange(cats, "c"))
    t2 = join(t1, t1_got, after=step)
    t2_got = exchange(t2, "x", 1)
    t3 = join(t2, t2_got)
    t3_got = exchange(t3, "y", 0)
    step = (a3_got, b3_got, t3_got, twos_got)
    xa, xb = (join((a, 0, 4), (got, 0, 4), after=step) for a, got in ((a3, a3_got), (b3, b3_got)))
    xa, xb = (xa, exchange(xa, "y", 1)), (xb, exchange(xb, "x", 1))
    t4 = join(t3, t3_got, after=step)
    tiny = (t4, exchange(t4, "y", 1))
    twos = join(twos, twos_got, after=step)
    twos = (twos, exchange(twos, "z", 1), exchange(twos, "c"))
    cats = cats + (exchange(cats[1], "c"),)
    step = (xa[1], xb[1])
    ga, gb = (join((a, 4, 8), (got, 4, 8), after=step) for a, got in ((a3, a3_got), (b3, b3_got)))
    ga, gb = (ga, exchange(ga, "y", 1)), (gb, exchange(gb, "x", 1))
    twos = twos + (exchange(twos[1], "c"),)

    normed, qkv, pre, act, centered, inv, gains = norm_call(gather_tab, xa, xb, tiny, cats, cos, sa, sb)
    att = attend_call(docs, qkv)
    out_a = project_call(0, send_a, att, act, twos)
    out_b = project_call(1, send_b, att, act, twos)
    out_a_got, out_b_got = exchange(out_a[8:], "y", 0), exchange(out_b[8:], "x", 0)
    g_all, d_hid, d_att, hsum, gsum = upstream_call(gather_tab, ga, gb, twos, pre, (out_a, out_b))
    d_mix, msum = attend_back_call(docs, qkv, d_att, cos, sa, sb)
    step = (out_a_got, out_b_got)
    back_a = downstream_call(0, send_a, d_mix, d_hid, normed, gains, cats, step)
    back_b = downstream_call(1, send_b, d_mix, d_hid, normed, gains, cats, step)
    back_a_got, back_b_got = exchange(back_a[8:], "y", 0), exchange(back_b[8:], "x", 0)
    two = grad_two_call(att, act, g_all, gsum, after=(back_a, back_b))
    cat_grad = scatter_row(grad_cat_call(normed, d_mix, d_hid, msum, hsum, after=(two,)))
    two = scatter_row(two)
    a = fold_call(8, out_a, back_a, out_a_got, back_a_got)
    b = fold_call(8, out_b, back_b, out_b_got, back_b_got)
    for blocks, axes, n in ((4, "yx", 1), (2, "xy", 0)):
        a = fold_call(blocks, a[0], a[1], exchange(a[2], axes[0], n))
        b = fold_call(blocks, b[0], b[1], exchange(b[2], axes[1], n))
    a = (a[0], a[1], exchange(a[2], "x", 1))
    b = (b[0], b[1], exchange(b[2], "y", 1))
    block_out, input_grad, sums = finish_call(*a, *b, x, g, centered, inv, small)
    sums = sums + exchange(sums, "c")
    sums = sums + exchange(sums, "z", 0) + exchange(sums, "z", 1) + exchange(sums, "z", 2)
    mine = lambda v, width: lax.dynamic_slice_in_dim(v, row * width, width, v.ndim - 1)
    out_bias = mine(two[ACT, 0:128], 16)
    return (
        block_out,
        input_grad,
        cat_grad[0:BLK, 0:QKV].reshape(BLK, 3, 128),
        mine(cat_grad[BLK, 0:QKV].reshape(3, 128), 16),
        two[0:128],
        out_bias,
        cat_grad[0:BLK, QKV:CAT],
        mine(cat_grad[BLK, QKV:CAT], 64),
        two[128:ACT],
        out_bias,
        mine(sums[0], 16),
        mine(sums[1], 16),
    )


def solution(mesh):
    both = P(("col", "row"))
    in_specs = (
        P("row", "col"),
        P("row", None),
        P("row", None, "col"),
        P(None, ("col", "row")),
        P("col", "row"),
        both,
        P("row", "col"),
        both,
        P("col", "row"),
        both,
        both,
        both,
        P("row", "col"),
    )
    out_specs = (
        P("row", "col"),
        P("row", "col"),
        P("row", None, "col"),
        P(None, ("col", "row")),
        P("col", "row"),
        both,
        P("row", "col"),
        both,
        P("col", "row"),
        both,
        both,
        both,
    )
    return jax.shard_map(shards, mesh=mesh, in_specs=in_specs, out_specs=out_specs, check_vma=False)
```

```python
import functools

import jax
import jax.numpy as jnp
from jax import lax
from jax.experimental import pallas as pl
from jax.experimental.pallas import tpu as pltpu
from jax.sharding import PartitionSpec as P

D = 2048
HEAD_DIM = 64
ROT = 32
EPS = 1e-05
TOK = 1024
HALF = 512
QKV = 384
FFL = 512
CAT = QKV + FFL
ACT = 128 + FFL
ALL = CAT + ACT
PAD = 16
BLK = 256
F32 = jnp.float32
BF16 = jnp.bfloat16
MIB = 2**20

MASKS = ((1, 3, 2), (3, 1, 2))


def exchange(value, axis, step=0):
    pairs = []
    for z in range(4):
        for k in range(2):
            m = MASKS[k][step]
            for y in range(4):
                for x in range(4):
                    to = {
                        "x": (x ^ m, y, z, k),
                        "y": (x, y ^ m, z, k),
                        "z": (x, y, z ^ m, k),
                        "c": (x, y, z, 1 - k),
                    }[axis]
                    pairs.append(((z * 2 + k) * 16 + y * 4 + x, (to[2] * 2 + to[3]) * 16 + to[1] * 4 + to[0]))
    return lax.ppermute(value, ("row", "col"), pairs)


PIECE_OF = [(i // 8, i % 8) for i in range(16)]
ROW_PIECES = (4, 4)
NN = ((1,), (0,))
NT = ((1,), (1,))
TN = ((0,), (0,))


def dot(a, b, dims):
    return lax.dot_general(a, b, (dims, ((), ())), preferred_element_type=F32)


def weight_blocks(refs):
    first = 0
    for n, ref in zip(ROW_PIECES, refs):
        yield first, n, ref
        first += n


def weight_of(refs, j):
    for first, n, ref in weight_blocks(refs):
        if first <= j < first + n:
            return ref.at[j - first]


def gelu_tanh_part(v):
    return jnp.tanh(0.7978845608028654 * (v + 0.044715 * v * v * v))


class Place:
    def __init__(self):
        row, col = lax.axis_index("row"), lax.axis_index("col")
        self.row = row
        self.z, self.core, self.y, self.x = lax.div(row, 2), lax.rem(row, 2), lax.div(col, 4), lax.rem(col, 4)
        self.m1 = jnp.where(self.core == 0, 1, 3)
        self.m2 = 4 - self.m1
        self.seen = (0, self.m1, self.m2, 2)

    def swapped(self, mask):
        return jnp.where(mask == self.m2, 1, jnp.where(mask == self.m1, 2, jnp.where(mask == 2, 3, 0)))

    def lane(self, half, i):
        outer, inner = self.seen[i // 4], self.seen[i % 4]
        y, x = (self.y ^ outer, self.x ^ inner) if half == 0 else (self.y ^ inner, self.x ^ outer)
        owner = y * 2 + lax.div(x, 2)
        mask = lax.div(owner, 2) ^ self.z
        same = lax.rem(owner, 2) == self.core
        first = jnp.where(mask == self.m1, 1, jnp.where(mask == self.m2, 2, jnp.where(mask == 2, 3, 0)))
        block = jnp.where(same, first, 4 + self.swapped(mask))
        return pl.multiple_of((block * 2 + lax.rem(x, 2)) * 128, 128)

    def spot(self, half, j, i):
        if j < 4:
            z, core = self.z ^ self.seen[j], self.core
        else:
            z, core = self.z ^ (0, self.m2, self.m1, 2)[j - 4], 1 - self.core
        owner = (z * 2 + core) * 2 + i
        y, x = self.swapped(lax.div(owner, 4) ^ self.y), self.swapped(lax.rem(owner, 4) ^ self.x)
        return y * 4 + x if half == 0 else x * 4 + y


def vmem():
    return pl.BlockSpec(memory_space=pltpu.VMEM)


def smem():
    return pl.BlockSpec(memory_space=pltpu.SMEM)


def any_spec():
    return pl.BlockSpec(memory_space=pl.ANY)


def shape(dims, dtype):
    return jax.ShapeDtypeStruct(dims, dtype)


WORK = dict(norm_proj=9, attend=3, project=5, upstream=6, attend_back=7, downstream=6, grads=11)
VMEM_MIB = dict(norm_proj=7, attend=8, project=7, upstream=7, attend_back=11, downstream=8, grads=8)


def call(name, kernel, specs, outs, args, scratch=(), after=(), final=False):
    if after:
        body, n = kernel, len(args)
        kernel = lambda *refs: body(*refs[:n], *refs[n + len(after) :])
        specs = list(specs) + [any_spec()] * len(after)
    return pl.pallas_call(
        kernel,
        in_specs=specs,
        out_specs=[vmem()] * len(outs),
        out_shape=outs if final else [pltpu.VMEM(o.shape, o.dtype) for o in outs],
        scratch_shapes=list(scratch),
        compiler_params=pltpu.CompilerParams(vmem_limit_bytes=VMEM_MIB.get(name, 3) * MIB),
        cost_estimate=pl.CostEstimate(flops=int(WORK.get(name, 0) * 2.5e8), bytes_accessed=0, transcendentals=0),
        name=name,
    )(*args, *after)


def norm_kernel(*refs):
    place = Place()
    halves, tiny, wts = (refs[0:2], refs[2:4]), refs[4:6], refs[6:8]
    cos_ref, sa_ref, sb_ref = refs[8:11]
    normed_ref, qkv_ref, pre_ref, act_ref, cen_ref, inv_ref, gb_ref = refs[11:]

    lanes = [[place.lane(half, i) for i in range(16)] for half in range(2)]

    def lane(half, i):
        return lanes[half][i]

    def tiny_of(i):
        return PIECE_OF[(0, 2, 1, 3)[i // 4] * 4 + i % 4]

    def tiny_row(i, row):
        a, k = tiny_of(i)
        return tiny[a][k, row : row + 1, :].astype(F32)

    for i in range(16):
        a, k = tiny_of(i)
        gb_ref[:, pl.ds(lane(0, i), 128)] = tiny[a][k].astype(F32)[0:8]
    bias = jnp.concatenate([tiny_row(0, 4 + i) for i in range(7)], axis=1)

    for half in range(2):
        pieces = halves[half]

        def chunk(t, _, half=half, pieces=pieces):
            here = pl.ds(pl.multiple_of(t * 16, 16), 16)
            rows = pl.ds(pl.multiple_of(half * HALF + t * 16, 16), 16)
            xs = [pieces[a][k, here, :].astype(F32) for a, k in PIECE_OF]
            total = xs[0]
            square = xs[0] * xs[0]
            for x in xs[1:]:
                total = total + x
                square = square + x * x
            mean = jnp.sum(total, axis=1, keepdims=True) * (1.0 / D)
            square = jnp.sum(square, axis=1, keepdims=True) * (1.0 / D)
            inv = lax.rsqrt(square - mean * mean + EPS)
            for i, x in enumerate(xs):
                j = i if half == 0 else (i % 4) * 4 + i // 4
                centered = (x - mean) * inv
                if i == 0:
                    cen_ref[rows, :] = centered
                normed_ref[rows, pl.ds(lane(half, i), 128)] = (centered * tiny_row(j, 0) + tiny_row(j, 1)).astype(BF16)
            inv_ref[rows, :] = jnp.broadcast_to(inv, (16, 128))
            return _

        lax.fori_loop(0, HALF // 16, chunk, 0, unroll=4)

    @pl.loop(0, TOK // BLK)
    def _(t):
        rows = pl.ds(pl.multiple_of(t * BLK, BLK), BLK)
        mixed = bias
        for first, n, ref in weight_blocks(wts):
            lines = slice(first * BLK, (first + n) * BLK)
            mixed = mixed + dot(normed_ref[rows, lines], ref[...].reshape(n * BLK, CAT), NN)
        for s in range(2):
            v = mixed[:, s * 128 : (s + 1) * 128]
            v = v * cos_ref[rows, :] + pltpu.roll(v, 128 - 16, 1) * sa_ref[rows, :] + pltpu.roll(v, 16, 1) * sb_ref[rows, :]
            qkv_ref[rows, s * 128 : (s + 1) * 128] = v.astype(BF16)
        qkv_ref[rows, 256:384] = mixed[:, 256:384].astype(BF16)
        pre = mixed[:, QKV:CAT]
        pre_ref[rows, :] = pre
        act_ref[rows, :] = (0.5 * pre * (1.0 + gelu_tanh_part(pre))).astype(BF16)


def norm_call(xa, xb, tiny, wts, cos, sa, sb):
    outs = [
        shape((TOK, D), BF16),
        shape((TOK, QKV), BF16),
        shape((TOK, FFL), F32),
        shape((TOK, FFL), BF16),
        shape((TOK, 128), F32),
        shape((TOK, 128), F32),
        shape((8, D), F32),
    ]
    args = (*xa, *xb, *tiny, *wts, cos, sa, sb)
    return call("norm_proj", norm_kernel, [vmem()] * 11, outs, args)


def head_masks():
    lane = lax.broadcasted_iota(jnp.int32, (1, 128), 1)
    return [(lane < HEAD_DIM).astype(BF16), (lane >= HEAD_DIM).astype(BF16)]


def masked_scores(qh, k, qi):
    s = dot(qh, k, NT)
    row = lax.broadcasted_iota(jnp.int32, (BLK, BLK), 0)
    column = lax.broadcasted_iota(jnp.int32, (BLK, BLK), 1)
    last = jnp.where(row >= column, s[:, qi * BLK :], -1e30)
    return last if qi == 0 else jnp.concatenate([s[:, : qi * BLK], last], axis=1)


def for_blocks(lengths, body):
    long_first = lengths[0, 0] > lengths[0, 1]
    long_start, short_start = jnp.where(long_first, 0, 256), jnp.where(long_first, 768, 0)

    @pl.loop(0, 2)
    def _(document):
        body(jnp.where(document == 0, long_start, short_start), 0)

    for qi in (1, 2):
        body(long_start, qi)


def attend_kernel(tab, qkv_ref, out_ref):
    masks = head_masks()

    def body(start, qi):
        rows = pl.ds(pl.multiple_of(start + qi * BLK, BLK), BLK)
        keys = pl.ds(pl.multiple_of(start, BLK), (qi + 1) * BLK)
        q = qkv_ref[rows, 0:128] * jnp.asarray(0.125, BF16)
        k = qkv_ref[keys, 128:256]
        v = qkv_ref[keys, 256:384]
        total = None
        for m in masks:
            s = masked_scores(q * m, k, qi)
            e = jnp.exp(s - jnp.max(s, axis=1, keepdims=True))
            p = (e * (1.0 / jnp.sum(e, axis=1, keepdims=True))).astype(BF16)
            o = dot(p, v * m, NN)
            total = o if total is None else total + o
        out_ref[rows, :] = total.astype(BF16)

    for_blocks(tab, body)


def attend_call(tab, qkv):
    outs = [shape((TOK, 128), BF16)]
    return call("attend", attend_kernel, [smem(), vmem()], outs, (tab, qkv))[0]


def attend_back_kernel(tab, qkv_ref, do_ref, cos_ref, sa_ref, sb_ref, out_ref, sum_ref, dq, dk, dv):
    masks = head_masks()
    dk[...] = jnp.zeros_like(dk)
    dv[...] = jnp.zeros_like(dv)

    def body(start, qi):
        rows = pl.ds(pl.multiple_of(start + qi * BLK, BLK), BLK)
        keys = pl.ds(pl.multiple_of(start, BLK), (qi + 1) * BLK)
        q = qkv_ref[rows, 0:128]
        k = qkv_ref[keys, 128:256]
        v = qkv_ref[keys, 256:384]
        do = do_ref[rows, :]
        total = None
        for m in masks:
            qh = q * m
            doh = do * m
            s = masked_scores(qh * jnp.asarray(0.125, BF16), k, qi)
            e = jnp.exp(s - jnp.max(s, axis=1, keepdims=True))
            p = e * (1.0 / jnp.sum(e, axis=1, keepdims=True))
            dp = dot(doh, v, NT)
            delta = jnp.sum(p * dp, axis=1, keepdims=True)
            ds = (p * (dp - delta) * 0.125).astype(BF16)
            part = dot(ds, k * m, NN)
            total = part if total is None else total + part
            dk[keys, :] += dot(ds, qh, TN)
            dv[keys, :] += dot(p.astype(BF16), doh, TN)
        dq[rows, :] = total

    for_blocks(tab, body)
    for s, ref in enumerate((dq, dk, dv)):
        d = ref[...]
        if s < 2:
            d = d * cos_ref[...] - pltpu.roll(d, 128 - 16, 1) * sa_ref[...] - pltpu.roll(d, 16, 1) * sb_ref[...]
        low = d.astype(BF16)
        out_ref[:, s * 128 : (s + 1) * 128] = low
        sum_ref[:, s * 128 : (s + 1) * 128] = jnp.broadcast_to(jnp.sum(low.astype(F32), axis=0, keepdims=True), (8, 128))


def attend_back_call(tab, qkv, do, cos, sa, sb):
    outs = [shape((TOK, QKV), BF16), shape((8, QKV), F32)]
    scratch = [pltpu.VMEM((TOK, 128), F32)] * 3
    args = (tab, qkv, do, cos, sa, sb)
    return call("attend_back", attend_back_kernel, [smem()] + [vmem()] * 5, outs, args, scratch)


def project_kernel(att_ref, act_ref, *refs):
    wts, outs, whole = refs[0:2], refs[2:6], refs[6]
    place = Place()
    for half in range(2):
        spots = [[place.spot(half, j, i) for i in range(2)] for j in range(8)]

        @pl.loop(0, HALF // BLK)
        def _(t, half=half, spots=spots):
            rows = pl.ds(pl.multiple_of(half * HALF + t * BLK, BLK), BLK)
            here = pl.ds(pl.multiple_of(t * BLK, BLK), BLK)
            both = jnp.concatenate([att_ref[rows, :], act_ref[rows, :]], axis=1)
            for j in range(8):
                part = dot(both, weight_of(wts, j)[...], NT).astype(BF16)
                for i in range(2):
                    whole[spots[j][i], here, :] = part[:, i * 128 : (i + 1) * 128]

        outs[2 * half][...] = whole[0:8]
        outs[2 * half + 1][...] = whole[8:16]


def project_call(att, act, wts):
    outs = [shape((8, HALF, 128), BF16)] * 4
    scratch = [pltpu.VMEM((16, HALF, 128), BF16)]
    return call("project", project_kernel, [vmem()] * 4, outs, (att, act, *wts), scratch)


def upstream_kernel(*refs):
    place = Place()
    halves, wts, pre_ref = (refs[0:2], refs[2:4]), refs[4:6], refs[6]
    g_ref, hid_ref, att_ref, hsum_ref, gsum_ref = refs[7:12]
    mine = jnp.zeros((1, 128), F32)
    for half in range(2):
        for i, (a, k) in enumerate(PIECE_OF):
            g_ref[half * HALF : (half + 1) * HALF, pl.ds(place.lane(half, i), 128)] = halves[half][a][k]
        mine = mine + jnp.sum(halves[half][0][0].astype(F32), axis=0, keepdims=True)
    gsum_ref[...] = jnp.broadcast_to(mine, (8, 128))
    hsum_ref[...] = jnp.zeros_like(hsum_ref)

    @pl.loop(0, TOK // BLK)
    def _(t):
        rows = pl.ds(pl.multiple_of(t * BLK, BLK), BLK)
        d_act = None
        for first, n, ref in weight_blocks(wts):
            lines = slice(first * BLK, (first + n) * BLK)
            part = dot(g_ref[rows, lines], ref[...].reshape(n * BLK, ACT), NN)
            d_act = part if d_act is None else d_act + part
        att_ref[rows, :] = d_act[:, 0:128].astype(BF16)
        v = pre_ref[rows, :]
        th = gelu_tanh_part(v)
        slope = 0.5 * (1.0 + th) + 0.5 * v * (1.0 - th * th) * (0.7978845608028654 * (1.0 + 3.0 * 0.044715 * v * v))
        low = (d_act[:, 128:ACT] * slope).astype(BF16)
        hid_ref[rows, :] = low
        hsum_ref[...] += jnp.broadcast_to(jnp.sum(low.astype(F32), axis=0, keepdims=True), (8, FFL))


def upstream_call(ga, gb, wts, pre, after):
    outs = [
        shape((TOK, D), BF16),
        shape((TOK, FFL), BF16),
        shape((TOK, 128), BF16),
        shape((8, FFL), F32),
        shape((8, 128), F32),
    ]
    args = (*ga, *gb, *wts, pre)
    return call("upstream", upstream_kernel, [vmem()] * 7, outs, args, after=after)


def downstream_kernel(dm_ref, dh_ref, normed_ref, gb_ref, *refs):
    wts, outs, whole, flat = refs[0:2], refs[2:6], refs[6], refs[7]
    place = Place()
    flat[...] = jnp.zeros_like(flat)
    for half in range(2):
        spots = [[place.spot(half, j, i) for i in range(2)] for j in range(8)]

        @pl.loop(0, HALF // BLK)
        def _(b, half=half, spots=spots):
            rows = pl.ds(pl.multiple_of(half * HALF + b * BLK, BLK), BLK)
            here = pl.ds(pl.multiple_of(b * BLK, BLK), BLK)
            both = jnp.concatenate([dm_ref[rows, :], dh_ref[rows, :]], axis=1)
            s1 = jnp.zeros((BLK, 128), F32)
            s2 = jnp.zeros((BLK, 128), F32)
            for j in range(8):
                lines = slice(j * BLK, (j + 1) * BLK)
                part = dot(both, weight_of(wts, j)[...], NT)
                low = part.astype(BF16)
                u1 = part * gb_ref[0:1, lines]
                u2 = part * (normed_ref[rows, lines].astype(F32) - gb_ref[1:2, lines])
                for i in range(2):
                    cut = slice(i * 128, (i + 1) * 128)
                    whole[spots[j][i], here, :] = low[:, cut]
                    s1 = s1 + u1[:, cut]
                    s2 = s2 + u2[:, cut]
            for i in range(BLK // 128):
                cut = slice(i * 128, (i + 1) * 128)
                at = b * (BLK // 64) + 2 * i
                flat[pl.ds(at, 1), :] = jnp.sum(jnp.transpose(s1[cut, :]), axis=0, keepdims=True)
                flat[pl.ds(at + 1, 1), :] = jnp.sum(jnp.transpose(s2[cut, :]), axis=0, keepdims=True)

        low = flat[...].astype(BF16)
        for n, out in enumerate(outs[2 * half : 2 * half + 2]):
            out[:, 0:HALF, :] = whole[8 * n : 8 * n + 8]
            for c in range(8):
                out[c, HALF : HALF + PAD, :] = low


def downstream_call(dm, dh, normed, gb, wts, after):
    outs = [shape((8, HALF + PAD, 128), BF16)] * 4
    scratch = [pltpu.VMEM((16, HALF, 128), BF16), pltpu.VMEM((PAD, 128), F32)]
    args = (dm, dh, normed, gb, *wts)
    return call("downstream", downstream_kernel, [vmem()] * 6, outs, args, scratch, after)


def grad_lanes(p):
    place = lax.rem(p, 4)
    j = p + jnp.where(place == 1, 1, 0) - jnp.where(place == 2, 1, 0)
    return pl.ds(pl.multiple_of(j * BLK, BLK), BLK)


TILE = BLK + PAD
TILE_TWO = ACT + PAD
GRAD_ROWS = 7 * TILE + 2 * TILE_TWO


def grads_kernel(normed_ref, dm_ref, dh_ref, msum_ref, hsum_ref, att_ref, act_ref, g_ref, gsum_ref, keep, send, turned):
    turned[0:128, :] = jnp.transpose(att_ref[...])
    turned[128:ACT, :] = jnp.transpose(act_ref[...])
    zero = jnp.zeros((8, 128), F32)
    for first, out_ref in ((4, send), (0, keep)):

        @pl.loop(0, 4)
        def _(p, first=first, out_ref=out_ref):
            lanes = grad_lanes(first + p)
            block = normed_ref[:, lanes]
            t = 0
            for ref, sums_ref, n in ((dm_ref, msum_ref, 3), (dh_ref, hsum_ref, 4)):
                part = dot(block, ref[...], TN).astype(BF16)
                for i in range(n):
                    cut = slice(i * 128, (i + 1) * 128)
                    out_ref[p, t * TILE : t * TILE + BLK, :] = part[:, cut]
                    sums = jnp.concatenate([sums_ref[:, cut], zero], axis=0).astype(BF16)
                    out_ref[p, t * TILE + BLK : (t + 1) * TILE, :] = sums
                    t += 1
            part = dot(turned[...], g_ref[:, lanes], NN).astype(BF16)
            sums = jnp.concatenate([gsum_ref[...], zero], axis=0).astype(BF16)
            for i in range(2):
                at = 7 * TILE + i * TILE_TWO
                out_ref[p, at : at + ACT, :] = part[:, i * 128 : (i + 1) * 128]
                out_ref[p, at + ACT : at + TILE_TWO, :] = sums


def grads_call(*args, after):
    scratch = [pltpu.VMEM((ACT, TOK), BF16)]
    return call("grads", grads_kernel, [vmem()] * 9, [shape((4, GRAD_ROWS, 128), BF16)] * 2, args, scratch, after)


def fold_part(blocks, out_ref, back_ref, got, keep_out, keep_back, send):
    half = blocks // 2
    for i in range(blocks):
        for back, (ref, rows, keep) in enumerate(((out_ref, HALF, keep_out), (back_ref, HALF + PAD, keep_back))):
            if len(got) == 2:
                new = got[back][i]
            else:
                base = back * blocks * HALF + i * rows
                new = got[0][base : base + rows, :]
            total = ref[i].astype(F32) + new.astype(F32)
            if i < half:
                keep[i] = total
            else:
                at = back * half * HALF + (i - half) * rows
                send[at : at + rows, :] = total.astype(BF16)


def fold_call(blocks, a, b, *extra, after=()):
    half, n = blocks // 2, len(a)

    def kernel(*refs):
        ins, outs = refs[: 2 * n], refs[2 * n + len(extra) :]
        for h in range(2):
            mine = ins[h * n : (h + 1) * n]
            fold_part(blocks, mine[0], mine[1], mine[2:], *outs[3 * h : 3 * h + 3])
        for ref, out in zip(refs[2 * n :], outs[6:]):
            out[...] = ref[...]

    outs = [
        shape((half, HALF, 128), F32),
        shape((half, HALF + PAD, 128), F32),
        shape((half * (2 * HALF + PAD), 128), BF16),
    ] * 2 + [shape(e.shape, e.dtype) for e in extra]
    got = call("fold", kernel, [vmem()] * (2 * n + len(extra)), outs, (*a, *b, *extra), after=after)
    return got[0:3], got[3:6], got[6:]


def finish_kernel(oa, ba, ga, ob, bb, gb, x_ref, g_ref, cen_ref, inv_ref, small_ref, out_ref, grad_ref, sum_ref):
    gain = small_ref[0:1, :].astype(F32)
    shift = small_ref[2:3, :].astype(F32) + small_ref[3:4, :].astype(F32)
    total_gain = jnp.zeros((1, 128), F32)
    total_shift = jnp.zeros((1, 128), F32)
    for half, (o_ref, b_ref, got) in enumerate(((oa, ba, ga), (ob, bb, gb))):
        sums = b_ref[0, HALF : HALF + PAD, :] + got[2 * HALF : 2 * HALF + PAD, :].astype(F32)
        sums = jnp.transpose(sums) * (1.0 / D)
        for i in range(HALF // 128):
            here = slice(i * 128, (i + 1) * 128)
            there = slice(HALF + i * 128, HALF + (i + 1) * 128)
            rows = slice(half * HALF + i * 128, half * HALF + (i + 1) * 128)
            branch = o_ref[0, here, :] + got[here, :].astype(F32)
            out_ref[rows, :] = (x_ref[rows, :].astype(F32) + branch + shift).astype(BF16)
            d = b_ref[0, here, :] + got[there, :].astype(F32)
            cen = cen_ref[rows, :]
            total_gain = total_gain + jnp.sum(d * cen, axis=0, keepdims=True)
            total_shift = total_shift + jnp.sum(d, axis=0, keepdims=True)
            m1 = sums[:, 2 * i : 2 * i + 1]
            m2 = sums[:, 2 * i + 1 : 2 * i + 2]
            grad_ref[rows, :] = g_ref[rows, :].astype(F32) + inv_ref[rows, :] * (d * gain - m1 - cen * m2)
    sum_ref[...] = jnp.concatenate([total_gain, total_shift, jnp.zeros((6, 128), F32)], axis=0)


def finish_call(*args):
    outs = [shape((TOK, 128), BF16), shape((TOK, 128), F32), shape((8, 128), F32)]
    return call("finish", finish_kernel, [vmem()] * 11, outs, args, final=True)


def fold_row_call(kept, *got, parts=1, after=()):
    n = got[0].shape[0] // 2
    cut = GRAD_ROWS // parts

    def kernel(kept_ref, *refs):
        ins, keep_ref, sends = refs[: len(got)], refs[len(got)], refs[len(got) + 1 :]
        step = GRAD_ROWS // len(got)
        for i in range(n):
            for m, ref in enumerate(ins):
                rows = slice(m * step, (m + 1) * step)
                keep_ref[i, rows, :] = kept_ref[i, rows, :].astype(F32) + ref[i].astype(F32)
            for m, send in enumerate(sends):
                rows = slice(m * cut, (m + 1) * cut)
                if len(got) == 1:
                    new = ins[0][n + i, rows, :].astype(F32)
                else:
                    new = jnp.concatenate([ref[n + i].astype(F32) for ref in ins], axis=0)
                send[i] = (kept_ref[n + i, rows, :].astype(F32) + new).astype(BF16)

    outs = [shape((n, GRAD_ROWS, 128), F32)] + [shape((n, cut, 128), BF16)] * parts
    return call("fold_row", kernel, [vmem()] * (1 + len(got)), outs, (kept, *got), after=after)


def lanes_of(v, row, width):
    total = 8 * width
    return pltpu.roll(v, lax.rem(total - row * width, total), 1)[:, 0:width]


def close_kernel(kept_ref, got_ref, qkv_ref, qb_ref, up_ref, ub_ref, out_ref, down_ref, bias_ref, again_ref):
    total = lambda first, n: kept_ref[0, first : first + n, :] + got_ref[0, first : first + n, :].astype(F32)
    row = lax.axis_index("row")
    for s in range(3):
        qkv_ref[s] = total(s * TILE, BLK)
        qb_ref[s : s + 1, :] = lanes_of(total(s * TILE + BLK, PAD)[0:8], row, 16)[0:1]
    for i in range(4):
        up_ref[:, i * 128 : (i + 1) * 128] = total((3 + i) * TILE, BLK)
    bias = jnp.concatenate([total((3 + i) * TILE + BLK, PAD)[0:8] for i in range(4)], axis=1)
    ub_ref[...] = lanes_of(bias, row, 64)[0:1]
    for i in range(2):
        at = 7 * TILE + i * TILE_TWO
        out_ref[:, i * 128 : (i + 1) * 128] = total(at, 128)
        down_ref[:, i * 128 : (i + 1) * 128] = total(at + 128, FFL)
    bias = lanes_of(total(7 * TILE + ACT, PAD)[0:8], row, 16)[0:1]
    bias_ref[...] = bias
    again_ref[...] = bias


def close_call(kept, got):
    outs = [
        shape((3, BLK, 128), F32),
        shape((3, 16), F32),
        shape((BLK, FFL), F32),
        shape((1, 64), F32),
        shape((128, BLK), F32),
        shape((FFL, BLK), F32),
        shape((1, 16), F32),
        shape((1, 16), F32),
    ]
    return call("close", close_kernel, [vmem()] * 2, outs, (kept, got), final=True)


def close_norm_kernel(*refs):
    total = refs[0][...]
    for ref in refs[1:4]:
        total = total + ref[...]
    mine = lanes_of(total, lax.axis_index("row"), 16)
    refs[4][...] = mine[0:1]
    refs[5][...] = mine[1:2]


def close_norm_call(*args):
    return call("close_norm", close_norm_kernel, [vmem()] * 4, [shape((1, 16), F32)] * 2, args, final=True)


def join(*groups, after=()):
    groups = [[p if isinstance(p, tuple) else (p, 0, p.shape[0]) for p in group] for group in groups]
    flat = [p for group in groups for p in group]

    def kernel(*refs):
        ins, outs = refs[: len(flat)], refs[len(flat) :]
        n = 0
        for group, out in zip(groups, outs):
            at = 0
            for _, lo, hi in group:
                out[at : at + hi - lo] = ins[n][lo:hi]
                at += hi - lo
                n += 1

    outs = []
    for group in groups:
        first = group[0][0]
        outs.append(shape((sum(hi - lo for _, lo, hi in group),) + first.shape[1:], first.dtype))
    return call("join", kernel, [vmem()] * len(flat), outs, [p[0] for p in flat], after=after)


def fetch(copies):
    for copy in copies:
        copy.start()
    for copy in copies:
        copy.wait()


def in_hbm(*arrays):
    return [pltpu.with_memory_space_constraint(a, pltpu.HBM) for a in arrays]


def begin_kernel(x_ref, g_ref, a_ref, b_ref, sem):
    copies = []
    for half, out in enumerate((a_ref, b_ref)):
        for i, ref in enumerate((x_ref, g_ref)):
            copies.append(pltpu.make_async_copy(ref.at[pl.ds(half * HALF, HALF)], out.at[i], sem.at[half * 2 + i]))
    fetch(copies)


def begin_call(*args, after):
    scratch = [pltpu.SemaphoreType.DMA((4,))]
    specs = [pl.BlockSpec(memory_space=pltpu.HBM)] * 2
    return call("begin", begin_kernel, specs, [shape((2, HALF, 128), BF16)] * 2, in_hbm(*args), scratch, after)


def pack_kernel(qkv_ref, up_ref, out_ref, down_ref, cats, twos, out_here, down_here, sem):
    copies = [
        pltpu.make_async_copy(qkv_ref.at[s], cats.at[0, :, pl.ds(s * 128, 128)], sem.at[s]) for s in range(3)
    ]
    copies.append(pltpu.make_async_copy(up_ref, cats.at[0, :, pl.ds(QKV, FFL)], sem.at[3]))
    copies.append(pltpu.make_async_copy(out_ref, out_here, sem.at[4]))
    copies.append(pltpu.make_async_copy(down_ref, down_here, sem.at[5]))
    fetch(copies)
    twos[0, :, 0:128] = jnp.transpose(out_here[...])
    twos[0, :, 128:ACT] = jnp.transpose(down_here[...])


def pack_call(*args, after):
    outs = [shape((1, BLK, CAT), BF16), shape((1, BLK, ACT), BF16)]
    scratch = [pltpu.VMEM((128, BLK), BF16), pltpu.VMEM((FFL, BLK), BF16), pltpu.SemaphoreType.DMA((6,))]
    specs = [pl.BlockSpec(memory_space=pltpu.HBM)] * 4
    return call("pack", pack_kernel, specs, outs, in_hbm(*args), scratch, after)


def both(mine, got):
    n = mine.shape[0] // 2
    return [(mine, 0, n), (got, 0, n), (mine, n, 2 * n), (got, n, 2 * n)]


def rotary_tables(long_start):
    places = jnp.arange(TOK, dtype=jnp.int32)
    begin_second = jnp.where(long_start == 0, 768, 256)
    positions = jnp.where(places >= begin_second, places - begin_second, places)
    lane = jnp.arange(128, dtype=jnp.int32)
    spot = lane % HEAD_DIM
    half = ROT // 2
    inverse = 10000.0 ** (-2.0 * (spot % half).astype(F32) / ROT)
    angles = positions.astype(F32)[:, None] * inverse[None, :]
    turned = (spot < ROT)[None, :]
    cos = jnp.where(turned, jnp.cos(angles), 1.0)
    sine = jnp.sin(angles)
    low = jnp.where((spot < half)[None, :], -sine, 0.0)
    high = jnp.where(((spot >= half) & (spot < ROT))[None, :], sine, 0.0)
    return cos, low, high


def shards(x, lengths, w_qkv, b_qkv, w_out, b_out, w_up, b_up, w_down, b_down, gain, shift, g):
    row = lax.axis_index("row")
    cos, sa, sb = rotary_tables(jnp.where(lengths[0, 0] > lengths[0, 1], 0, 256))

    def spread(v, width):
        wide = jnp.zeros(v.shape[:-1] + (8, width), BF16)
        return lax.dynamic_update_slice_in_dim(wide, v[..., None, :], row, v.ndim - 1).reshape(-1, 128)

    small = [spread(jnp.stack([gain, shift, b_out, b_down]), 16), spread(b_qkv, 16), spread(b_up, 64)]
    small = jnp.concatenate(small + [jnp.zeros((PAD - 11, 128), BF16)])
    a, b = begin_call(x, g, after=(small,))
    a_got, b_got = exchange(a, "x", 0), exchange(b, "y", 0)
    small = small + exchange(small, "c")
    cats, twos = pack_call(w_qkv.transpose(1, 0, 2), w_up, w_out, w_down, after=(small,))
    small = small + exchange(small, "z", 0)
    small, cats, twos, a, b = join([small], [cats], [twos], both(a, a_got), both(b, b_got))
    a_got, b_got = exchange(a, "x", 1), exchange(b, "y", 1)
    cats_got, twos_got = exchange(cats, "z", 0), exchange(twos, "z", 0)
    small = small + exchange(small, "z", 1)
    tiny = small[None]
    tiny_got = exchange(tiny, "x", 0)
    tiny, cats, a, b = join([tiny, tiny_got], [cats, cats_got], both(a, a_got), both(b, b_got), after=(twos_got,))
    tiny_got = exchange(tiny, "x", 1)
    a_got, b_got = exchange(a, "y", 0), exchange(b, "x", 0)
    cats_got = exchange(cats, "z", 1)
    (tiny,) = join([tiny, tiny_got])
    tiny_got = exchange(tiny, "y", 1)
    first = lambda v, got: [(v, 0, 4), (got, 0, 4)]
    last = lambda v, got: [(v, 4, 8), (got, 4, 8)]
    tiny, xa, xb, cats, twos, ga, gb = join(
        [tiny, tiny_got],
        first(a, a_got),
        first(b, b_got),
        [cats, cats_got],
        [twos, twos_got],
        last(a, a_got),
        last(b, b_got),
    )
    tiny = (tiny, exchange(tiny, "y", 0))
    xa, xb = (xa, exchange(xa, "y", 1)), (xb, exchange(xb, "x", 1))
    cats = (cats, exchange(cats, "c"))
    twos_got = exchange(twos, "z", 1)
    ga, gb = (ga, exchange(ga, "y", 1)), (gb, exchange(gb, "x", 1))
    (twos,) = join([twos, twos_got])
    twos = (twos, exchange(twos, "c"))

    normed, qkv, pre, act, centered, inv, gains = norm_call(xa, xb, tiny, cats, cos, sa, sb)
    att = attend_call(lengths, qkv)
    out_a, send_a, out_b, send_b = project_call(att, act, twos)
    out_a_got, out_b_got = exchange(send_a, "y", 0), exchange(send_b, "x", 0)
    g_all, d_hid, d_att, hsum, gsum = upstream_call(ga, gb, twos, pre, (out_a,))
    d_mix, msum = attend_back_call(lengths, qkv, d_att, cos, sa, sb)
    back_a, send_a, back_b, send_b = downstream_call(d_mix, d_hid, normed, gains, cats, (out_a_got, out_b_got))
    back_a_got, back_b_got = exchange(send_a, "y", 0), exchange(send_b, "x", 0)
    keep, send = grads_call(normed, d_mix, d_hid, msum, hsum, att, act, g_all, gsum, after=(back_a,))
    a, b, (send,) = fold_call(8, (out_a, back_a, out_a_got, back_a_got), (out_b, back_b, out_b_got, back_b_got), send)
    a_got, b_got = exchange(a[2], "y", 1), exchange(b[2], "x", 1)
    keep, *sends = fold_row_call(keep, exchange(send, "c"), parts=3)
    got = [exchange(send, "z", 0) for send in sends]
    a, b, _ = fold_call(4, (a[0], a[1], a_got), (b[0], b[1], b_got), after=(got[0],))
    a_got, b_got = exchange(a[2], "x", 0), exchange(b[2], "y", 0)
    a, b, _ = fold_call(2, (a[0], a[1], a_got), (b[0], b[1], b_got), after=(got[1],))
    a_got, b_got = exchange(a[2], "x", 1), exchange(b[2], "y", 1)
    keep, send = fold_row_call(keep, *got, after=(a[0],))
    got = exchange(send, "z", 1)
    block_out, input_grad, sums = finish_call(a[0], a[1], a_got, b[0], b[1], b_got, x, g, centered, inv, small)
    sums = sums + exchange(sums, "c")
    gain_grad, shift_grad = close_norm_call(sums, *(exchange(sums, "z", n) for n in range(3)))
    qkv_grad, qkv_bias, up_grad, up_bias, out_grad, down_grad, out_bias, down_bias = close_call(keep, got)
    return (
        block_out,
        input_grad,
        qkv_grad.transpose(1, 0, 2),
        qkv_bias,
        out_grad,
        out_bias.reshape(16),
        up_grad,
        up_bias.reshape(64),
        down_grad,
        down_bias.reshape(16),
        gain_grad.reshape(16),
        shift_grad.reshape(16),
    )


def solution(mesh):
    both = P(("col", "row"))
    in_specs = (
        P("row", "col"),
        P("row", None),
        P("row", None, "col"),
        P(None, ("col", "row")),
        P("col", "row"),
        both,
        P("row", "col"),
        both,
        P("col", "row"),
        both,
        both,
        both,
        P("row", "col"),
    )
    out_specs = (
        P("row", "col"),
        P("row", "col"),
        P("row", None, "col"),
        P(None, ("col", "row")),
        P("col", "row"),
        both,
        P("row", "col"),
        both,
        P("col", "row"),
        both,
        both,
        both,
    )
    return jax.shard_map(shards, mesh=mesh, in_specs=in_specs, out_specs=out_specs, check_vma=False)
```

```python
import functools

import jax
import jax.numpy as jnp
from jax import lax
from jax.experimental import pallas as pl
from jax.experimental.pallas import tpu as pltpu
from jax.sharding import PartitionSpec as P

D = 2048
HEAD_DIM = 64
ROT = 32
EPS = 1e-05
TOK = 1024
HALF = 512
QKV = 384
FFL = 512
CAT = QKV + FFL
ACT = 128 + FFL
ALL = CAT + ACT
PAD = 16
BLK = 256
F32 = jnp.float32
BF16 = jnp.bfloat16
MIB = 2**20

MASKS = ((1, 3, 2), (3, 1, 2))


def exchange(value, axis, step=0):
    pairs = []
    for z in range(4):
        for k in range(2):
            m = MASKS[k][step]
            for y in range(4):
                for x in range(4):
                    to = {
                        "x": (x ^ m, y, z, k),
                        "y": (x, y ^ m, z, k),
                        "z": (x, y, z ^ m, k),
                        "c": (x, y, z, 1 - k),
                    }[axis]
                    pairs.append(((z * 2 + k) * 16 + y * 4 + x, (to[2] * 2 + to[3]) * 16 + to[1] * 4 + to[0]))
    return lax.ppermute(value, ("row", "col"), pairs)


PIECE_OF = [(i // 8, i % 8) for i in range(16)]
NN = ((1,), (0,))
NT = ((1,), (1,))
TN = ((0,), (0,))


def dot(a, b, dims):
    return lax.dot_general(a, b, (dims, ((), ())), preferred_element_type=F32)


def weight_blocks(refs):
    first = 0
    for ref in refs:
        yield first, ref.shape[0], ref
        first += ref.shape[0]


def weight_of(refs, j):
    for first, n, ref in weight_blocks(refs):
        if first <= j < first + n:
            return ref.at[j - first]


def gelu_tanh_part(v):
    return jnp.tanh(0.7978845608028654 * (v + 0.044715 * v * v * v))


class Place:
    def __init__(self):
        row, col = lax.axis_index("row"), lax.axis_index("col")
        self.row = row
        self.z, self.core, self.y, self.x = lax.div(row, 2), lax.rem(row, 2), lax.div(col, 4), lax.rem(col, 4)
        self.m1 = jnp.where(self.core == 0, 1, 3)
        self.m2 = 4 - self.m1
        self.seen = (0, self.m1, self.m2, 2)

    def swapped(self, mask):
        return jnp.where(mask == self.m2, 1, jnp.where(mask == self.m1, 2, jnp.where(mask == 2, 3, 0)))

    def lane(self, half, i):
        outer, inner = self.seen[i // 4], self.seen[i % 4]
        y, x = (self.y ^ outer, self.x ^ inner) if half == 0 else (self.y ^ inner, self.x ^ outer)
        owner = y * 2 + lax.div(x, 2)
        mask = lax.div(owner, 2) ^ self.z
        same = lax.rem(owner, 2) == self.core
        first = jnp.where(mask == self.m1, 1, jnp.where(mask == self.m2, 2, jnp.where(mask == 2, 3, 0)))
        block = jnp.where(same, first, 4 + self.swapped(mask))
        return pl.multiple_of((block * 2 + lax.rem(x, 2)) * 128, 128)

    def spot(self, half, j, i):
        if j < 4:
            z, core = self.z ^ self.seen[j], self.core
        else:
            z, core = self.z ^ (0, self.m2, self.m1, 2)[j - 4], 1 - self.core
        owner = (z * 2 + core) * 2 + i
        y, x = self.swapped(lax.div(owner, 4) ^ self.y), self.swapped(lax.rem(owner, 4) ^ self.x)
        return y * 4 + x if half == 0 else x * 4 + y


def vmem():
    return pl.BlockSpec(memory_space=pltpu.VMEM)


def smem():
    return pl.BlockSpec(memory_space=pltpu.SMEM)


def any_spec():
    return pl.BlockSpec(memory_space=pl.ANY)


def shape(dims, dtype):
    return jax.ShapeDtypeStruct(dims, dtype)


WORK = dict(norm_proj=9, attend=3, project=5, upstream=6, attend_back=7, downstream=6, grads=11)
VMEM_MIB = dict(norm_proj=7, attend=8, project=7, upstream=7, attend_back=11, downstream=8, grads=8)


def call(name, kernel, specs, outs, args, scratch=(), after=(), final=False):
    if after:
        body, n = kernel, len(args)
        kernel = lambda *refs: body(*refs[:n], *refs[n + len(after) :])
        specs = list(specs) + [any_spec()] * len(after)
    return pl.pallas_call(
        kernel,
        in_specs=specs,
        out_specs=[vmem()] * len(outs),
        out_shape=outs if final else [pltpu.VMEM(o.shape, o.dtype) for o in outs],
        scratch_shapes=list(scratch),
        compiler_params=pltpu.CompilerParams(vmem_limit_bytes=VMEM_MIB.get(name, 3) * MIB),
        cost_estimate=pl.CostEstimate(flops=int(WORK.get(name, 0) * 2.5e8), bytes_accessed=0, transcendentals=0),
        name=name,
    )(*args, *after)


def norm_kernel(*refs):
    place = Place()
    halves, tiny, wts = (refs[0:2], refs[2:4]), refs[4:6], refs[6:10]
    cos_ref, sa_ref, sb_ref = refs[10:13]
    normed_ref, qkv_ref, pre_ref, act_ref, cen_ref, inv_ref, gb_ref = refs[13:]

    lanes = [[place.lane(half, i) for i in range(16)] for half in range(2)]

    def lane(half, i):
        return lanes[half][i]

    def tiny_of(i):
        return PIECE_OF[(0, 8, 2, 10)[i // 4] + (0, 4, 1, 5)[i % 4]]

    def tiny_row(i, row):
        a, k = tiny_of(i)
        return tiny[a][k, row : row + 1, :].astype(F32)

    for i in range(16):
        a, k = tiny_of(i)
        gb_ref[:, pl.ds(lane(0, i), 128)] = tiny[a][k].astype(F32)[0:8]
    bias = jnp.concatenate([tiny_row(0, 4 + i) for i in range(7)], axis=1)

    for half in range(2):
        pieces = halves[half]

        def chunk(t, _, half=half, pieces=pieces):
            here = pl.ds(pl.multiple_of(t * 16, 16), 16)
            rows = pl.ds(pl.multiple_of(half * HALF + t * 16, 16), 16)
            xs = [pieces[a][k, here, :].astype(F32) for a, k in PIECE_OF]
            total = xs[0]
            square = xs[0] * xs[0]
            for x in xs[1:]:
                total = total + x
                square = square + x * x
            mean = jnp.sum(total, axis=1, keepdims=True) * (1.0 / D)
            square = jnp.sum(square, axis=1, keepdims=True) * (1.0 / D)
            inv = lax.rsqrt(square - mean * mean + EPS)
            for i, x in enumerate(xs):
                j = i if half == 0 else (i % 4) * 4 + i // 4
                centered = (x - mean) * inv
                if i == 0:
                    cen_ref[rows, :] = centered
                normed_ref[rows, pl.ds(lane(half, i), 128)] = (centered * tiny_row(j, 0) + tiny_row(j, 1)).astype(BF16)
            inv_ref[rows, :] = jnp.broadcast_to(inv, (16, 128))
            return _

        lax.fori_loop(0, HALF // 16, chunk, 0, unroll=4)

    @pl.loop(0, TOK // BLK)
    def _(t):
        rows = pl.ds(pl.multiple_of(t * BLK, BLK), BLK)
        mixed = bias
        for first, n, ref in weight_blocks(wts):
            lines = slice(first * BLK, (first + n) * BLK)
            mixed = mixed + dot(normed_ref[rows, lines], ref[...].reshape(n * BLK, CAT), NN)
        for s in range(2):
            v = mixed[:, s * 128 : (s + 1) * 128]
            v = v * cos_ref[rows, :] + pltpu.roll(v, 128 - 16, 1) * sa_ref[rows, :] + pltpu.roll(v, 16, 1) * sb_ref[rows, :]
            qkv_ref[rows, s * 128 : (s + 1) * 128] = v.astype(BF16)
        qkv_ref[rows, 256:384] = mixed[:, 256:384].astype(BF16)
        pre = mixed[:, QKV:CAT]
        pre_ref[rows, :] = pre
        act_ref[rows, :] = (0.5 * pre * (1.0 + gelu_tanh_part(pre))).astype(BF16)


def norm_call(xa, xb, tiny, wts, cos, sa, sb):
    outs = [
        shape((TOK, D), BF16),
        shape((TOK, QKV), BF16),
        shape((TOK, FFL), F32),
        shape((TOK, FFL), BF16),
        shape((TOK, 128), F32),
        shape((TOK, 128), F32),
        shape((8, D), F32),
    ]
    args = (*xa, *xb, *tiny, *wts, cos, sa, sb)
    return call("norm_proj", norm_kernel, [vmem()] * 13, outs, args)


def head_masks():
    lane = lax.broadcasted_iota(jnp.int32, (1, 128), 1)
    return [(lane < HEAD_DIM).astype(BF16), (lane >= HEAD_DIM).astype(BF16)]


def masked_scores(qh, k, qi):
    s = dot(qh, k, NT)
    row = lax.broadcasted_iota(jnp.int32, (BLK, BLK), 0)
    column = lax.broadcasted_iota(jnp.int32, (BLK, BLK), 1)
    last = jnp.where(row >= column, s[:, qi * BLK :], -1e30)
    return last if qi == 0 else jnp.concatenate([s[:, : qi * BLK], last], axis=1)


def for_blocks(lengths, body):
    long_first = lengths[0, 0] > lengths[0, 1]
    long_start, short_start = jnp.where(long_first, 0, 256), jnp.where(long_first, 768, 0)

    @pl.loop(0, 2)
    def _(document):
        body(jnp.where(document == 0, long_start, short_start), 0)

    for qi in (1, 2):
        body(long_start, qi)


def attend_kernel(tab, qkv_ref, out_ref, exact_ref, lse_ref):
    masks = head_masks()
    low_lanes = lax.broadcasted_iota(jnp.int32, (BLK, 128), 1) < HEAD_DIM

    def body(start, qi):
        rows = pl.ds(pl.multiple_of(start + qi * BLK, BLK), BLK)
        keys = pl.ds(pl.multiple_of(start, BLK), (qi + 1) * BLK)
        q = qkv_ref[rows, 0:128] * jnp.asarray(0.125, BF16)
        k = qkv_ref[keys, 128:256]
        v = qkv_ref[keys, 256:384]
        total = None
        logs = []
        for m in masks:
            s = masked_scores(q * m, k, qi)
            most = jnp.max(s, axis=1, keepdims=True)
            e = jnp.exp(s - most)
            count = jnp.sum(e, axis=1, keepdims=True)
            p = (e * (1.0 / count)).astype(BF16)
            o = dot(p, v * m, NN)
            total = o if total is None else total + o
            logs.append(most + jnp.log(count))
        out_ref[rows, :] = total.astype(BF16)
        exact_ref[rows, :] = total
        lse_ref[rows, :] = jnp.where(low_lanes, logs[0], logs[1])

    for_blocks(tab, body)


def attend_call(tab, qkv):
    outs = [shape((TOK, 128), BF16), shape((TOK, 128), F32), shape((TOK, 128), F32)]
    return call("attend", attend_kernel, [smem(), vmem()], outs, (tab, qkv))


def attend_back_kernel(
    tab, qkv_ref, do_ref, exact_ref, lse_ref, cos_ref, sa_ref, sb_ref, out_ref, sum_ref, dq, dk, dv
):
    masks = head_masks()
    dk[...] = jnp.zeros_like(dk)
    dv[...] = jnp.zeros_like(dv)
    eighth = jnp.asarray(0.125, BF16)
    causal = lax.broadcasted_iota(jnp.int32, (BLK, BLK), 0) >= lax.broadcasted_iota(jnp.int32, (BLK, BLK), 1)

    def body(start, qi):
        rows = pl.ds(pl.multiple_of(start + qi * BLK, BLK), BLK)
        q = qkv_ref[rows, 0:128]
        do = do_ref[rows, :]
        weighted = do.astype(F32) * exact_ref[rows, :] * 0.125
        lse = lse_ref[rows, :]
        deltas = [jnp.sum(weighted * m.astype(F32), axis=1, keepdims=True) for m in masks]
        logs = [lse[:, 0:1], lse[:, HEAD_DIM : HEAD_DIM + 1]]
        qs = [q * m for m in masks]
        dos = [do * m for m in masks]
        q_both = jnp.concatenate(qs, axis=0)
        do_both = jnp.concatenate(dos, axis=0)
        total = None
        for kj in range(qi + 1):
            keys = pl.ds(pl.multiple_of(start + kj * BLK, BLK), BLK)
            k = qkv_ref[keys, 128:256]
            v = qkv_ref[keys, 256:384]
            ps, dss = [], []
            for h in range(2):
                s = dot(qs[h] * eighth, k, NT)
                if kj == qi:
                    s = jnp.where(causal, s, -1e30)
                p = jnp.exp(s - logs[h])
                dp = dot(dos[h] * eighth, v, NT)
                dss.append((p * (dp - deltas[h])).astype(BF16))
                ps.append(p.astype(BF16))
            part = dot(jnp.concatenate(dss, axis=1), jnp.concatenate([k * m for m in masks], axis=0), NN)
            total = part if total is None else total + part
            dk[keys, :] += dot(jnp.concatenate(dss, axis=0), q_both, TN)
            dv[keys, :] += dot(jnp.concatenate(ps, axis=0), do_both, TN)
        dq[rows, :] = total

    for_blocks(tab, body)
    for s, ref in enumerate((dq, dk, dv)):
        d = ref[...]
        if s < 2:
            d = d * cos_ref[...] - pltpu.roll(d, 128 - 16, 1) * sa_ref[...] - pltpu.roll(d, 16, 1) * sb_ref[...]
        low = d.astype(BF16)
        out_ref[:, s * 128 : (s + 1) * 128] = low
        sum_ref[:, s * 128 : (s + 1) * 128] = jnp.broadcast_to(jnp.sum(low.astype(F32), axis=0, keepdims=True), (8, 128))


def attend_back_call(*args):
    outs = [shape((TOK, QKV), BF16), shape((8, QKV), F32)]
    scratch = [pltpu.VMEM((TOK, 128), F32)] * 3
    return call("attend_back", attend_back_kernel, [smem()] + [vmem()] * 7, outs, args, scratch)


def project_kernel(att_ref, act_ref, *refs):
    wts, outs, whole = refs[0:4], refs[4:8], refs[8]
    place = Place()
    for half in range(2):
        spots = [[place.spot(half, j, i) for i in range(2)] for j in range(8)]

        @pl.loop(0, HALF // BLK)
        def _(t, half=half, spots=spots):
            rows = pl.ds(pl.multiple_of(half * HALF + t * BLK, BLK), BLK)
            here = pl.ds(pl.multiple_of(t * BLK, BLK), BLK)
            both = jnp.concatenate([att_ref[rows, :], act_ref[rows, :]], axis=1)
            for j in range(8):
                part = dot(both, weight_of(wts, j)[...], NT).astype(BF16)
                for i in range(2):
                    whole[spots[j][i], here, :] = part[:, i * 128 : (i + 1) * 128]

        outs[2 * half][...] = whole[0:8]
        outs[2 * half + 1][...] = whole[8:16]


def project_call(att, act, wts):
    outs = [shape((8, HALF, 128), BF16)] * 4
    scratch = [pltpu.VMEM((16, HALF, 128), BF16)]
    return call("project", project_kernel, [vmem()] * 6, outs, (att, act, *wts), scratch)


def upstream_kernel(*refs):
    place = Place()
    halves, wts, pre_ref = (refs[0:2], refs[2:4]), refs[4:8], refs[8]
    g_ref, hid_ref, att_ref, hsum_ref, gsum_ref = refs[9:14]
    mine = jnp.zeros((1, 128), F32)
    for half in range(2):
        for i, (a, k) in enumerate(PIECE_OF):
            g_ref[half * HALF : (half + 1) * HALF, pl.ds(place.lane(half, i), 128)] = halves[half][a][k]
        mine = mine + jnp.sum(halves[half][0][0].astype(F32), axis=0, keepdims=True)
    gsum_ref[...] = jnp.broadcast_to(mine, (8, 128))
    hsum_ref[...] = jnp.zeros_like(hsum_ref)

    @pl.loop(0, TOK // BLK)
    def _(t):
        rows = pl.ds(pl.multiple_of(t * BLK, BLK), BLK)
        d_act = None
        for first, n, ref in weight_blocks(wts):
            lines = slice(first * BLK, (first + n) * BLK)
            part = dot(g_ref[rows, lines], ref[...].reshape(n * BLK, ACT), NN)
            d_act = part if d_act is None else d_act + part
        att_ref[rows, :] = d_act[:, 0:128].astype(BF16)
        v = pre_ref[rows, :]
        th = gelu_tanh_part(v)
        slope = 0.5 * (1.0 + th) + 0.5 * v * (1.0 - th * th) * (0.7978845608028654 * (1.0 + 3.0 * 0.044715 * v * v))
        low = (d_act[:, 128:ACT] * slope).astype(BF16)
        hid_ref[rows, :] = low
        hsum_ref[...] += jnp.broadcast_to(jnp.sum(low.astype(F32), axis=0, keepdims=True), (8, FFL))


def upstream_call(ga, gb, wts, pre, after):
    outs = [
        shape((TOK, D), BF16),
        shape((TOK, FFL), BF16),
        shape((TOK, 128), BF16),
        shape((8, FFL), F32),
        shape((8, 128), F32),
    ]
    args = (*ga, *gb, *wts, pre)
    return call("upstream", upstream_kernel, [vmem()] * 9, outs, args, after=after)


def downstream_kernel(dm_ref, dh_ref, normed_ref, gb_ref, *refs):
    wts, outs, whole, flat = refs[0:4], refs[4:8], refs[8], refs[9]
    place = Place()
    flat[...] = jnp.zeros_like(flat)
    for half in range(2):
        spots = [[place.spot(half, j, i) for i in range(2)] for j in range(8)]

        @pl.loop(0, HALF // BLK)
        def _(b, half=half, spots=spots):
            rows = pl.ds(pl.multiple_of(half * HALF + b * BLK, BLK), BLK)
            here = pl.ds(pl.multiple_of(b * BLK, BLK), BLK)
            both = jnp.concatenate([dm_ref[rows, :], dh_ref[rows, :]], axis=1)
            s1 = jnp.zeros((BLK, 128), F32)
            s2 = jnp.zeros((BLK, 128), F32)
            for j in range(8):
                lines = slice(j * BLK, (j + 1) * BLK)
                part = dot(both, weight_of(wts, j)[...], NT)
                low = part.astype(BF16)
                u1 = part * gb_ref[0:1, lines]
                u2 = part * (normed_ref[rows, lines].astype(F32) - gb_ref[1:2, lines])
                for i in range(2):
                    cut = slice(i * 128, (i + 1) * 128)
                    whole[spots[j][i], here, :] = low[:, cut]
                    s1 = s1 + u1[:, cut]
                    s2 = s2 + u2[:, cut]
            for i in range(BLK // 128):
                cut = slice(i * 128, (i + 1) * 128)
                at = b * (BLK // 64) + 2 * i
                flat[pl.ds(at, 1), :] = jnp.sum(jnp.transpose(s1[cut, :]), axis=0, keepdims=True)
                flat[pl.ds(at + 1, 1), :] = jnp.sum(jnp.transpose(s2[cut, :]), axis=0, keepdims=True)

        low = flat[...].astype(BF16)
        for n, out in enumerate(outs[2 * half : 2 * half + 2]):
            out[:, 0:HALF, :] = whole[8 * n : 8 * n + 8]
            for c in range(8):
                out[c, HALF : HALF + PAD, :] = low


def downstream_call(dm, dh, normed, gb, wts, after):
    outs = [shape((8, HALF + PAD, 128), BF16)] * 4
    scratch = [pltpu.VMEM((16, HALF, 128), BF16), pltpu.VMEM((PAD, 128), F32)]
    args = (dm, dh, normed, gb, *wts)
    return call("downstream", downstream_kernel, [vmem()] * 8, outs, args, scratch, after)


def grad_lanes(p):
    place = lax.rem(p, 4)
    j = p + jnp.where(place == 1, 1, 0) - jnp.where(place == 2, 1, 0)
    return pl.ds(pl.multiple_of(j * BLK, BLK), BLK)


TILE = BLK + PAD
TILE_TWO = ACT + PAD
SPARE = 48
GRAD_ROWS = 7 * TILE + 2 * TILE_TWO + SPARE


def grads_kernel(normed_ref, dm_ref, dh_ref, msum_ref, hsum_ref, att_ref, act_ref, g_ref, gsum_ref, *refs):
    keep, sends, turned = refs[0], refs[1:5], refs[5]
    turned[0:128, :] = jnp.transpose(att_ref[...])
    turned[128:ACT, :] = jnp.transpose(act_ref[...])
    zero = jnp.zeros((8, 128), F32)
    for first in (4, 0):
        if first == 4:
            def put(p, row, value):
                n = value.shape[0]
                while n:
                    part, at = divmod(row, GRAD_ROWS // 4)
                    here = min(n, GRAD_ROWS // 4 - at)
                    sends[part][p, at : at + here, :] = value[:here]
                    value, row, n = value[here:], row + here, n - here
        else:
            def put(p, row, value):
                keep[p, row : row + value.shape[0], :] = value

        @pl.loop(0, 4)
        def _(p, first=first, put=put):
            lanes = grad_lanes(first + p)
            block = normed_ref[:, lanes]
            t = 0
            for ref, sums_ref, n in ((dm_ref, msum_ref, 3), (dh_ref, hsum_ref, 4)):
                part = dot(block, ref[...], TN).astype(BF16)
                for i in range(n):
                    cut = slice(i * 128, (i + 1) * 128)
                    put(p, t * TILE, part[:, cut])
                    sums = jnp.concatenate([sums_ref[:, cut], zero], axis=0).astype(BF16)
                    put(p, t * TILE + BLK, sums)
                    t += 1
            part = dot(turned[...], g_ref[:, lanes], NN).astype(BF16)
            sums = jnp.concatenate([gsum_ref[...], zero], axis=0).astype(BF16)
            for i in range(2):
                at = 7 * TILE + i * TILE_TWO
                put(p, at, part[:, i * 128 : (i + 1) * 128])
                put(p, at + ACT, sums)
            put(p, GRAD_ROWS - SPARE, jnp.zeros((SPARE, 128), BF16))


def grads_call(*args, after):
    scratch = [pltpu.VMEM((ACT, TOK), BF16)]
    return call("grads", grads_kernel, [vmem()] * 9, [shape((4, GRAD_ROWS, 128), BF16)] + [shape((4, GRAD_ROWS // 4, 128), BF16)] * 4, args, scratch, after)


def fold_part(blocks, out_ref, back_ref, got, keep_out, keep_back, send):
    half = blocks // 2
    for i in range(blocks):
        for back, (ref, rows, keep) in enumerate(((out_ref, HALF, keep_out), (back_ref, HALF + PAD, keep_back))):
            if len(got) == 2:
                new = got[back][i]
            else:
                base = back * blocks * HALF + i * rows
                new = got[0][base : base + rows, :]
            total = ref[i].astype(F32) + new.astype(F32)
            if i < half:
                keep[i] = total
            else:
                at = back * half * HALF + (i - half) * rows
                send[at : at + rows, :] = total.astype(BF16)


def fold_call(blocks, a, b, *extra, after=()):
    half, n = blocks // 2, len(a)

    def kernel(*refs):
        ins, outs = refs[: 2 * n], refs[2 * n + len(extra) :]
        for h in range(2):
            mine = ins[h * n : (h + 1) * n]
            fold_part(blocks, mine[0], mine[1], mine[2:], *outs[3 * h : 3 * h + 3])
        for ref, out in zip(refs[2 * n :], outs[6:]):
            out[...] = ref[...]

    outs = [
        shape((half, HALF, 128), F32),
        shape((half, HALF + PAD, 128), F32),
        shape((half * (2 * HALF + PAD), 128), BF16),
    ] * 2 + [shape(e.shape, e.dtype) for e in extra]
    got = call("fold", kernel, [vmem()] * (2 * n + len(extra)), outs, (*a, *b, *extra), after=after)
    return got[0:3], got[3:6], got[6:]


def finish_kernel(oa, ba, ga, ob, bb, gb, x_ref, g_ref, cen_ref, inv_ref, small_ref, out_ref, grad_ref):
    gain = small_ref[0:1, :].astype(F32)
    shift = small_ref[2:3, :].astype(F32) + small_ref[3:4, :].astype(F32)
    for half, (o_ref, b_ref, got) in enumerate(((oa, ba, ga), (ob, bb, gb))):
        sums = b_ref[0, HALF : HALF + PAD, :] + got[2 * HALF : 2 * HALF + PAD, :].astype(F32)
        sums = jnp.transpose(sums) * (1.0 / D)
        for i in range(HALF // 128):
            here = slice(i * 128, (i + 1) * 128)
            there = slice(HALF + i * 128, HALF + (i + 1) * 128)
            rows = slice(half * HALF + i * 128, half * HALF + (i + 1) * 128)
            branch = o_ref[0, here, :] + got[here, :].astype(F32)
            out_ref[rows, :] = (x_ref[rows, :].astype(F32) + branch + shift).astype(BF16)
            d = b_ref[0, here, :] + got[there, :].astype(F32)
            cen = cen_ref[rows, :]
            m1 = sums[:, 2 * i : 2 * i + 1]
            m2 = sums[:, 2 * i + 1 : 2 * i + 2]
            grad_ref[rows, :] = g_ref[rows, :].astype(F32) + inv_ref[rows, :] * (d * gain - m1 - cen * m2)


def finish_call(*args):
    outs = [shape((TOK, 128), BF16), shape((TOK, 128), F32)]
    return call("finish", finish_kernel, [vmem()] * 11, outs, args, final=True)


def norm_sums_kernel(ba, ga, bb, gb, cen_ref, sum_ref):
    gain = jnp.zeros((1, 128), F32)
    shift = jnp.zeros((1, 128), F32)
    for half, (b_ref, got) in enumerate(((ba, ga), (bb, gb))):
        d = b_ref[0, 0:HALF, :] + got[HALF : 2 * HALF, :].astype(F32)
        gain = gain + jnp.sum(d * cen_ref[half * HALF : (half + 1) * HALF, :], axis=0, keepdims=True)
        shift = shift + jnp.sum(d, axis=0, keepdims=True)
    sum_ref[...] = jnp.concatenate([gain, shift, jnp.zeros((6, 128), F32)], axis=0)


def norm_sums_call(*args, after):
    return call("norm_sums", norm_sums_kernel, [vmem()] * 5, [shape((8, 128), F32)], args, after=after)[0]


def fold_core_call(kept, *got):
    n = GRAD_ROWS // len(got)

    def kernel(kept_ref, *refs):
        ins, keep_ref, sends = refs[0 : len(got)], refs[len(got)], refs[len(got) + 1 :]
        for m, ref in enumerate(ins):
            rows = slice(m * n, (m + 1) * n)
            for i in range(2):
                keep_ref[i, rows, :] = kept_ref[i, rows, :].astype(F32) + ref[i].astype(F32)
                sends[1 - i][0, rows, :] = (kept_ref[2 + i, rows, :].astype(F32) + ref[2 + i].astype(F32)).astype(BF16)

    outs = [shape((2, GRAD_ROWS, 128), F32)] + [shape((1, GRAD_ROWS, 128), BF16)] * 2
    return call("fold_core", kernel, [vmem()] * (1 + len(got)), outs, (kept, *got))


def fold_row_call(kept, got, after):
    def kernel(kept_ref, got_ref, send_ref):
        send_ref[0] = (kept_ref[1] + got_ref[0].astype(F32)).astype(BF16)

    return call("fold_row", kernel, [vmem()] * 2, [shape((1, GRAD_ROWS, 128), BF16)], (kept, got), after=after)[0]


def lanes_of(v, row, width):
    total = 8 * width
    return pltpu.roll(v, lax.rem(total - row * width, total), 1)[:, 0:width]


def close_kernel(kept_ref, near_ref, far_ref, qkv_ref, qb_ref, up_ref, ub_ref, out_ref, down_ref, bias_ref, again_ref):
    def total(first, n):
        rows = slice(first, first + n)
        return kept_ref[0, rows, :] + near_ref[0, rows, :].astype(F32) + far_ref[0, rows, :].astype(F32)

    row = lax.axis_index("row")
    for s in range(3):
        qkv_ref[s] = total(s * TILE, BLK)
        qb_ref[s : s + 1, :] = lanes_of(total(s * TILE + BLK, PAD)[0:8], row, 16)[0:1]
    for i in range(4):
        up_ref[:, i * 128 : (i + 1) * 128] = total((3 + i) * TILE, BLK)
    bias = jnp.concatenate([total((3 + i) * TILE + BLK, PAD)[0:8] for i in range(4)], axis=1)
    ub_ref[...] = lanes_of(bias, row, 64)[0:1]
    for i in range(2):
        at = 7 * TILE + i * TILE_TWO
        out_ref[:, i * 128 : (i + 1) * 128] = total(at, 128)
        down_ref[:, i * 128 : (i + 1) * 128] = total(at + 128, FFL)
    bias = lanes_of(total(7 * TILE + ACT, PAD)[0:8], row, 16)[0:1]
    bias_ref[...] = bias
    again_ref[...] = bias


def close_call(*args):
    outs = [
        shape((3, BLK, 128), F32),
        shape((3, 16), F32),
        shape((BLK, FFL), F32),
        shape((1, 64), F32),
        shape((128, BLK), F32),
        shape((FFL, BLK), F32),
        shape((1, 16), F32),
        shape((1, 16), F32),
    ]
    return call("close", close_kernel, [vmem()] * 3, outs, args, final=True)


def close_norm_kernel(*refs):
    total = refs[0][...]
    for ref in refs[1:4]:
        total = total + ref[...]
    mine = lanes_of(total, lax.axis_index("row"), 16)
    refs[4][...] = mine[0:1]
    refs[5][...] = mine[1:2]


def close_norm_call(*args, after):
    return call("close_norm", close_norm_kernel, [vmem()] * 4, [shape((1, 16), F32)] * 2, args, after=after, final=True)


def join(*groups, after=()):
    groups = [[p if isinstance(p, tuple) else (p, 0, p.shape[0]) for p in group] for group in groups]
    flat = [p for group in groups for p in group]

    def kernel(*refs):
        ins, outs = refs[: len(flat)], refs[len(flat) :]
        n = 0
        for group, out in zip(groups, outs):
            at = 0
            for _, lo, hi in group:
                out[at : at + hi - lo] = ins[n][lo:hi]
                at += hi - lo
                n += 1

    outs = []
    for group in groups:
        first = group[0][0]
        outs.append(shape((sum(hi - lo for _, lo, hi in group),) + first.shape[1:], first.dtype))
    return call("join", kernel, [vmem()] * len(flat), outs, [p[0] for p in flat], after=after)


def fetch(copies):
    for copy in copies:
        copy.start()
    for copy in copies:
        copy.wait()


def in_hbm(*arrays):
    return [pltpu.with_memory_space_constraint(a, pltpu.HBM) for a in arrays]


def begin_kernel(x_ref, g_ref, a_ref, b_ref, sem):
    copies = []
    for half, out in enumerate((a_ref, b_ref)):
        for i, ref in enumerate((x_ref, g_ref)):
            copies.append(pltpu.make_async_copy(ref.at[pl.ds(half * HALF, HALF)], out.at[i], sem.at[half * 2 + i]))
    fetch(copies)


def begin_call(*args, after):
    scratch = [pltpu.SemaphoreType.DMA((4,))]
    specs = [pl.BlockSpec(memory_space=pltpu.HBM)] * 2
    return call("begin", begin_kernel, specs, [shape((2, HALF, 128), BF16)] * 2, in_hbm(*args), scratch, after)


def pack_kernel(qkv_ref, up_ref, out_ref, down_ref, packed, out_here, down_here, sem):
    copies = [
        pltpu.make_async_copy(qkv_ref.at[s], packed.at[0, :, pl.ds(s * 128, 128)], sem.at[s]) for s in range(3)
    ]
    copies.append(pltpu.make_async_copy(up_ref, packed.at[0, :, pl.ds(QKV, FFL)], sem.at[3]))
    copies.append(pltpu.make_async_copy(out_ref, out_here, sem.at[4]))
    copies.append(pltpu.make_async_copy(down_ref, down_here, sem.at[5]))
    fetch(copies)
    packed[0, :, CAT : CAT + 128] = jnp.transpose(out_here[...])
    packed[0, :, CAT + 128 : ALL] = jnp.transpose(down_here[...])


def pack_call(*args, after):
    outs = [shape((1, BLK, ALL), BF16)]
    scratch = [pltpu.VMEM((128, BLK), BF16), pltpu.VMEM((FFL, BLK), BF16), pltpu.SemaphoreType.DMA((6,))]
    specs = [pl.BlockSpec(memory_space=pltpu.HBM)] * 4
    return call("pack", pack_kernel, specs, outs, in_hbm(*args), scratch, after)[0]


def unpack_kernel(mine, got, cats, twos):
    for i, ref in enumerate((mine, got)):
        cats[i] = ref[0, :, 0:CAT]
        twos[i] = ref[0, :, CAT:ALL]


def unpack_call(*args):
    outs = [shape((2, BLK, CAT), BF16), shape((2, BLK, ACT), BF16)]
    return call("unpack", unpack_kernel, [vmem()] * 2, outs, args)


def both(mine, got):
    n = mine.shape[0] // 2
    return [(mine, 0, n), (got, 0, n), (mine, n, 2 * n), (got, n, 2 * n)]


def rotary_tables(long_start):
    places = jnp.arange(TOK, dtype=jnp.int32)
    begin_second = jnp.where(long_start == 0, 768, 256)
    positions = jnp.where(places >= begin_second, places - begin_second, places)
    lane = jnp.arange(128, dtype=jnp.int32)
    spot = lane % HEAD_DIM
    half = ROT // 2
    inverse = 10000.0 ** (-2.0 * (spot % half).astype(F32) / ROT)
    angles = positions.astype(F32)[:, None] * inverse[None, :]
    turned = (spot < ROT)[None, :]
    cos = jnp.where(turned, jnp.cos(angles), 1.0)
    sine = jnp.sin(angles)
    low = jnp.where((spot < half)[None, :], -sine, 0.0)
    high = jnp.where(((spot >= half) & (spot < ROT))[None, :], sine, 0.0)
    return cos, low, high


def shards(x, lengths, w_qkv, b_qkv, w_out, b_out, w_up, b_up, w_down, b_down, gain, shift, g):
    row = lax.axis_index("row")
    cos, sa, sb = rotary_tables(jnp.where(lengths[0, 0] > lengths[0, 1], 0, 256))

    def spread(v, width):
        wide = jnp.zeros(v.shape[:-1] + (8, width), BF16)
        return lax.dynamic_update_slice_in_dim(wide, v[..., None, :], row, v.ndim - 1).reshape(-1, 128)

    small = [spread(jnp.stack([gain, shift, b_out, b_down]), 16), spread(b_qkv, 16), spread(b_up, 64)]
    small = jnp.concatenate(small + [jnp.zeros((PAD - 11, 128), BF16)])
    small = small + exchange(small, "c")
    weights = pack_call(w_qkv.transpose(1, 0, 2), w_up, w_out, w_down, after=(small,))
    weights_got = exchange(weights, "z", 0)
    a, b = begin_call(x, g, after=(small,))
    a_got, b_got = exchange(a, "x", 0), exchange(b, "y", 0)
    small = small + exchange(small, "z", 1)
    small, a, b = join([small], both(a, a_got), both(b, b_got), after=(weights_got,))
    a_got, b_got = exchange(a, "x", 1), exchange(b, "y", 1)
    cats, twos = unpack_call(weights, weights_got)
    cats_got = exchange(cats, "z", 1)
    cats = (cats, cats_got, exchange(cats, "c"), exchange(cats_got, "c"))
    small = small + exchange(small, "z", 0)
    tiny, twos, a, b = join([small[None]], [twos], both(a, a_got), both(b, b_got))
    tiny_got = exchange(tiny, "x", 1)
    a_got, b_got = exchange(a, "y", 0), exchange(b, "x", 0)
    twos_got = exchange(twos, "z", 1)
    twos = (twos, twos_got, exchange(twos, "c"), exchange(twos_got, "c"))
    (tiny,) = join([tiny, tiny_got], after=(cats_got,))
    tiny_got = exchange(tiny, "y", 1)
    first = lambda v, got: [(v, 0, 4), (got, 0, 4)]
    last = lambda v, got: [(v, 4, 8), (got, 4, 8)]
    tiny, xa, xb, ga, gb = join(
        [tiny, tiny_got],
        first(a, a_got),
        first(b, b_got),
        last(a, a_got),
        last(b, b_got),
        after=(twos_got, cos, sa, sb),
    )
    tiny_got = exchange(tiny, "x", 0)
    xa, xb = (xa, exchange(xa, "y", 1)), (xb, exchange(xb, "x", 1))
    (tiny,) = join([tiny, tiny_got])
    tiny = (tiny, exchange(tiny, "y", 0))
    ga, gb = (ga, exchange(ga, "y", 1)), (gb, exchange(gb, "x", 1))

    normed, qkv, pre, act, centered, inv, gains = norm_call(xa, xb, tiny, cats, cos, sa, sb)
    att, exact, lse = attend_call(lengths, qkv)
    out_a, send_a, out_b, send_b = project_call(att, act, twos)
    out_a_got, out_b_got = exchange(send_a, "y", 0), exchange(send_b, "x", 0)
    g_all, d_hid, d_att, hsum, gsum = upstream_call(ga, gb, twos, pre, (out_a,))
    d_mix, msum = attend_back_call(lengths, qkv, d_att, exact, lse, cos, sa, sb)
    back_a, send_a, back_b, send_b = downstream_call(d_mix, d_hid, normed, gains, cats, ())
    back_a_got, back_b_got = exchange(send_a, "y", 0), exchange(send_b, "x", 0)
    keep, *sends = grads_call(normed, d_mix, d_hid, msum, hsum, att, act, g_all, gsum, after=(back_a, out_a_got, out_b_got))
    got = [exchange(send, "c") for send in sends]
    a, b, _ = fold_call(8, (out_a, back_a, out_a_got, back_a_got), (out_b, back_b, out_b_got, back_b_got))
    a_got, b_got = exchange(a[2], "y", 1), exchange(b[2], "x", 1)
    keep, *sends = fold_core_call(keep, *got)
    first, last = [exchange(send, "z", 0) for send in sends]
    a, b, _ = fold_call(4, (a[0], a[1], a_got), (b[0], b[1], b_got))
    a_got, b_got = exchange(a[2], "x", 0), exchange(b[2], "y", 0)
    a, b, _ = fold_call(2, (a[0], a[1], a_got), (b[0], b[1], b_got))
    a_got, b_got = exchange(a[2], "x", 1), exchange(b[2], "y", 1)
    got = exchange(fold_row_call(keep, first, (a[0],)), "z", 1)
    sums = norm_sums_call(a[1], a_got, b[1], b_got, centered, after=(last,))
    sums = sums + exchange(sums, "c")
    block_out, input_grad = finish_call(a[0], a[1], a_got, b[0], b[1], b_got, x, g, centered, inv, small)
    qkv_grad, qkv_bias, up_grad, up_bias, out_grad, down_grad, out_bias, down_bias = close_call(keep, last, got)
    gain_grad, shift_grad = close_norm_call(
        sums, *(exchange(sums, "z", n) for n in range(3)), after=in_hbm(up_grad, input_grad)
    )
    return (
        block_out,
        input_grad,
        qkv_grad.transpose(1, 0, 2),
        qkv_bias,
        out_grad,
        out_bias.reshape(16),
        up_grad,
        up_bias.reshape(64),
        down_grad,
        down_bias.reshape(16),
        gain_grad.reshape(16),
        shift_grad.reshape(16),
    )


def solution(mesh):
    both = P(("col", "row"))
    in_specs = (
        P("row", "col"),
        P("row", None),
        P("row", None, "col"),
        P(None, ("col", "row")),
        P("col", "row"),
        both,
        P("row", "col"),
        both,
        P("col", "row"),
        both,
        both,
        both,
        P("row", "col"),
    )
    out_specs = (
        P("row", "col"),
        P("row", "col"),
        P("row", None, "col"),
        P(None, ("col", "row")),
        P("col", "row"),
        both,
        P("row", "col"),
        both,
        P("col", "row"),
        both,
        both,
        both,
    )
    return jax.shard_map(shards, mesh=mesh, in_specs=in_specs, out_specs=out_specs, check_vma=False)
```

```python
import functools

import jax
import jax.numpy as jnp
from jax import lax
from jax.experimental import pallas as pl
from jax.experimental.pallas import tpu as pltpu
from jax.sharding import PartitionSpec as P

D = 2048
HEAD_DIM = 64
ROT = 32
EPS = 1e-05
TOK = 1024
HALF = 512
QKV = 384
FFL = 512
CAT = QKV + FFL
ACT = 128 + FFL
ALL = CAT + ACT
PAD = 16
BLK = 256
F32 = jnp.float32
BF16 = jnp.bfloat16
MIB = 2**20

MASKS = ((1, 3, 2), (3, 1, 2))


def exchange(value, axis, step=0):
    pairs = []
    for z in range(4):
        for k in range(2):
            m = MASKS[k][step]
            for y in range(4):
                for x in range(4):
                    to = {
                        "x": (x ^ m, y, z, k),
                        "y": (x, y ^ m, z, k),
                        "z": (x, y, z ^ m, k),
                        "c": (x, y, z, 1 - k),
                    }[axis]
                    pairs.append(((z * 2 + k) * 16 + y * 4 + x, (to[2] * 2 + to[3]) * 16 + to[1] * 4 + to[0]))
    return lax.ppermute(value, ("row", "col"), pairs)


PIECE_OF = [(i // 8, i % 8) for i in range(16)]
NN = ((1,), (0,))
NT = ((1,), (1,))
TN = ((0,), (0,))


def dot(a, b, dims):
    return lax.dot_general(a, b, (dims, ((), ())), preferred_element_type=F32)


def weight_blocks(refs):
    first = 0
    for ref in refs:
        yield first, ref.shape[0], ref
        first += ref.shape[0]


def weight_of(refs, j):
    for first, n, ref in weight_blocks(refs):
        if first <= j < first + n:
            return ref.at[j - first]


def gelu_tanh_part(v):
    return jnp.tanh(0.7978845608028654 * (v + 0.044715 * v * v * v))


class Place:
    def __init__(self):
        row, col = lax.axis_index("row"), lax.axis_index("col")
        self.row = row
        self.z, self.core, self.y, self.x = lax.div(row, 2), lax.rem(row, 2), lax.div(col, 4), lax.rem(col, 4)
        self.m1 = jnp.where(self.core == 0, 1, 3)
        self.m2 = 4 - self.m1
        self.seen = (0, self.m1, self.m2, 2)

    def swapped(self, mask):
        return jnp.where(mask == self.m2, 1, jnp.where(mask == self.m1, 2, jnp.where(mask == 2, 3, 0)))

    def lane(self, half, i):
        outer, inner = self.seen[i // 4], self.seen[i % 4]
        y, x = (self.y ^ outer, self.x ^ inner) if half == 0 else (self.y ^ inner, self.x ^ outer)
        owner = y * 2 + lax.div(x, 2)
        mask = lax.div(owner, 2) ^ self.z
        same = lax.rem(owner, 2) == self.core
        first = jnp.where(mask == self.m1, 1, jnp.where(mask == self.m2, 2, jnp.where(mask == 2, 3, 0)))
        block = jnp.where(same, first, 4 + self.swapped(mask))
        return pl.multiple_of((block * 2 + lax.rem(x, 2)) * 128, 128)

    def spot(self, half, j, i):
        if j < 4:
            z, core = self.z ^ self.seen[j], self.core
        else:
            z, core = self.z ^ (0, self.m2, self.m1, 2)[j - 4], 1 - self.core
        owner = (z * 2 + core) * 2 + i
        y, x = self.swapped(lax.div(owner, 4) ^ self.y), self.swapped(lax.rem(owner, 4) ^ self.x)
        return y * 4 + x if half == 0 else x * 4 + y


def vmem():
    return pl.BlockSpec(memory_space=pltpu.VMEM)


def smem():
    return pl.BlockSpec(memory_space=pltpu.SMEM)


def any_spec():
    return pl.BlockSpec(memory_space=pl.ANY)


def shape(dims, dtype):
    return jax.ShapeDtypeStruct(dims, dtype)


WORK = dict(norm_proj=9, attend=3, project=5, upstream=6, attend_back=7, downstream=6, grads=11)
VMEM_MIB = dict(norm_proj=7, attend=8, project=7, upstream=7, attend_back=11, downstream=8, grads=8)


def call(name, kernel, specs, outs, args, scratch=(), after=(), final=False):
    if after:
        body, n = kernel, len(args)
        kernel = lambda *refs: body(*refs[:n], *refs[n + len(after) :])
        specs = list(specs) + [any_spec()] * len(after)
    return pl.pallas_call(
        kernel,
        in_specs=specs,
        out_specs=[vmem()] * len(outs),
        out_shape=outs if final else [pltpu.VMEM(o.shape, o.dtype) for o in outs],
        scratch_shapes=list(scratch),
        compiler_params=pltpu.CompilerParams(vmem_limit_bytes=VMEM_MIB.get(name, 3) * MIB),
        cost_estimate=pl.CostEstimate(flops=int(WORK.get(name, 0) * 2.5e8), bytes_accessed=0, transcendentals=0),
        name=name,
    )(*args, *after)


def norm_kernel(*refs):
    place = Place()
    halves, tiny, wts = (refs[0:2], refs[2:4]), refs[4:6], refs[6:10]
    cos_ref, sa_ref, sb_ref = refs[10:13]
    normed_ref, qkv_ref, pre_ref, act_ref, cen_ref, inv_ref, gb_ref = refs[13:]

    lanes = [[place.lane(half, i) for i in range(16)] for half in range(2)]

    def lane(half, i):
        return lanes[half][i]

    def tiny_of(i):
        return PIECE_OF[(0, 8, 2, 10)[i // 4] + (0, 4, 1, 5)[i % 4]]

    def tiny_row(i, row):
        a, k = tiny_of(i)
        return tiny[a][k, row : row + 1, :].astype(F32)

    for i in range(16):
        a, k = tiny_of(i)
        gb_ref[:, pl.ds(lane(0, i), 128)] = tiny[a][k].astype(F32)[0:8]
    bias = jnp.concatenate([tiny_row(0, 4 + i) for i in range(7)], axis=1)

    for half in range(2):
        pieces = halves[half]

        def chunk(t, _, half=half, pieces=pieces):
            here = pl.ds(pl.multiple_of(t * 16, 16), 16)
            rows = pl.ds(pl.multiple_of(half * HALF + t * 16, 16), 16)
            xs = [pieces[a][k, here, :].astype(F32) for a, k in PIECE_OF]
            total = xs[0]
            square = xs[0] * xs[0]
            for x in xs[1:]:
                total = total + x
                square = square + x * x
            mean = jnp.sum(total, axis=1, keepdims=True) * (1.0 / D)
            square = jnp.sum(square, axis=1, keepdims=True) * (1.0 / D)
            inv = lax.rsqrt(square - mean * mean + EPS)
            for i, x in enumerate(xs):
                j = i if half == 0 else (i % 4) * 4 + i // 4
                centered = (x - mean) * inv
                if i == 0:
                    cen_ref[rows, :] = centered
                normed_ref[rows, pl.ds(lane(half, i), 128)] = (centered * tiny_row(j, 0) + tiny_row(j, 1)).astype(BF16)
            inv_ref[rows, :] = jnp.broadcast_to(inv, (16, 128))
            return _

        lax.fori_loop(0, HALF // 16, chunk, 0, unroll=4)

    @pl.loop(0, TOK // BLK)
    def _(t):
        rows = pl.ds(pl.multiple_of(t * BLK, BLK), BLK)
        mixed = bias
        for first, n, ref in weight_blocks(wts):
            lines = slice(first * BLK, (first + n) * BLK)
            mixed = mixed + dot(normed_ref[rows, lines], ref[...].reshape(n * BLK, CAT), NN)
        for s in range(2):
            v = mixed[:, s * 128 : (s + 1) * 128]
            v = v * cos_ref[rows, :] + pltpu.roll(v, 128 - 16, 1) * sa_ref[rows, :] + pltpu.roll(v, 16, 1) * sb_ref[rows, :]
            qkv_ref[rows, s * 128 : (s + 1) * 128] = v.astype(BF16)
        qkv_ref[rows, 256:384] = mixed[:, 256:384].astype(BF16)
        pre = mixed[:, QKV:CAT]
        pre_ref[rows, :] = pre
        act_ref[rows, :] = (0.5 * pre * (1.0 + gelu_tanh_part(pre))).astype(BF16)


def norm_call(xa, xb, tiny, wts, cos, sa, sb):
    outs = [
        shape((TOK, D), BF16),
        shape((TOK, QKV), BF16),
        shape((TOK, FFL), F32),
        shape((TOK, FFL), BF16),
        shape((TOK, 128), F32),
        shape((TOK, 128), F32),
        shape((8, D), F32),
    ]
    args = (*xa, *xb, *tiny, *wts, cos, sa, sb)
    return call("norm_proj", norm_kernel, [vmem()] * 13, outs, args)


def head_masks():
    lane = lax.broadcasted_iota(jnp.int32, (1, 128), 1)
    return [(lane < HEAD_DIM).astype(BF16), (lane >= HEAD_DIM).astype(BF16)]


def masked_scores(qh, k, qi):
    s = dot(qh, k, NT)
    row = lax.broadcasted_iota(jnp.int32, (BLK, BLK), 0)
    column = lax.broadcasted_iota(jnp.int32, (BLK, BLK), 1)
    last = jnp.where(row >= column, s[:, qi * BLK :], -1e30)
    return last if qi == 0 else jnp.concatenate([s[:, : qi * BLK], last], axis=1)


def for_blocks(lengths, body):
    long_first = lengths[0, 0] > lengths[0, 1]
    long_start, short_start = jnp.where(long_first, 0, 256), jnp.where(long_first, 768, 0)

    @pl.loop(0, 2)
    def _(document):
        body(jnp.where(document == 0, long_start, short_start), 0)

    for qi in (1, 2):
        body(long_start, qi)


def attend_kernel(tab, qkv_ref, out_ref, exact_ref, lse_ref):
    masks = head_masks()
    low_lanes = lax.broadcasted_iota(jnp.int32, (BLK, 128), 1) < HEAD_DIM

    def body(start, qi):
        rows = pl.ds(pl.multiple_of(start + qi * BLK, BLK), BLK)
        keys = pl.ds(pl.multiple_of(start, BLK), (qi + 1) * BLK)
        q = qkv_ref[rows, 0:128] * jnp.asarray(0.125, BF16)
        k = qkv_ref[keys, 128:256]
        v = qkv_ref[keys, 256:384]
        total = None
        logs = []
        for m in masks:
            s = masked_scores(q * m, k, qi)
            most = jnp.max(s, axis=1, keepdims=True)
            e = jnp.exp(s - most)
            count = jnp.sum(e, axis=1, keepdims=True)
            p = (e * (1.0 / count)).astype(BF16)
            o = dot(p, v * m, NN)
            total = o if total is None else total + o
            logs.append(most + jnp.log(count))
        out_ref[rows, :] = total.astype(BF16)
        exact_ref[rows, :] = total
        lse_ref[rows, :] = jnp.where(low_lanes, logs[0], logs[1])

    for_blocks(tab, body)


def attend_call(tab, qkv):
    outs = [shape((TOK, 128), BF16), shape((TOK, 128), F32), shape((TOK, 128), F32)]
    return call("attend", attend_kernel, [smem(), vmem()], outs, (tab, qkv))


def attend_back_kernel(
    tab, qkv_ref, do_ref, exact_ref, lse_ref, cos_ref, sa_ref, sb_ref, out_ref, sum_ref, dq, dk, dv
):
    masks = head_masks()
    dk[...] = jnp.zeros_like(dk)
    dv[...] = jnp.zeros_like(dv)
    eighth = jnp.asarray(0.125, BF16)
    causal = lax.broadcasted_iota(jnp.int32, (BLK, BLK), 0) >= lax.broadcasted_iota(jnp.int32, (BLK, BLK), 1)

    def body(start, qi):
        rows = pl.ds(pl.multiple_of(start + qi * BLK, BLK), BLK)
        q = qkv_ref[rows, 0:128]
        do = do_ref[rows, :]
        weighted = do.astype(F32) * exact_ref[rows, :] * 0.125
        lse = lse_ref[rows, :]
        deltas = [jnp.sum(weighted * m.astype(F32), axis=1, keepdims=True) for m in masks]
        logs = [lse[:, 0:1], lse[:, HEAD_DIM : HEAD_DIM + 1]]
        qs = [q * m for m in masks]
        dos = [do * m for m in masks]
        q_both = jnp.concatenate(qs, axis=0)
        do_both = jnp.concatenate(dos, axis=0)
        total = None
        for kj in range(qi + 1):
            keys = pl.ds(pl.multiple_of(start + kj * BLK, BLK), BLK)
            k = qkv_ref[keys, 128:256]
            v = qkv_ref[keys, 256:384]
            ps, dss = [], []
            for h in range(2):
                s = dot(qs[h] * eighth, k, NT)
                if kj == qi:
                    s = jnp.where(causal, s, -1e30)
                p = jnp.exp(s - logs[h])
                dp = dot(dos[h] * eighth, v, NT)
                dss.append((p * (dp - deltas[h])).astype(BF16))
                ps.append(p.astype(BF16))
            part = dot(jnp.concatenate(dss, axis=1), jnp.concatenate([k * m for m in masks], axis=0), NN)
            total = part if total is None else total + part
            dk[keys, :] += dot(jnp.concatenate(dss, axis=0), q_both, TN)
            dv[keys, :] += dot(jnp.concatenate(ps, axis=0), do_both, TN)
        dq[rows, :] = total

    for_blocks(tab, body)
    for s, ref in enumerate((dq, dk, dv)):
        d = ref[...]
        if s < 2:
            d = d * cos_ref[...] - pltpu.roll(d, 128 - 16, 1) * sa_ref[...] - pltpu.roll(d, 16, 1) * sb_ref[...]
        low = d.astype(BF16)
        out_ref[:, s * 128 : (s + 1) * 128] = low
        sum_ref[:, s * 128 : (s + 1) * 128] = jnp.broadcast_to(jnp.sum(low.astype(F32), axis=0, keepdims=True), (8, 128))


def attend_back_call(*args):
    outs = [shape((TOK, QKV), BF16), shape((8, QKV), F32)]
    scratch = [pltpu.VMEM((TOK, 128), F32)] * 3
    return call("attend_back", attend_back_kernel, [smem()] + [vmem()] * 7, outs, args, scratch)


def project_kernel(att_ref, act_ref, *refs):
    wts, outs, whole = refs[0:4], refs[4:8], refs[8]
    place = Place()
    for half in range(2):
        spots = [[place.spot(half, j, i) for i in range(2)] for j in range(8)]

        @pl.loop(0, HALF // BLK)
        def _(t, half=half, spots=spots):
            rows = pl.ds(pl.multiple_of(half * HALF + t * BLK, BLK), BLK)
            here = pl.ds(pl.multiple_of(t * BLK, BLK), BLK)
            both = jnp.concatenate([att_ref[rows, :], act_ref[rows, :]], axis=1)
            for j in range(8):
                part = dot(both, weight_of(wts, j)[...], NT).astype(BF16)
                for i in range(2):
                    whole[spots[j][i], here, :] = part[:, i * 128 : (i + 1) * 128]

        outs[2 * half][...] = whole[0:8]
        outs[2 * half + 1][...] = whole[8:16]


def project_call(att, act, wts):
    outs = [shape((8, HALF, 128), BF16)] * 4
    scratch = [pltpu.VMEM((16, HALF, 128), BF16)]
    return call("project", project_kernel, [vmem()] * 6, outs, (att, act, *wts), scratch)


def upstream_kernel(*refs):
    place = Place()
    halves, wts, pre_ref = (refs[0:2], refs[2:4]), refs[4:8], refs[8]
    g_ref, hid_ref, att_ref, hsum_ref, gsum_ref = refs[9:14]
    mine = jnp.zeros((1, 128), F32)
    for half in range(2):
        for i, (a, k) in enumerate(PIECE_OF):
            g_ref[half * HALF : (half + 1) * HALF, pl.ds(place.lane(half, i), 128)] = halves[half][a][k]
        mine = mine + jnp.sum(halves[half][0][0].astype(F32), axis=0, keepdims=True)
    gsum_ref[...] = jnp.broadcast_to(mine, (8, 128))
    hsum_ref[...] = jnp.zeros_like(hsum_ref)

    @pl.loop(0, TOK // BLK)
    def _(t):
        rows = pl.ds(pl.multiple_of(t * BLK, BLK), BLK)
        d_act = None
        for first, n, ref in weight_blocks(wts):
            lines = slice(first * BLK, (first + n) * BLK)
            part = dot(g_ref[rows, lines], ref[...].reshape(n * BLK, ACT), NN)
            d_act = part if d_act is None else d_act + part
        att_ref[rows, :] = d_act[:, 0:128].astype(BF16)
        v = pre_ref[rows, :]
        th = gelu_tanh_part(v)
        slope = 0.5 * (1.0 + th) + 0.5 * v * (1.0 - th * th) * (0.7978845608028654 * (1.0 + 3.0 * 0.044715 * v * v))
        low = (d_act[:, 128:ACT] * slope).astype(BF16)
        hid_ref[rows, :] = low
        hsum_ref[...] += jnp.broadcast_to(jnp.sum(low.astype(F32), axis=0, keepdims=True), (8, FFL))


def upstream_call(ga, gb, wts, pre, after):
    outs = [
        shape((TOK, D), BF16),
        shape((TOK, FFL), BF16),
        shape((TOK, 128), BF16),
        shape((8, FFL), F32),
        shape((8, 128), F32),
    ]
    args = (*ga, *gb, *wts, pre)
    return call("upstream", upstream_kernel, [vmem()] * 9, outs, args, after=after)


def downstream_kernel(dm_ref, dh_ref, normed_ref, gb_ref, *refs):
    wts, outs, whole, flat = refs[0:4], refs[4:8], refs[8], refs[9]
    place = Place()
    flat[...] = jnp.zeros_like(flat)
    for half in range(2):
        spots = [[place.spot(half, j, i) for i in range(2)] for j in range(8)]

        @pl.loop(0, HALF // BLK)
        def _(b, half=half, spots=spots):
            rows = pl.ds(pl.multiple_of(half * HALF + b * BLK, BLK), BLK)
            here = pl.ds(pl.multiple_of(b * BLK, BLK), BLK)
            both = jnp.concatenate([dm_ref[rows, :], dh_ref[rows, :]], axis=1)
            s1 = jnp.zeros((BLK, 128), F32)
            s2 = jnp.zeros((BLK, 128), F32)
            for j in range(8):
                lines = slice(j * BLK, (j + 1) * BLK)
                part = dot(both, weight_of(wts, j)[...], NT)
                low = part.astype(BF16)
                u1 = part * gb_ref[0:1, lines]
                u2 = part * (normed_ref[rows, lines].astype(F32) - gb_ref[1:2, lines])
                for i in range(2):
                    cut = slice(i * 128, (i + 1) * 128)
                    whole[spots[j][i], here, :] = low[:, cut]
                    s1 = s1 + u1[:, cut]
                    s2 = s2 + u2[:, cut]
            for i in range(BLK // 128):
                cut = slice(i * 128, (i + 1) * 128)
                at = b * (BLK // 64) + 2 * i
                flat[pl.ds(at, 1), :] = jnp.sum(jnp.transpose(s1[cut, :]), axis=0, keepdims=True)
                flat[pl.ds(at + 1, 1), :] = jnp.sum(jnp.transpose(s2[cut, :]), axis=0, keepdims=True)

        low = flat[...].astype(BF16)
        for n, out in enumerate(outs[2 * half : 2 * half + 2]):
            out[:, 0:HALF, :] = whole[8 * n : 8 * n + 8]
            for c in range(8):
                out[c, HALF : HALF + PAD, :] = low


def downstream_call(dm, dh, normed, gb, wts, after):
    outs = [shape((8, HALF + PAD, 128), BF16)] * 4
    scratch = [pltpu.VMEM((16, HALF, 128), BF16), pltpu.VMEM((PAD, 128), F32)]
    args = (dm, dh, normed, gb, *wts)
    return call("downstream", downstream_kernel, [vmem()] * 8, outs, args, scratch, after)


def grad_lanes(p):
    place = lax.rem(p, 4)
    j = p + jnp.where(place == 1, 1, 0) - jnp.where(place == 2, 1, 0)
    return pl.ds(pl.multiple_of(j * BLK, BLK), BLK)


TILE = BLK + PAD
TILE_TWO = ACT + PAD
SPARE = 48
GRAD_ROWS = 7 * TILE + 2 * TILE_TWO + SPARE


def grads_kernel(normed_ref, dm_ref, dh_ref, msum_ref, hsum_ref, att_ref, act_ref, g_ref, gsum_ref, *refs):
    keep, sends, turned = refs[0], refs[1:5], refs[5]
    turned[0:128, :] = jnp.transpose(att_ref[...])
    turned[128:ACT, :] = jnp.transpose(act_ref[...])
    zero = jnp.zeros((8, 128), F32)
    for first in (4, 0):
        if first == 4:
            def put(p, row, value):
                n = value.shape[0]
                while n:
                    part, at = divmod(row, GRAD_ROWS // 4)
                    here = min(n, GRAD_ROWS // 4 - at)
                    sends[part][p, at : at + here, :] = value[:here]
                    value, row, n = value[here:], row + here, n - here
        else:
            def put(p, row, value):
                keep[p, row : row + value.shape[0], :] = value

        @pl.loop(0, 4)
        def _(p, first=first, put=put):
            lanes = grad_lanes(first + p)
            block = normed_ref[:, lanes]
            t = 0
            for ref, sums_ref, n in ((dm_ref, msum_ref, 3), (dh_ref, hsum_ref, 4)):
                part = dot(block, ref[...], TN).astype(BF16)
                for i in range(n):
                    cut = slice(i * 128, (i + 1) * 128)
                    put(p, t * TILE, part[:, cut])
                    sums = jnp.concatenate([sums_ref[:, cut], zero], axis=0).astype(BF16)
                    put(p, t * TILE + BLK, sums)
                    t += 1
            part = dot(turned[...], g_ref[:, lanes], NN).astype(BF16)
            sums = jnp.concatenate([gsum_ref[...], zero], axis=0).astype(BF16)
            for i in range(2):
                at = 7 * TILE + i * TILE_TWO
                put(p, at, part[:, i * 128 : (i + 1) * 128])
                put(p, at + ACT, sums)
            put(p, GRAD_ROWS - SPARE, jnp.zeros((SPARE, 128), BF16))


def grads_call(*args, after):
    scratch = [pltpu.VMEM((ACT, TOK), BF16)]
    return call("grads", grads_kernel, [vmem()] * 9, [shape((4, GRAD_ROWS, 128), BF16)] + [shape((4, GRAD_ROWS // 4, 128), BF16)] * 4, args, scratch, after)


def fold_part(blocks, out_ref, back_ref, got, keep_out, keep_back, send):
    half = blocks // 2
    for i in range(blocks):
        for back, (ref, rows, keep) in enumerate(((out_ref, HALF, keep_out), (back_ref, HALF + PAD, keep_back))):
            if len(got) == 2:
                new = got[back][i]
            else:
                base = back * blocks * HALF + i * rows
                new = got[0][base : base + rows, :]
            total = ref[i].astype(F32) + new.astype(F32)
            if i < half:
                keep[i] = total
            else:
                at = back * half * HALF + (i - half) * rows
                send[at : at + rows, :] = total.astype(BF16)


def fold_call(blocks, a, b, *extra, after=()):
    half, n = blocks // 2, len(a)

    def kernel(*refs):
        ins, outs = refs[: 2 * n], refs[2 * n + len(extra) :]
        for h in range(2):
            mine = ins[h * n : (h + 1) * n]
            fold_part(blocks, mine[0], mine[1], mine[2:], *outs[3 * h : 3 * h + 3])
        for ref, out in zip(refs[2 * n :], outs[6:]):
            out[...] = ref[...]

    outs = [
        shape((half, HALF, 128), F32),
        shape((half, HALF + PAD, 128), F32),
        shape((half * (2 * HALF + PAD), 128), BF16),
    ] * 2 + [shape(e.shape, e.dtype) for e in extra]
    got = call("fold", kernel, [vmem()] * (2 * n + len(extra)), outs, (*a, *b, *extra), after=after)
    return got[0:3], got[3:6], got[6:]


def finish_kernel(oa, ba, ga, ob, bb, gb, x_ref, g_ref, cen_ref, inv_ref, small_ref, out_ref, grad_ref):
    gain = small_ref[0:1, :].astype(F32)
    shift = small_ref[2:3, :].astype(F32) + small_ref[3:4, :].astype(F32)
    for half, (o_ref, b_ref, got) in enumerate(((oa, ba, ga), (ob, bb, gb))):
        sums = b_ref[0, HALF : HALF + PAD, :] + got[2 * HALF : 2 * HALF + PAD, :].astype(F32)
        sums = jnp.transpose(sums) * (1.0 / D)
        for i in range(HALF // 128):
            here = slice(i * 128, (i + 1) * 128)
            there = slice(HALF + i * 128, HALF + (i + 1) * 128)
            rows = slice(half * HALF + i * 128, half * HALF + (i + 1) * 128)
            branch = o_ref[0, here, :] + got[here, :].astype(F32)
            out_ref[rows, :] = (x_ref[rows, :].astype(F32) + branch + shift).astype(BF16)
            d = b_ref[0, here, :] + got[there, :].astype(F32)
            cen = cen_ref[rows, :]
            m1 = sums[:, 2 * i : 2 * i + 1]
            m2 = sums[:, 2 * i + 1 : 2 * i + 2]
            grad_ref[rows, :] = g_ref[rows, :].astype(F32) + inv_ref[rows, :] * (d * gain - m1 - cen * m2)


def finish_call(*args):
    outs = [shape((TOK, 128), BF16), shape((TOK, 128), F32)]
    return call("finish", finish_kernel, [vmem()] * 11, outs, args, final=True)


def norm_sums_kernel(ba, ga, bb, gb, cen_ref, sum_ref):
    gain = jnp.zeros((1, 128), F32)
    shift = jnp.zeros((1, 128), F32)
    for half, (b_ref, got) in enumerate(((ba, ga), (bb, gb))):
        d = b_ref[0, 0:HALF, :] + got[HALF : 2 * HALF, :].astype(F32)
        gain = gain + jnp.sum(d * cen_ref[half * HALF : (half + 1) * HALF, :], axis=0, keepdims=True)
        shift = shift + jnp.sum(d, axis=0, keepdims=True)
    sum_ref[...] = jnp.concatenate([gain, shift, jnp.zeros((6, 128), F32)], axis=0)


def norm_sums_call(*args, after):
    return call("norm_sums", norm_sums_kernel, [vmem()] * 5, [shape((8, 128), F32)], args, after=after)[0]


def fold_core_call(kept, *got):
    n = GRAD_ROWS // len(got)

    def kernel(kept_ref, *refs):
        ins, keep_ref, sends = refs[0 : len(got)], refs[len(got)], refs[len(got) + 1 :]
        for m, ref in enumerate(ins):
            rows = slice(m * n, (m + 1) * n)
            for i in range(2):
                keep_ref[i, rows, :] = kept_ref[i, rows, :].astype(F32) + ref[i].astype(F32)
                sends[1 - i][0, rows, :] = (kept_ref[2 + i, rows, :].astype(F32) + ref[2 + i].astype(F32)).astype(BF16)

    outs = [shape((2, GRAD_ROWS, 128), F32)] + [shape((1, GRAD_ROWS, 128), BF16)] * 2
    return call("fold_core", kernel, [vmem()] * (1 + len(got)), outs, (kept, *got))


def fold_row_call(kept, got, after):
    def kernel(kept_ref, got_ref, send_ref):
        send_ref[0] = (kept_ref[1] + got_ref[0].astype(F32)).astype(BF16)

    return call("fold_row", kernel, [vmem()] * 2, [shape((1, GRAD_ROWS, 128), BF16)], (kept, got), after=after)[0]


def lanes_of(v, row, width):
    total = 8 * width
    return pltpu.roll(v, lax.rem(total - row * width, total), 1)[:, 0:width]


def close_kernel(kept_ref, near_ref, far_ref, qkv_ref, qb_ref, up_ref, ub_ref, out_ref, down_ref, bias_ref, again_ref):
    def total(first, n):
        rows = slice(first, first + n)
        return kept_ref[0, rows, :] + near_ref[0, rows, :].astype(F32) + far_ref[0, rows, :].astype(F32)

    row = lax.axis_index("row")
    for s in range(3):
        qkv_ref[s] = total(s * TILE, BLK)
        qb_ref[s : s + 1, :] = lanes_of(total(s * TILE + BLK, PAD)[0:8], row, 16)[0:1]
    for i in range(4):
        up_ref[:, i * 128 : (i + 1) * 128] = total((3 + i) * TILE, BLK)
    bias = jnp.concatenate([total((3 + i) * TILE + BLK, PAD)[0:8] for i in range(4)], axis=1)
    ub_ref[...] = lanes_of(bias, row, 64)[0:1]
    for i in range(2):
        at = 7 * TILE + i * TILE_TWO
        out_ref[:, i * 128 : (i + 1) * 128] = total(at, 128)
        down_ref[:, i * 128 : (i + 1) * 128] = total(at + 128, FFL)
    bias = lanes_of(total(7 * TILE + ACT, PAD)[0:8], row, 16)[0:1]
    bias_ref[...] = bias
    again_ref[...] = bias


def close_call(*args):
    outs = [
        shape((3, BLK, 128), F32),
        shape((3, 16), F32),
        shape((BLK, FFL), F32),
        shape((1, 64), F32),
        shape((128, BLK), F32),
        shape((FFL, BLK), F32),
        shape((1, 16), F32),
        shape((1, 16), F32),
    ]
    return call("close", close_kernel, [vmem()] * 3, outs, args, final=True)


def close_norm_kernel(*refs):
    total = refs[0][...]
    for ref in refs[1:4]:
        total = total + ref[...]
    mine = lanes_of(total, lax.axis_index("row"), 16)
    refs[4][...] = mine[0:1]
    refs[5][...] = mine[1:2]


def close_norm_call(*args, after):
    return call("close_norm", close_norm_kernel, [vmem()] * 4, [shape((1, 16), F32)] * 2, args, after=after, final=True)


def join(*groups, after=()):
    groups = [[p if isinstance(p, tuple) else (p, 0, p.shape[0]) for p in group] for group in groups]
    flat = [p for group in groups for p in group]

    def kernel(*refs):
        ins, outs = refs[: len(flat)], refs[len(flat) :]
        n = 0
        for group, out in zip(groups, outs):
            at = 0
            for _, lo, hi in group:
                out[at : at + hi - lo] = ins[n][lo:hi]
                at += hi - lo
                n += 1

    outs = []
    for group in groups:
        first = group[0][0]
        outs.append(shape((sum(hi - lo for _, lo, hi in group),) + first.shape[1:], first.dtype))
    return call("join", kernel, [vmem()] * len(flat), outs, [p[0] for p in flat], after=after)


def fetch(copies):
    for copy in copies:
        copy.start()
    for copy in copies:
        copy.wait()


def in_hbm(*arrays):
    return [pltpu.with_memory_space_constraint(a, pltpu.HBM) for a in arrays]


def begin_kernel(x_ref, g_ref, a_ref, b_ref, sem):
    copies = []
    for half, out in enumerate((a_ref, b_ref)):
        for i, ref in enumerate((x_ref, g_ref)):
            copies.append(pltpu.make_async_copy(ref.at[pl.ds(half * HALF, HALF)], out.at[i], sem.at[half * 2 + i]))
    fetch(copies)


def begin_call(*args, after):
    scratch = [pltpu.SemaphoreType.DMA((4,))]
    specs = [pl.BlockSpec(memory_space=pltpu.HBM)] * 2
    return call("begin", begin_kernel, specs, [shape((2, HALF, 128), BF16)] * 2, in_hbm(*args), scratch, after)


def pack_kernel(qkv_ref, up_ref, out_ref, down_ref, packed, out_here, down_here, sem):
    copies = [
        pltpu.make_async_copy(qkv_ref.at[s], packed.at[0, :, pl.ds(s * 128, 128)], sem.at[s]) for s in range(3)
    ]
    copies.append(pltpu.make_async_copy(up_ref, packed.at[0, :, pl.ds(QKV, FFL)], sem.at[3]))
    copies.append(pltpu.make_async_copy(out_ref, out_here, sem.at[4]))
    copies.append(pltpu.make_async_copy(down_ref, down_here, sem.at[5]))
    fetch(copies)
    packed[0, :, CAT : CAT + 128] = jnp.transpose(out_here[...])
    packed[0, :, CAT + 128 : ALL] = jnp.transpose(down_here[...])


def pack_call(*args, after):
    outs = [shape((1, BLK, ALL), BF16)]
    scratch = [pltpu.VMEM((128, BLK), BF16), pltpu.VMEM((FFL, BLK), BF16), pltpu.SemaphoreType.DMA((6,))]
    specs = [pl.BlockSpec(memory_space=pltpu.HBM)] * 4
    return call("pack", pack_kernel, specs, outs, in_hbm(*args), scratch, after)[0]


def unpack_kernel(mine, got, cats, twos):
    for i, ref in enumerate((mine, got)):
        cats[i] = ref[0, :, 0:CAT]
        twos[i] = ref[0, :, CAT:ALL]


def unpack_call(*args):
    outs = [shape((2, BLK, CAT), BF16), shape((2, BLK, ACT), BF16)]
    return call("unpack", unpack_kernel, [vmem()] * 2, outs, args)


def both(mine, got):
    n = mine.shape[0] // 2
    return [(mine, 0, n), (got, 0, n), (mine, n, 2 * n), (got, n, 2 * n)]


def rotary_tables(long_start):
    places = jnp.arange(TOK, dtype=jnp.int32)
    begin_second = jnp.where(long_start == 0, 768, 256)
    positions = jnp.where(places >= begin_second, places - begin_second, places)
    lane = jnp.arange(128, dtype=jnp.int32)
    spot = lane % HEAD_DIM
    half = ROT // 2
    inverse = 10000.0 ** (-2.0 * (spot % half).astype(F32) / ROT)
    angles = positions.astype(F32)[:, None] * inverse[None, :]
    turned = (spot < ROT)[None, :]
    cos = jnp.where(turned, jnp.cos(angles), 1.0)
    sine = jnp.sin(angles)
    low = jnp.where((spot < half)[None, :], -sine, 0.0)
    high = jnp.where(((spot >= half) & (spot < ROT))[None, :], sine, 0.0)
    return cos, low, high


def shards(x, lengths, w_qkv, b_qkv, w_out, b_out, w_up, b_up, w_down, b_down, gain, shift, g):
    row = lax.axis_index("row")
    cos, sa, sb = rotary_tables(jnp.where(lengths[0, 0] > lengths[0, 1], 0, 256))

    def spread(v, width):
        wide = jnp.zeros(v.shape[:-1] + (8, width), BF16)
        return lax.dynamic_update_slice_in_dim(wide, v[..., None, :], row, v.ndim - 1).reshape(-1, 128)

    small = [spread(jnp.stack([gain, shift, b_out, b_down]), 16), spread(b_qkv, 16), spread(b_up, 64)]
    small = jnp.concatenate(small + [jnp.zeros((PAD - 11, 128), BF16)])
    small = small + exchange(small, "c")
    weights = pack_call(w_qkv.transpose(1, 0, 2), w_up, w_out, w_down, after=())
    weights_got = exchange(weights, "z", 0)
    a, b = begin_call(x, g, after=(weights,))
    a_got, b_got = exchange(a, "x", 0), exchange(b, "y", 0)
    small = small + exchange(small, "z", 1)
    small, a, b = join([small], both(a, a_got), both(b, b_got), after=(weights_got,))
    a_got, b_got = exchange(a, "x", 1), exchange(b, "y", 1)
    cats, twos = unpack_call(weights, weights_got)
    cats_got = exchange(cats, "z", 1)
    cats = (cats, cats_got, exchange(cats, "c"), exchange(cats_got, "c"))
    small = small + exchange(small, "z", 0)
    tiny, twos, a, b = join([small[None]], [twos], both(a, a_got), both(b, b_got))
    tiny_got = exchange(tiny, "x", 1)
    a_got, b_got = exchange(a, "y", 0), exchange(b, "x", 0)
    twos_got = exchange(twos, "z", 1)
    twos = (twos, twos_got, exchange(twos, "c"), exchange(twos_got, "c"))
    (tiny,) = join([tiny, tiny_got], after=(cats_got,))
    tiny_got = exchange(tiny, "y", 1)
    first = lambda v, got: [(v, 0, 4), (got, 0, 4)]
    last = lambda v, got: [(v, 4, 8), (got, 4, 8)]
    tiny, xa, xb, ga, gb = join(
        [tiny, tiny_got],
        first(a, a_got),
        first(b, b_got),
        last(a, a_got),
        last(b, b_got),
        after=(twos_got, cos, sa, sb),
    )
    tiny_got = exchange(tiny, "x", 0)
    xa, xb = (xa, exchange(xa, "y", 1)), (xb, exchange(xb, "x", 1))
    (tiny,) = join([tiny, tiny_got])
    tiny = (tiny, exchange(tiny, "y", 0))
    ga, gb = (ga, exchange(ga, "y", 1)), (gb, exchange(gb, "x", 1))

    normed, qkv, pre, act, centered, inv, gains = norm_call(xa, xb, tiny, cats, cos, sa, sb)
    att, exact, lse = attend_call(lengths, qkv)
    out_a, send_a, out_b, send_b = project_call(att, act, twos)
    out_a_got, out_b_got = exchange(send_a, "y", 0), exchange(send_b, "x", 0)
    g_all, d_hid, d_att, hsum, gsum = upstream_call(ga, gb, twos, pre, (out_a,))
    d_mix, msum = attend_back_call(lengths, qkv, d_att, exact, lse, cos, sa, sb)
    back_a, send_a, back_b, send_b = downstream_call(d_mix, d_hid, normed, gains, cats, ())
    back_a_got, back_b_got = exchange(send_a, "y", 0), exchange(send_b, "x", 0)
    keep, *sends = grads_call(normed, d_mix, d_hid, msum, hsum, att, act, g_all, gsum, after=(back_a, out_a_got, out_b_got))
    got = [exchange(send, "c") for send in sends]
    a, b, _ = fold_call(8, (out_a, back_a, out_a_got, back_a_got), (out_b, back_b, out_b_got, back_b_got))
    a_got, b_got = exchange(a[2], "y", 1), exchange(b[2], "x", 1)
    keep, *sends = fold_core_call(keep, *got)
    first, last = [exchange(send, "z", 0) for send in sends]
    send = fold_row_call(keep, first, ())
    got = exchange(send, "z", 1)
    a, b, _ = fold_call(4, (a[0], a[1], a_got), (b[0], b[1], b_got), after=(send,))
    a_got, b_got = exchange(a[2], "x", 0), exchange(b[2], "y", 0)
    a, b, _ = fold_call(2, (a[0], a[1], a_got), (b[0], b[1], b_got))
    a_got, b_got = exchange(a[2], "x", 1), exchange(b[2], "y", 1)
    sums = norm_sums_call(a[1], a_got, b[1], b_got, centered, after=(last,))
    sums = sums + exchange(sums, "c")
    block_out, input_grad = finish_call(a[0], a[1], a_got, b[0], b[1], b_got, x, g, centered, inv, small)
    qkv_grad, qkv_bias, up_grad, up_bias, out_grad, down_grad, out_bias, down_bias = close_call(keep, last, got)
    gain_grad, shift_grad = close_norm_call(
        sums, *(exchange(sums, "z", n) for n in range(3)), after=in_hbm(up_grad, input_grad)
    )
    return (
        block_out,
        input_grad,
        qkv_grad.transpose(1, 0, 2),
        qkv_bias,
        out_grad,
        out_bias.reshape(16),
        up_grad,
        up_bias.reshape(64),
        down_grad,
        down_bias.reshape(16),
        gain_grad.reshape(16),
        shift_grad.reshape(16),
    )


def solution(mesh):
    both = P(("col", "row"))
    in_specs = (
        P("row", "col"),
        P("row", None),
        P("row", None, "col"),
        P(None, ("col", "row")),
        P("col", "row"),
        both,
        P("row", "col"),
        both,
        P("col", "row"),
        both,
        both,
        both,
        P("row", "col"),
    )
    out_specs = (
        P("row", "col"),
        P("row", "col"),
        P("row", None, "col"),
        P(None, ("col", "row")),
        P("col", "row"),
        both,
        P("row", "col"),
        both,
        P("col", "row"),
        both,
        both,
        both,
    )
    return jax.shard_map(shards, mesh=mesh, in_specs=in_specs, out_specs=out_specs, check_vma=False)
```

```python
import functools

import jax
import jax.numpy as jnp
from jax import lax
from jax.experimental import pallas as pl
from jax.experimental.pallas import tpu as pltpu
from jax.sharding import PartitionSpec as P

D = 2048
HEAD_DIM = 64
ROT = 32
EPS = 1e-05
TOK = 1024
HALF = 512
QKV = 384
FFL = 512
CAT = QKV + FFL
ACT = 128 + FFL
ALL = CAT + ACT
PAD = 16
BLK = 256
ROWS = 512
F32 = jnp.float32
BF16 = jnp.bfloat16
MIB = 2**20

MASKS = ((1, 3, 2), (3, 1, 2))


def exchange(value, axis, step=0):
    pairs = []
    for z in range(4):
        for k in range(2):
            m = MASKS[k][step]
            for y in range(4):
                for x in range(4):
                    to = {
                        "x": (x ^ m, y, z, k),
                        "y": (x, y ^ m, z, k),
                        "z": (x, y, z ^ m, k),
                        "c": (x, y, z, 1 - k),
                    }[axis]
                    pairs.append(((z * 2 + k) * 16 + y * 4 + x, (to[2] * 2 + to[3]) * 16 + to[1] * 4 + to[0]))
    return lax.ppermute(value, ("row", "col"), pairs)


PIECE_OF = [(i // 8, i % 8) for i in range(16)]
NN = ((1,), (0,))
NT = ((1,), (1,))
TN = ((0,), (0,))


def dot(a, b, dims):
    return lax.dot_general(a, b, (dims, ((), ())), preferred_element_type=F32)


def weight_blocks(refs):
    first = 0
    for ref in refs:
        yield first, ref.shape[0], ref
        first += ref.shape[0]


def weight_of(refs, j):
    for first, n, ref in weight_blocks(refs):
        if first <= j < first + n:
            return ref.at[j - first]


def gelu_tanh_part(v):
    return jnp.tanh(0.7978845608028654 * (v + 0.044715 * v * v * v))


class Place:
    def __init__(self):
        row, col = lax.axis_index("row"), lax.axis_index("col")
        self.row = row
        self.z, self.core, self.y, self.x = lax.div(row, 2), lax.rem(row, 2), lax.div(col, 4), lax.rem(col, 4)
        self.m1 = jnp.where(self.core == 0, 1, 3)
        self.m2 = 4 - self.m1
        self.seen = (0, self.m1, self.m2, 2)

    def swapped(self, mask):
        return jnp.where(mask == self.m2, 1, jnp.where(mask == self.m1, 2, jnp.where(mask == 2, 3, 0)))

    def lane(self, half, i):
        outer, inner = self.seen[i // 4], self.seen[i % 4]
        y, x = (self.y ^ outer, self.x ^ inner) if half == 0 else (self.y ^ inner, self.x ^ outer)
        owner = y * 2 + lax.div(x, 2)
        mask = lax.div(owner, 2) ^ self.z
        same = lax.rem(owner, 2) == self.core
        first = jnp.where(mask == self.m1, 1, jnp.where(mask == self.m2, 2, jnp.where(mask == 2, 3, 0)))
        block = jnp.where(same, first, 4 + self.swapped(mask))
        return pl.multiple_of((block * 2 + lax.rem(x, 2)) * 128, 128)

    def spot(self, half, j, i):
        if j < 4:
            z, core = self.z ^ self.seen[j], self.core
        else:
            z, core = self.z ^ (0, self.m2, self.m1, 2)[j - 4], 1 - self.core
        owner = (z * 2 + core) * 2 + i
        y, x = self.swapped(lax.div(owner, 4) ^ self.y), self.swapped(lax.rem(owner, 4) ^ self.x)
        return y * 4 + x if half == 0 else x * 4 + y


def vmem():
    return pl.BlockSpec(memory_space=pltpu.VMEM)


def smem():
    return pl.BlockSpec(memory_space=pltpu.SMEM)


def any_spec():
    return pl.BlockSpec(memory_space=pl.ANY)


def shape(dims, dtype):
    return jax.ShapeDtypeStruct(dims, dtype)


WORK = dict(norm_proj=9, attend=3, project=5, upstream=6, attend_back=7, downstream=6, grads=11)
VMEM_MIB = dict(norm_proj=12, attend=8, project=9, upstream=11, attend_back=11, downstream=12, grads=8)


def call(name, kernel, specs, outs, args, scratch=(), after=(), final=False):
    if after:
        body, n = kernel, len(args)
        kernel = lambda *refs: body(*refs[:n], *refs[n + len(after) :])
        specs = list(specs) + [any_spec()] * len(after)
    return pl.pallas_call(
        kernel,
        in_specs=specs,
        out_specs=[vmem()] * len(outs),
        out_shape=outs if final else [pltpu.VMEM(o.shape, o.dtype) for o in outs],
        scratch_shapes=list(scratch),
        compiler_params=pltpu.CompilerParams(vmem_limit_bytes=VMEM_MIB.get(name, 3) * MIB),
        cost_estimate=pl.CostEstimate(flops=int(WORK.get(name, 0) * 2.5e8), bytes_accessed=0, transcendentals=0),
        name=name,
    )(*args, *after)


def norm_kernel(*refs):
    place = Place()
    halves, tiny, wts = (refs[0:2], refs[2:4]), refs[4:6], refs[6:10]
    cos_ref, sa_ref, sb_ref = refs[10:13]
    normed_ref, qkv_ref, pre_ref, act_ref, cen_ref, inv_ref, gb_ref = refs[13:]

    lanes = [[place.lane(half, i) for i in range(16)] for half in range(2)]

    def lane(half, i):
        return lanes[half][i]

    def tiny_of(i):
        return PIECE_OF[(0, 8, 2, 10)[i // 4] + (0, 4, 1, 5)[i % 4]]

    def tiny_row(i, row):
        a, k = tiny_of(i)
        return tiny[a][k, row : row + 1, :].astype(F32)

    for i in range(16):
        a, k = tiny_of(i)
        gb_ref[:, pl.ds(lane(0, i), 128)] = tiny[a][k].astype(F32)[0:8]
    bias = jnp.concatenate([tiny_row(0, 4 + i) for i in range(7)], axis=1)

    for half in range(2):
        pieces = halves[half]

        def chunk(t, _, half=half, pieces=pieces):
            here = pl.ds(pl.multiple_of(t * 16, 16), 16)
            rows = pl.ds(pl.multiple_of(half * HALF + t * 16, 16), 16)
            xs = [pieces[a][k, here, :].astype(F32) for a, k in PIECE_OF]
            total = xs[0]
            square = xs[0] * xs[0]
            for x in xs[1:]:
                total = total + x
                square = square + x * x
            mean = jnp.sum(total, axis=1, keepdims=True) * (1.0 / D)
            square = jnp.sum(square, axis=1, keepdims=True) * (1.0 / D)
            inv = lax.rsqrt(square - mean * mean + EPS)
            for i, x in enumerate(xs):
                j = i if half == 0 else (i % 4) * 4 + i // 4
                centered = (x - mean) * inv
                if i == 0:
                    cen_ref[rows, :] = centered
                normed_ref[rows, pl.ds(lane(half, i), 128)] = (centered * tiny_row(j, 0) + tiny_row(j, 1)).astype(BF16)
            inv_ref[rows, :] = jnp.broadcast_to(inv, (16, 128))
            return _

        lax.fori_loop(0, HALF // 16, chunk, 0, unroll=8)

    @pl.loop(0, TOK // ROWS)
    def _(t):
        rows = pl.ds(pl.multiple_of(t * ROWS, ROWS), ROWS)
        mixed = bias
        for first, n, ref in weight_blocks(wts):
            lines = slice(first * BLK, (first + n) * BLK)
            mixed = mixed + dot(normed_ref[rows, lines], ref[...].reshape(n * BLK, CAT), NN)
        for s in range(2):
            v = mixed[:, s * 128 : (s + 1) * 128]
            v = v * cos_ref[rows, :] + pltpu.roll(v, 128 - 16, 1) * sa_ref[rows, :] + pltpu.roll(v, 16, 1) * sb_ref[rows, :]
            qkv_ref[rows, s * 128 : (s + 1) * 128] = v.astype(BF16)
        qkv_ref[rows, 256:384] = mixed[:, 256:384].astype(BF16)
        pre = mixed[:, QKV:CAT]
        pre_ref[rows, :] = pre
        act_ref[rows, :] = (0.5 * pre * (1.0 + gelu_tanh_part(pre))).astype(BF16)


def norm_call(xa, xb, tiny, wts, cos, sa, sb):
    outs = [
        shape((TOK, D), BF16),
        shape((TOK, QKV), BF16),
        shape((TOK, FFL), F32),
        shape((TOK, FFL), BF16),
        shape((TOK, 128), F32),
        shape((TOK, 128), F32),
        shape((8, D), F32),
    ]
    args = (*xa, *xb, *tiny, *wts, cos, sa, sb)
    return call("norm_proj", norm_kernel, [vmem()] * 13, outs, args)


def head_masks():
    lane = lax.broadcasted_iota(jnp.int32, (1, 128), 1)
    return [(lane < HEAD_DIM).astype(BF16), (lane >= HEAD_DIM).astype(BF16)]


def masked_scores(qh, k, qi):
    s = dot(qh, k, NT)
    row = lax.broadcasted_iota(jnp.int32, (BLK, BLK), 0)
    column = lax.broadcasted_iota(jnp.int32, (BLK, BLK), 1)
    last = jnp.where(row >= column, s[:, qi * BLK :], -1e30)
    return last if qi == 0 else jnp.concatenate([s[:, : qi * BLK], last], axis=1)


def for_blocks(lengths, body):
    long_first = lengths[0, 0] > lengths[0, 1]
    long_start, short_start = jnp.where(long_first, 0, 256), jnp.where(long_first, 768, 0)

    @pl.loop(0, 2)
    def _(document):
        body(jnp.where(document == 0, long_start, short_start), 0)

    for qi in (1, 2):
        body(long_start, qi)


def attend_kernel(tab, qkv_ref, out_ref, exact_ref, lse_ref):
    masks = head_masks()
    low_lanes = lax.broadcasted_iota(jnp.int32, (BLK, 128), 1) < HEAD_DIM

    def body(start, qi):
        rows = pl.ds(pl.multiple_of(start + qi * BLK, BLK), BLK)
        keys = pl.ds(pl.multiple_of(start, BLK), (qi + 1) * BLK)
        q = qkv_ref[rows, 0:128] * jnp.asarray(0.125, BF16)
        k = qkv_ref[keys, 128:256]
        v = qkv_ref[keys, 256:384]
        total = None
        logs = []
        for m in masks:
            s = masked_scores(q * m, k, qi)
            most = jnp.max(s, axis=1, keepdims=True)
            e = jnp.exp(s - most)
            count = jnp.sum(e, axis=1, keepdims=True)
            p = (e * (1.0 / count)).astype(BF16)
            o = dot(p, v * m, NN)
            total = o if total is None else total + o
            logs.append(most + jnp.log(count))
        out_ref[rows, :] = total.astype(BF16)
        exact_ref[rows, :] = total
        lse_ref[rows, :] = jnp.where(low_lanes, logs[0], logs[1])

    for_blocks(tab, body)


def attend_call(tab, qkv):
    outs = [shape((TOK, 128), BF16), shape((TOK, 128), F32), shape((TOK, 128), F32)]
    return call("attend", attend_kernel, [smem(), vmem()], outs, (tab, qkv))


def attend_back_kernel(
    tab, qkv_ref, do_ref, exact_ref, lse_ref, cos_ref, sa_ref, sb_ref, out_ref, sum_ref, dq, dk, dv
):
    masks = head_masks()
    dk[...] = jnp.zeros_like(dk)
    dv[...] = jnp.zeros_like(dv)
    eighth = jnp.asarray(0.125, BF16)
    causal = lax.broadcasted_iota(jnp.int32, (BLK, BLK), 0) >= lax.broadcasted_iota(jnp.int32, (BLK, BLK), 1)

    def body(start, qi):
        rows = pl.ds(pl.multiple_of(start + qi * BLK, BLK), BLK)
        q = qkv_ref[rows, 0:128]
        do = do_ref[rows, :]
        weighted = do.astype(F32) * exact_ref[rows, :] * 0.125
        lse = lse_ref[rows, :]
        deltas = [jnp.sum(weighted * m.astype(F32), axis=1, keepdims=True) for m in masks]
        logs = [lse[:, 0:1], lse[:, HEAD_DIM : HEAD_DIM + 1]]
        qs = [q * m for m in masks]
        dos = [do * m for m in masks]
        q_both = jnp.concatenate(qs, axis=0)
        do_both = jnp.concatenate(dos, axis=0)
        total = None
        for kj in range(qi + 1):
            keys = pl.ds(pl.multiple_of(start + kj * BLK, BLK), BLK)
            k = qkv_ref[keys, 128:256]
            v = qkv_ref[keys, 256:384]
            ps, dss = [], []
            for h in range(2):
                s = dot(qs[h] * eighth, k, NT)
                if kj == qi:
                    s = jnp.where(causal, s, -1e30)
                p = jnp.exp(s - logs[h])
                dp = dot(dos[h] * eighth, v, NT)
                dss.append((p * (dp - deltas[h])).astype(BF16))
                ps.append(p.astype(BF16))
            part = dot(jnp.concatenate(dss, axis=1), jnp.concatenate([k * m for m in masks], axis=0), NN)
            total = part if total is None else total + part
            dk[keys, :] += dot(jnp.concatenate(dss, axis=0), q_both, TN)
            dv[keys, :] += dot(jnp.concatenate(ps, axis=0), do_both, TN)
        dq[rows, :] = total

    for_blocks(tab, body)
    for s, ref in enumerate((dq, dk, dv)):
        d = ref[...]
        if s < 2:
            d = d * cos_ref[...] - pltpu.roll(d, 128 - 16, 1) * sa_ref[...] - pltpu.roll(d, 16, 1) * sb_ref[...]
        low = d.astype(BF16)
        out_ref[:, s * 128 : (s + 1) * 128] = low
        sum_ref[:, s * 128 : (s + 1) * 128] = jnp.broadcast_to(jnp.sum(low.astype(F32), axis=0, keepdims=True), (8, 128))


def attend_back_call(*args):
    outs = [shape((TOK, QKV), BF16), shape((8, QKV), F32)]
    scratch = [pltpu.VMEM((TOK, 128), F32)] * 3
    return call("attend_back", attend_back_kernel, [smem()] + [vmem()] * 7, outs, args, scratch)


def project_kernel(att_ref, act_ref, *refs):
    wts, outs, whole = refs[0:4], refs[4:8], refs[8]
    place = Place()
    for half in range(2):
        spots = [[place.spot(half, j, i) for i in range(2)] for j in range(8)]

        rows = slice(half * HALF, (half + 1) * HALF)
        both = jnp.concatenate([att_ref[rows, :], act_ref[rows, :]], axis=1)
        for j in range(8):
            part = dot(both, weight_of(wts, j)[...], NT).astype(BF16)
            for i in range(2):
                whole[spots[j][i]] = part[:, i * 128 : (i + 1) * 128]

        outs[2 * half][...] = whole[0:8]
        outs[2 * half + 1][...] = whole[8:16]


def project_call(att, act, wts):
    outs = [shape((8, HALF, 128), BF16)] * 4
    scratch = [pltpu.VMEM((16, HALF, 128), BF16)]
    return call("project", project_kernel, [vmem()] * 6, outs, (att, act, *wts), scratch)


def upstream_kernel(*refs):
    place = Place()
    halves, wts, pre_ref = (refs[0:2], refs[2:4]), refs[4:8], refs[8]
    g_ref, hid_ref, att_ref, hsum_ref, gsum_ref = refs[9:14]
    mine = jnp.zeros((1, 128), F32)
    for half in range(2):
        for i, (a, k) in enumerate(PIECE_OF):
            g_ref[half * HALF : (half + 1) * HALF, pl.ds(place.lane(half, i), 128)] = halves[half][a][k]
        mine = mine + jnp.sum(halves[half][0][0].astype(F32), axis=0, keepdims=True)
    gsum_ref[...] = jnp.broadcast_to(mine, (8, 128))
    hsum_ref[...] = jnp.zeros_like(hsum_ref)

    @pl.loop(0, TOK // ROWS)
    def _(t):
        rows = pl.ds(pl.multiple_of(t * ROWS, ROWS), ROWS)
        d_act = None
        for first, n, ref in weight_blocks(wts):
            lines = slice(first * BLK, (first + n) * BLK)
            part = dot(g_ref[rows, lines], ref[...].reshape(n * BLK, ACT), NN)
            d_act = part if d_act is None else d_act + part
        att_ref[rows, :] = d_act[:, 0:128].astype(BF16)
        v = pre_ref[rows, :]
        th = gelu_tanh_part(v)
        slope = 0.5 * (1.0 + th) + 0.5 * v * (1.0 - th * th) * (0.7978845608028654 * (1.0 + 3.0 * 0.044715 * v * v))
        low = (d_act[:, 128:ACT] * slope).astype(BF16)
        hid_ref[rows, :] = low
        hsum_ref[...] += jnp.broadcast_to(jnp.sum(low.astype(F32), axis=0, keepdims=True), (8, FFL))


def upstream_call(ga, gb, wts, pre, after):
    outs = [
        shape((TOK, D), BF16),
        shape((TOK, FFL), BF16),
        shape((TOK, 128), BF16),
        shape((8, FFL), F32),
        shape((8, 128), F32),
    ]
    args = (*ga, *gb, *wts, pre)
    return call("upstream", upstream_kernel, [vmem()] * 9, outs, args, after=after)


def downstream_kernel(dm_ref, dh_ref, normed_ref, gb_ref, *refs):
    wts, outs, whole, flat = refs[0:4], refs[4:8], refs[8], refs[9]
    place = Place()
    flat[...] = jnp.zeros_like(flat)
    for half in range(2):
        spots = [[place.spot(half, j, i) for i in range(2)] for j in range(8)]

        rows = slice(half * HALF, (half + 1) * HALF)
        both = jnp.concatenate([dm_ref[rows, :], dh_ref[rows, :]], axis=1)
        s1 = jnp.zeros((HALF, 128), F32)
        s2 = jnp.zeros((HALF, 128), F32)
        for j in range(8):
            lines = slice(j * BLK, (j + 1) * BLK)
            part = dot(both, weight_of(wts, j)[...], NT)
            low = part.astype(BF16)
            u1 = part * gb_ref[0:1, lines]
            u2 = part * (normed_ref[rows, lines].astype(F32) - gb_ref[1:2, lines])
            for i in range(2):
                cut = slice(i * 128, (i + 1) * 128)
                whole[spots[j][i]] = low[:, cut]
                s1 = s1 + u1[:, cut]
                s2 = s2 + u2[:, cut]
        for i in range(HALF // 128):
            cut = slice(i * 128, (i + 1) * 128)
            flat[2 * i : 2 * i + 1, :] = jnp.sum(jnp.transpose(s1[cut, :]), axis=0, keepdims=True)
            flat[2 * i + 1 : 2 * i + 2, :] = jnp.sum(jnp.transpose(s2[cut, :]), axis=0, keepdims=True)

        low = flat[...].astype(BF16)
        for n, out in enumerate(outs[2 * half : 2 * half + 2]):
            out[:, 0:HALF, :] = whole[8 * n : 8 * n + 8]
            for c in range(8):
                out[c, HALF : HALF + PAD, :] = low


def downstream_call(dm, dh, normed, gb, wts, after):
    outs = [shape((8, HALF + PAD, 128), BF16)] * 4
    scratch = [pltpu.VMEM((16, HALF, 128), BF16), pltpu.VMEM((PAD, 128), F32)]
    args = (dm, dh, normed, gb, *wts)
    return call("downstream", downstream_kernel, [vmem()] * 8, outs, args, scratch, after)


def grad_lanes(p):
    place = lax.rem(p, 4)
    j = p + jnp.where(place == 1, 1, 0) - jnp.where(place == 2, 1, 0)
    return pl.ds(pl.multiple_of(j * BLK, BLK), BLK)


TILE = BLK + PAD
TILE_TWO = ACT + PAD
SPARE = 48
GRAD_ROWS = 7 * TILE + 2 * TILE_TWO + SPARE


def grads_kernel(normed_ref, dm_ref, dh_ref, msum_ref, hsum_ref, att_ref, act_ref, g_ref, gsum_ref, *refs):
    keep, sends, turned = refs[0], refs[1:5], refs[5]
    turned[0:128, :] = jnp.transpose(att_ref[...])
    turned[128:ACT, :] = jnp.transpose(act_ref[...])
    zero = jnp.zeros((8, 128), F32)
    for first in (4, 0):
        if first == 4:
            def put(p, row, value):
                n = value.shape[0]
                while n:
                    part, at = divmod(row, GRAD_ROWS // 4)
                    here = min(n, GRAD_ROWS // 4 - at)
                    sends[part][p, at : at + here, :] = value[:here]
                    value, row, n = value[here:], row + here, n - here
        else:
            def put(p, row, value):
                keep[p, row : row + value.shape[0], :] = value

        @pl.loop(0, 4)
        def _(p, first=first, put=put):
            lanes = grad_lanes(first + p)
            block = normed_ref[:, lanes]
            t = 0
            for ref, sums_ref, n in ((dm_ref, msum_ref, 3), (dh_ref, hsum_ref, 4)):
                part = dot(block, ref[...], TN).astype(BF16)
                for i in range(n):
                    cut = slice(i * 128, (i + 1) * 128)
                    put(p, t * TILE, part[:, cut])
                    sums = jnp.concatenate([sums_ref[:, cut], zero], axis=0).astype(BF16)
                    put(p, t * TILE + BLK, sums)
                    t += 1
            part = dot(turned[...], g_ref[:, lanes], NN).astype(BF16)
            sums = jnp.concatenate([gsum_ref[...], zero], axis=0).astype(BF16)
            for i in range(2):
                at = 7 * TILE + i * TILE_TWO
                put(p, at, part[:, i * 128 : (i + 1) * 128])
                put(p, at + ACT, sums)
            put(p, GRAD_ROWS - SPARE, jnp.zeros((SPARE, 128), BF16))


def grads_call(*args, after):
    scratch = [pltpu.VMEM((ACT, TOK), BF16)]
    return call("grads", grads_kernel, [vmem()] * 9, [shape((4, GRAD_ROWS, 128), BF16)] + [shape((4, GRAD_ROWS // 4, 128), BF16)] * 4, args, scratch, after)


def fold_part(blocks, out_ref, back_ref, got, keep_out, keep_back, send):
    half = blocks // 2
    for i in range(blocks):
        for back, (ref, rows, keep) in enumerate(((out_ref, HALF, keep_out), (back_ref, HALF + PAD, keep_back))):
            if len(got) == 2:
                new = got[back][i]
            else:
                base = back * blocks * HALF + i * rows
                new = got[0][base : base + rows, :]
            total = ref[i].astype(F32) + new.astype(F32)
            if i < half:
                keep[i] = total
            else:
                at = back * half * HALF + (i - half) * rows
                send[at : at + rows, :] = total.astype(BF16)


def fold_call(blocks, a, b, *extra, after=()):
    half, n = blocks // 2, len(a)

    def kernel(*refs):
        ins, outs = refs[: 2 * n], refs[2 * n + len(extra) :]
        for h in range(2):
            mine = ins[h * n : (h + 1) * n]
            fold_part(blocks, mine[0], mine[1], mine[2:], *outs[3 * h : 3 * h + 3])
        for ref, out in zip(refs[2 * n :], outs[6:]):
            out[...] = ref[...]

    outs = [
        shape((half, HALF, 128), F32),
        shape((half, HALF + PAD, 128), F32),
        shape((half * (2 * HALF + PAD), 128), BF16),
    ] * 2 + [shape(e.shape, e.dtype) for e in extra]
    got = call("fold", kernel, [vmem()] * (2 * n + len(extra)), outs, (*a, *b, *extra), after=after)
    return got[0:3], got[3:6], got[6:]


def finish_kernel(oa, ba, ga, ob, bb, gb, x_ref, g_ref, cen_ref, inv_ref, small_ref, out_ref, grad_ref):
    gain = small_ref[0:1, :].astype(F32)
    shift = small_ref[2:3, :].astype(F32) + small_ref[3:4, :].astype(F32)
    for half, (o_ref, b_ref, got) in enumerate(((oa, ba, ga), (ob, bb, gb))):
        sums = b_ref[0, HALF : HALF + PAD, :] + got[2 * HALF : 2 * HALF + PAD, :].astype(F32)
        sums = jnp.transpose(sums) * (1.0 / D)
        for i in range(HALF // 128):
            here = slice(i * 128, (i + 1) * 128)
            there = slice(HALF + i * 128, HALF + (i + 1) * 128)
            rows = slice(half * HALF + i * 128, half * HALF + (i + 1) * 128)
            branch = o_ref[0, here, :] + got[here, :].astype(F32)
            out_ref[rows, :] = (x_ref[rows, :].astype(F32) + branch + shift).astype(BF16)
            d = b_ref[0, here, :] + got[there, :].astype(F32)
            cen = cen_ref[rows, :]
            m1 = sums[:, 2 * i : 2 * i + 1]
            m2 = sums[:, 2 * i + 1 : 2 * i + 2]
            grad_ref[rows, :] = g_ref[rows, :].astype(F32) + inv_ref[rows, :] * (d * gain - m1 - cen * m2)


def finish_call(*args):
    outs = [shape((TOK, 128), BF16), shape((TOK, 128), F32)]
    return call("finish", finish_kernel, [vmem()] * 11, outs, args, final=True)


def norm_sums_kernel(ba, ga, bb, gb, cen_ref, sum_ref):
    gain = jnp.zeros((1, 128), F32)
    shift = jnp.zeros((1, 128), F32)
    for half, (b_ref, got) in enumerate(((ba, ga), (bb, gb))):
        d = b_ref[0, 0:HALF, :] + got[HALF : 2 * HALF, :].astype(F32)
        gain = gain + jnp.sum(d * cen_ref[half * HALF : (half + 1) * HALF, :], axis=0, keepdims=True)
        shift = shift + jnp.sum(d, axis=0, keepdims=True)
    sum_ref[...] = jnp.concatenate([gain, shift, jnp.zeros((6, 128), F32)], axis=0)


def norm_sums_call(*args, after):
    return call("norm_sums", norm_sums_kernel, [vmem()] * 5, [shape((8, 128), F32)], args, after=after)[0]


def fold_core_call(kept, *got):
    n = GRAD_ROWS // len(got)

    def kernel(kept_ref, *refs):
        ins, keep_ref, sends = refs[0 : len(got)], refs[len(got)], refs[len(got) + 1 :]
        for m, ref in enumerate(ins):
            rows = slice(m * n, (m + 1) * n)
            for i in range(2):
                keep_ref[i, rows, :] = kept_ref[i, rows, :].astype(F32) + ref[i].astype(F32)
                sends[1 - i][0, rows, :] = (kept_ref[2 + i, rows, :].astype(F32) + ref[2 + i].astype(F32)).astype(BF16)

    outs = [shape((2, GRAD_ROWS, 128), F32)] + [shape((1, GRAD_ROWS, 128), BF16)] * 2
    return call("fold_core", kernel, [vmem()] * (1 + len(got)), outs, (kept, *got))


def fold_row_call(kept, got, after):
    def kernel(kept_ref, got_ref, send_ref):
        send_ref[0] = (kept_ref[1] + got_ref[0].astype(F32)).astype(BF16)

    return call("fold_row", kernel, [vmem()] * 2, [shape((1, GRAD_ROWS, 128), BF16)], (kept, got), after=after)[0]


def lanes_of(v, row, width):
    total = 8 * width
    return pltpu.roll(v, lax.rem(total - row * width, total), 1)[:, 0:width]


def close_kernel(kept_ref, near_ref, far_ref, qkv_ref, qb_ref, up_ref, ub_ref, out_ref, down_ref, bias_ref, again_ref):
    def total(first, n):
        rows = slice(first, first + n)
        return kept_ref[0, rows, :] + near_ref[0, rows, :].astype(F32) + far_ref[0, rows, :].astype(F32)

    row = lax.axis_index("row")
    for s in range(3):
        qkv_ref[s] = total(s * TILE, BLK)
        qb_ref[s : s + 1, :] = lanes_of(total(s * TILE + BLK, PAD)[0:8], row, 16)[0:1]
    for i in range(4):
        up_ref[:, i * 128 : (i + 1) * 128] = total((3 + i) * TILE, BLK)
    bias = jnp.concatenate([total((3 + i) * TILE + BLK, PAD)[0:8] for i in range(4)], axis=1)
    ub_ref[...] = lanes_of(bias, row, 64)[0:1]
    for i in range(2):
        at = 7 * TILE + i * TILE_TWO
        out_ref[:, i * 128 : (i + 1) * 128] = total(at, 128)
        down_ref[:, i * 128 : (i + 1) * 128] = total(at + 128, FFL)
    bias = lanes_of(total(7 * TILE + ACT, PAD)[0:8], row, 16)[0:1]
    bias_ref[...] = bias
    again_ref[...] = bias


def close_call(*args):
    outs = [
        shape((3, BLK, 128), F32),
        shape((3, 16), F32),
        shape((BLK, FFL), F32),
        shape((1, 64), F32),
        shape((128, BLK), F32),
        shape((FFL, BLK), F32),
        shape((1, 16), F32),
        shape((1, 16), F32),
    ]
    return call("close", close_kernel, [vmem()] * 3, outs, args, final=True)


def close_norm_kernel(*refs):
    total = refs[0][...]
    for ref in refs[1:4]:
        total = total + ref[...]
    mine = lanes_of(total, lax.axis_index("row"), 16)
    refs[4][...] = mine[0:1]
    refs[5][...] = mine[1:2]


def close_norm_call(*args, after):
    return call("close_norm", close_norm_kernel, [vmem()] * 4, [shape((1, 16), F32)] * 2, args, after=after, final=True)


def join(*groups, after=()):
    groups = [[p if isinstance(p, tuple) else (p, 0, p.shape[0]) for p in group] for group in groups]
    flat = [p for group in groups for p in group]

    def kernel(*refs):
        ins, outs = refs[: len(flat)], refs[len(flat) :]
        n = 0
        for group, out in zip(groups, outs):
            at = 0
            for _, lo, hi in group:
                out[at : at + hi - lo] = ins[n][lo:hi]
                at += hi - lo
                n += 1

    outs = []
    for group in groups:
        first = group[0][0]
        outs.append(shape((sum(hi - lo for _, lo, hi in group),) + first.shape[1:], first.dtype))
    return call("join", kernel, [vmem()] * len(flat), outs, [p[0] for p in flat], after=after)


def fetch(copies):
    for copy in copies:
        copy.start()
    for copy in copies:
        copy.wait()


def in_hbm(*arrays):
    return [pltpu.with_memory_space_constraint(a, pltpu.HBM) for a in arrays]


def begin_kernel(x_ref, g_ref, a_ref, b_ref, sem):
    copies = []
    for half, out in enumerate((a_ref, b_ref)):
        for i, ref in enumerate((x_ref, g_ref)):
            copies.append(pltpu.make_async_copy(ref.at[pl.ds(half * HALF, HALF)], out.at[i], sem.at[half * 2 + i]))
    fetch(copies)


def begin_call(*args, after):
    scratch = [pltpu.SemaphoreType.DMA((4,))]
    specs = [pl.BlockSpec(memory_space=pltpu.HBM)] * 2
    return call("begin", begin_kernel, specs, [shape((2, HALF, 128), BF16)] * 2, in_hbm(*args), scratch, after)


def pack_kernel(qkv_ref, up_ref, out_ref, down_ref, packed, out_here, down_here, sem):
    copies = [
        pltpu.make_async_copy(qkv_ref.at[s], packed.at[0, :, pl.ds(s * 128, 128)], sem.at[s]) for s in range(3)
    ]
    copies.append(pltpu.make_async_copy(up_ref, packed.at[0, :, pl.ds(QKV, FFL)], sem.at[3]))
    copies.append(pltpu.make_async_copy(out_ref, out_here, sem.at[4]))
    copies.append(pltpu.make_async_copy(down_ref, down_here, sem.at[5]))
    fetch(copies)
    packed[0, :, CAT : CAT + 128] = jnp.transpose(out_here[...])
    packed[0, :, CAT + 128 : ALL] = jnp.transpose(down_here[...])


def pack_call(*args, after):
    outs = [shape((1, BLK, ALL), BF16)]
    scratch = [pltpu.VMEM((128, BLK), BF16), pltpu.VMEM((FFL, BLK), BF16), pltpu.SemaphoreType.DMA((6,))]
    specs = [pl.BlockSpec(memory_space=pltpu.HBM)] * 4
    return call("pack", pack_kernel, specs, outs, in_hbm(*args), scratch, after)[0]


def unpack_kernel(mine, got, cats, twos):
    for i, ref in enumerate((mine, got)):
        cats[i] = ref[0, :, 0:CAT]
        twos[i] = ref[0, :, CAT:ALL]


def unpack_call(*args):
    outs = [shape((2, BLK, CAT), BF16), shape((2, BLK, ACT), BF16)]
    return call("unpack", unpack_kernel, [vmem()] * 2, outs, args)


def both(mine, got):
    n = mine.shape[0] // 2
    return [(mine, 0, n), (got, 0, n), (mine, n, 2 * n), (got, n, 2 * n)]


def rotary_tables(long_start):
    places = jnp.arange(TOK, dtype=jnp.int32)
    begin_second = jnp.where(long_start == 0, 768, 256)
    positions = jnp.where(places >= begin_second, places - begin_second, places)
    lane = jnp.arange(128, dtype=jnp.int32)
    spot = lane % HEAD_DIM
    half = ROT // 2
    inverse = 10000.0 ** (-2.0 * (spot % half).astype(F32) / ROT)
    angles = positions.astype(F32)[:, None] * inverse[None, :]
    turned = (spot < ROT)[None, :]
    cos = jnp.where(turned, jnp.cos(angles), 1.0)
    sine = jnp.sin(angles)
    low = jnp.where((spot < half)[None, :], -sine, 0.0)
    high = jnp.where(((spot >= half) & (spot < ROT))[None, :], sine, 0.0)
    return cos, low, high


def shards(x, lengths, w_qkv, b_qkv, w_out, b_out, w_up, b_up, w_down, b_down, gain, shift, g):
    row = lax.axis_index("row")
    cos, sa, sb = rotary_tables(jnp.where(lengths[0, 0] > lengths[0, 1], 0, 256))

    def spread(v, width):
        wide = jnp.zeros(v.shape[:-1] + (8, width), BF16)
        return lax.dynamic_update_slice_in_dim(wide, v[..., None, :], row, v.ndim - 1).reshape(-1, 128)

    small = [spread(jnp.stack([gain, shift, b_out, b_down]), 16), spread(b_qkv, 16), spread(b_up, 64)]
    small = jnp.concatenate(small + [jnp.zeros((PAD - 11, 128), BF16)])
    small = small + exchange(small, "c")
    weights = pack_call(w_qkv.transpose(1, 0, 2), w_up, w_out, w_down, after=())
    weights_got = exchange(weights, "z", 0)
    a, b = begin_call(x, g, after=(weights,))
    a_got, b_got = exchange(a, "x", 0), exchange(b, "y", 0)
    small = small + exchange(small, "z", 1)
    small, a, b = join([small], both(a, a_got), both(b, b_got), after=(weights_got,))
    a_got, b_got = exchange(a, "x", 1), exchange(b, "y", 1)
    cats, twos = unpack_call(weights, weights_got)
    cats_got = exchange(cats, "z", 1)
    cats = (cats, cats_got, exchange(cats, "c"), exchange(cats_got, "c"))
    small = small + exchange(small, "z", 0)
    tiny, twos, a, b = join([small[None]], [twos], both(a, a_got), both(b, b_got))
    tiny_got = exchange(tiny, "x", 1)
    a_got, b_got = exchange(a, "y", 0), exchange(b, "x", 0)
    twos_got = exchange(twos, "z", 1)
    twos = (twos, twos_got, exchange(twos, "c"), exchange(twos_got, "c"))
    (tiny,) = join([tiny, tiny_got], after=(cats_got,))
    tiny_got = exchange(tiny, "y", 1)
    first = lambda v, got: [(v, 0, 4), (got, 0, 4)]
    last = lambda v, got: [(v, 4, 8), (got, 4, 8)]
    tiny, xa, xb, ga, gb = join(
        [tiny, tiny_got],
        first(a, a_got),
        first(b, b_got),
        last(a, a_got),
        last(b, b_got),
        after=(twos_got, cos, sa, sb),
    )
    tiny_got = exchange(tiny, "x", 0)
    xa, xb = (xa, exchange(xa, "y", 1)), (xb, exchange(xb, "x", 1))
    (tiny,) = join([tiny, tiny_got])
    tiny = (tiny, exchange(tiny, "y", 0))
    ga, gb = (ga, exchange(ga, "y", 1)), (gb, exchange(gb, "x", 1))

    normed, qkv, pre, act, centered, inv, gains = norm_call(xa, xb, tiny, cats, cos, sa, sb)
    att, exact, lse = attend_call(lengths, qkv)
    out_a, send_a, out_b, send_b = project_call(att, act, twos)
    out_a_got, out_b_got = exchange(send_a, "y", 0), exchange(send_b, "x", 0)
    g_all, d_hid, d_att, hsum, gsum = upstream_call(ga, gb, twos, pre, (out_a,))
    d_mix, msum = attend_back_call(lengths, qkv, d_att, exact, lse, cos, sa, sb)
    back_a, send_a, back_b, send_b = downstream_call(d_mix, d_hid, normed, gains, cats, ())
    back_a_got, back_b_got = exchange(send_a, "y", 0), exchange(send_b, "x", 0)
    keep, *sends = grads_call(normed, d_mix, d_hid, msum, hsum, att, act, g_all, gsum, after=(back_a, out_a_got, out_b_got))
    got = [exchange(send, "c") for send in sends]
    a, b, _ = fold_call(8, (out_a, back_a, out_a_got, back_a_got), (out_b, back_b, out_b_got, back_b_got))
    a_got, b_got = exchange(a[2], "y", 1), exchange(b[2], "x", 1)
    keep, *sends = fold_core_call(keep, *got)
    first, last = [exchange(send, "z", 0) for send in sends]
    send = fold_row_call(keep, first, ())
    got = exchange(send, "z", 1)
    a, b, _ = fold_call(4, (a[0], a[1], a_got), (b[0], b[1], b_got), after=(send,))
    a_got, b_got = exchange(a[2], "x", 0), exchange(b[2], "y", 0)
    a, b, _ = fold_call(2, (a[0], a[1], a_got), (b[0], b[1], b_got))
    a_got, b_got = exchange(a[2], "x", 1), exchange(b[2], "y", 1)
    sums = norm_sums_call(a[1], a_got, b[1], b_got, centered, after=(last,))
    sums = sums + exchange(sums, "c")
    block_out, input_grad = finish_call(a[0], a[1], a_got, b[0], b[1], b_got, x, g, centered, inv, small)
    qkv_grad, qkv_bias, up_grad, up_bias, out_grad, down_grad, out_bias, down_bias = close_call(keep, last, got)
    gain_grad, shift_grad = close_norm_call(
        sums, *(exchange(sums, "z", n) for n in range(3)), after=in_hbm(up_grad, input_grad)
    )
    return (
        block_out,
        input_grad,
        qkv_grad.transpose(1, 0, 2),
        qkv_bias,
        out_grad,
        out_bias.reshape(16),
        up_grad,
        up_bias.reshape(64),
        down_grad,
        down_bias.reshape(16),
        gain_grad.reshape(16),
        shift_grad.reshape(16),
    )


def solution(mesh):
    both = P(("col", "row"))
    in_specs = (
        P("row", "col"),
        P("row", None),
        P("row", None, "col"),
        P(None, ("col", "row")),
        P("col", "row"),
        both,
        P("row", "col"),
        both,
        P("col", "row"),
        both,
        both,
        both,
        P("row", "col"),
    )
    out_specs = (
        P("row", "col"),
        P("row", "col"),
        P("row", None, "col"),
        P(None, ("col", "row")),
        P("col", "row"),
        both,
        P("row", "col"),
        both,
        P("col", "row"),
        both,
        both,
        both,
    )
    return jax.shard_map(shards, mesh=mesh, in_specs=in_specs, out_specs=out_specs, check_vma=False)
```
